32 devices in a mesh: dp: 8 (over z, x), fsdp: 4 (over y, core).
Axes of the slice: x: 2, y: 2, z: 4, core: 2. Of those that a mesh axis runs over, the one named last changes fastest.
Arguments:
- hidden: bfloat16 [512, 64, 768], P(('dp', 'fsdp')), may hold values from -6 to 6
- lengths: int32 [512], P(('dp', 'fsdp')), may hold values from 3 to 64, as said below
- cotangent: bfloat16 [512, 64, 768], P(('dp', 'fsdp')), may hold values from -6 to 6
- attgain: bfloat16 [768], P(('dp', 'fsdp')), may hold values from 0.25 to 1.75
- attshift: bfloat16 [768], P(('dp', 'fsdp')), may hold values from -2 to 2
- querymat: bfloat16 [768, 768], P(None, ('dp', 'fsdp')), may hold values from -0.21875 to 0.21875
- querybias: bfloat16 [768], P(('dp', 'fsdp')), may hold values from -2 to 2
- keymat: bfloat16 [768, 768], P(None, ('dp', 'fsdp')), may hold values from -0.21875 to 0.21875
- valuemat: bfloat16 [768, 768], P(None, ('dp', 'fsdp')), may hold values from -0.21875 to 0.21875
- valuebias: bfloat16 [768], P(('dp', 'fsdp')), may hold values from -2 to 2
- mixmat: bfloat16 [768, 768], P(None, ('dp', 'fsdp')), may hold values from -0.625 to 0.625
- mixbias: bfloat16 [768], P(('dp', 'fsdp')), may hold values from -2 to 2
- mlpgain: bfloat16 [768], P(('dp', 'fsdp')), may hold values from 0.25 to 1.75
- mlpshift: bfloat16 [768], P(('dp', 'fsdp')), may hold values from -2 to 2
- upmat_w: bfloat16 [768, 3072], P(None, ('dp', 'fsdp')), may hold values from -0.21875 to 0.21875
- upbias: bfloat16 [3072], P(('dp', 'fsdp')), may hold values from -2 to 2
- downmat: bfloat16 [3072, 768], P(None, ('dp', 'fsdp')), may hold values from -0.109375 to 0.109375
- downbias: bfloat16 [768], P(('dp', 'fsdp')), may hold values from -2 to 2
Outputs:
- block_out: bfloat16 [512, 64, 768], P(('dp', 'fsdp'))
- input_grad: float32 [512, 64, 768], P(('dp', 'fsdp'))
- attgain_grad: float32 [768], P(('dp', 'fsdp'))
- attshift_grad: float32 [768], P(('dp', 'fsdp'))
- querymat_grad: float32 [768, 768], P(None, ('dp', 'fsdp'))
- querybias_grad: float32 [768], P(('dp', 'fsdp'))
- keymat_grad: float32 [768, 768], P(None, ('dp', 'fsdp'))
- valuemat_grad: float32 [768, 768], P(None, ('dp', 'fsdp'))
- valuebias_grad: float32 [768], P(('dp', 'fsdp'))
- mixmat_grad: float32 [768, 768], P(None, ('dp', 'fsdp'))
- mixbias_grad: float32 [768], P(('dp', 'fsdp'))
- mlpgain_grad: float32 [768], P(('dp', 'fsdp'))
- mlpshift_grad: float32 [768], P(('dp', 'fsdp'))
- upmat_grad: float32 [768, 3072], P(None, ('dp', 'fsdp'))
- upbias_grad: float32 [3072], P(('dp', 'fsdp'))
- downmat_grad: float32 [3072, 768], P(None, ('dp', 'fsdp'))
- downbias_grad: float32 [768], P(('dp', 'fsdp'))
The draws below stay inside these ranges and needn't reach their ends.
Inputs may be any that keep to these rules, and one draw needn't show every extreme that they name: The first lengths[c] token slots of caption c are real, the rest padding; some caption has 64 real tokens and some has 3.
All inputs are finite; a program needn't handle non-finite values.
Results may differ from the reference program's by a relative error of at most 0.013.
Values may be sent and summed in bfloat16 or wider, within the bound.
No kernel may reach another device: no remote copies, remote signals or barrier semaphores. Data moves between devices by JAX's collectives and lax.ppermute only.
A program may use at most 192 MiB of HBM per device.

```python
import math
import jax
import jax.numpy as jnp
from jax import lax

D = 768
HEADS = 12
HEAD_DIM = 64
FF = 3072
LEN = 64
CAPTIONS = 512


def draw_lengths(key, part):
    key = jax.random.fold_in(key, 5)
    first_key, second_key, top_key, shift_key = jax.random.split(key, 4)
    first = jax.random.randint(first_key, (CAPTIONS,), 0, LEN - 2)
    second = jax.random.randint(second_key, (CAPTIONS,), 0, LEN - 2)
    counts = 3 + jnp.minimum(first, second)
    longest = jax.random.randint(top_key, (), 0, CAPTIONS)
    shortest = (longest + 1 + jax.random.randint(shift_key, (), 0, CAPTIONS - 1)) % CAPTIONS
    counts = counts.at[longest].set(LEN).at[shortest].set(3)
    return counts.astype(jnp.int32)


def raised(values, rng, source, target, blocks, factor):
    def block_of(dim):
        return (jnp.arange(values.shape[dim]) // (values.shape[dim] // blocks)).reshape((-1,) + (1,) * (values.ndim - 1 - dim))

    one_side = jax.random.permutation(rng, blocks)[block_of(target)]
    second = (block_of(target) + blocks // 2) % blocks
    return jnp.where((block_of(source) == one_side) | (block_of(source) == second), factor * values, values)


def levels(stream_key, extent, cuts, least, high):
    level = 1.0
    for axis_at, blocks in cuts:
        heights = jax.random.uniform(jax.random.fold_in(jax.random.fold_in(stream_key, 6), axis_at), (blocks,), jnp.float32, least / len(cuts), high / len(cuts))
        level = level * jnp.repeat(jnp.exp(heights), extent[axis_at] // blocks).reshape((-1,) + (1,) * (len(extent) - 1 - axis_at))
    return level


def noise(key, dims, scale, reach, shards=(), kind=jnp.bfloat16):
    factor_of = levels(key, dims, shards, -0.22, 0.18) if shards else 1.0
    array = jax.random.normal(key, dims, jnp.float32) * scale * factor_of
    return jnp.minimum(jnp.maximum(array, -reach), reach).astype(kind)


def gaussian_with(rng, dims, scale, reach, cuts, heavy, held_as=jnp.bfloat16):
    drawn = scale * jax.random.normal(rng, dims, jnp.float32)
    if cuts:
        drawn = drawn * levels(rng, dims, cuts, -0.22, 0.18)
    return jnp.clip(raised(drawn, jax.random.fold_in(rng, 3), *heavy), -reach, reach).astype(held_as)


def setup_inputs(seed: int = 0) -> dict:
    splits = jax.random.split(jax.random.key(seed), 19)
    return {
        "hidden": noise(splits[0], (CAPTIONS, LEN, D), 1.0, 6.0, ((0, 32),)),
        "lengths": draw_lengths(jax.random.fold_in(splits[18], 71), 0),
        "cotangent": gaussian_with(splits[2], (CAPTIONS, LEN, D), 1.0, 6.0, ((0, 32),), (0, 2, 32, 2.75)),
        "attgain": jnp.clip(1.0 + 0.15 * jax.random.normal(splits[3], (D,), jnp.float32), 0.25, 1.75).astype(jnp.bfloat16),
        "attshift": noise(splits[4], (D,), 0.3, 2.0, ((0, 32),)),
        "querymat": noise(splits[5], (D, D), D ** -0.5, 0.21875, ((1, 32),)),
        "querybias": noise(splits[6], (D,), 0.3, 2.0, ((0, 32),)),
        "keymat": noise(splits[7], (D, D), D ** -0.5, 0.21875, ((1, 32),)),
        "valuemat": noise(splits[8], (D, D), D ** -0.5, 0.21875, ((1, 32),)),
        "valuebias": noise(splits[9], (D,), 0.3, 2.0, ((0, 32),)),
        "mixmat": noise(splits[10], (D, D), (D // 8) ** -0.5, 0.625, ((1, 32),)),
        "mixbias": noise(splits[11], (D,), 0.3, 2.0, ((0, 32),)),
        "mlpgain": jnp.clip(1.0 + 0.15 * jax.random.normal(splits[12], (D,), jnp.float32), 0.25, 1.75).astype(jnp.bfloat16),
        "mlpshift": noise(splits[13], (D,), 0.3, 2.0, ((0, 32),)),
        "upmat_w": noise(splits[14], (D, FF), D ** -0.5, 0.21875, ((1, 32),)),
        "upbias": noise(splits[15], (FF,), 0.3, 2.0, ((0, 32),)),
        "downmat": noise(splits[16], (FF, D), FF ** -0.5, 0.109375, ((1, 32),)),
        "downbias": noise(splits[17], (D,), 0.3, 2.0, ((0, 32),)),
    }


@jax.custom_vjp
def low(v):
    return lax.optimization_barrier(v.astype(jnp.bfloat16)).astype(jnp.float32)

@jax.custom_vjp
def low_back(v):
    return v

def low_keep(v):
    return (low(v), None)

def low_pass(kept, grad):
    return (grad,)

def back_keep(v):
    return (v, None)

def back_low(kept, grad):
    return (low(grad),)
low.defvjp(low_keep, low_pass)
low_back.defvjp(back_keep, back_low)
highest = lax.Precision.HIGHEST

def layer_norm(values, gain, shift):
    centre = lax.optimization_barrier(jnp.mean(values, axis=-1, keepdims=True))
    centred = values - centre
    spread = lax.optimization_barrier(jnp.mean(centred * centred, axis=-1, keepdims=True))
    return centred * lax.rsqrt(spread + 1e-06) * gain + shift

def project(inputs, matrix):
    return jnp.einsum('cli,ij->clj', inputs, matrix, precision=highest)

def forward(block, params, keymask):
    attgain, attshift, querymat, querybias, keymat, valuemat, valuebias, mixmat, mixbias, mlpgain, mlpshift, upmat_w, upbias, downmat, downbias = params
    groups, length, width = block.shape
    normed = low(layer_norm(block, attgain, attshift))
    query = low(low_back(project(normed, querymat) + querybias)).reshape(groups, length, HEADS, HEAD_DIM)
    keys = low(low_back(project(normed, keymat))).reshape(groups, length, HEADS, HEAD_DIM)
    values = low(low_back(project(normed, valuemat) + valuebias)).reshape(groups, length, HEADS, HEAD_DIM)
    factor = 1.0 / math.sqrt(HEAD_DIM)
    scores = low_back(jnp.einsum('clhd,cmhd->chlm', query, keys, precision=highest) * factor)
    masked = jnp.where(keymask[:, None, None, :], scores, -1e+30)
    peak = lax.optimization_barrier(jnp.max(masked, axis=-1, keepdims=True))
    expd = jnp.exp(masked - peak)
    probs = low(expd / lax.optimization_barrier(jnp.sum(expd, axis=-1, keepdims=True)))
    mixed = jnp.einsum('chlm,cmhd->clhd', probs, values, precision=highest).reshape(groups, length, width)
    mixed = low(low_back(mixed))
    branch = low_back(project(mixed, mixmat) + mixbias)
    middle = block + branch
    normed2 = low(layer_norm(middle, mlpgain, mlpshift))
    upper = low_back(project(normed2, upmat_w) + upbias)
    active = low(jax.nn.gelu(upper, approximate=True))
    return middle + low_back(project(active, downmat) + downbias)

def reference(hidden, lengths, cotangent, attgain, attshift, querymat, querybias, keymat, valuemat, valuebias, mixmat, mixbias, mlpgain, mlpshift, upmat_w, upbias, downmat, downbias):
    params = tuple((p.astype(jnp.float32) for p in (attgain, attshift, querymat, querybias, keymat, valuemat, valuebias, mixmat, mixbias, mlpgain, mlpshift, upmat_w, upbias, downmat, downbias)))
    groupsize = math.gcd(CAPTIONS, max(1, 4096 // LEN))
    count = CAPTIONS // groupsize
    positions = jnp.arange(LEN, dtype=jnp.int32)
    keymask = positions[None, :] < lengths.astype(jnp.int32)[:, None]
    blocks = hidden.astype(jnp.float32).reshape(count, groupsize, LEN, D)
    masks = keymask.reshape(count, groupsize, LEN)
    cots = cotangent.astype(jnp.float32).reshape(count, groupsize, LEN, D)

    def step(totals, pieces):
        block, maskpart, cotpart = pieces
        result, pull = jax.vjp(lambda b, p: forward(b, p, maskpart), block, params)
        weighting = cotpart * maskpart[..., None].astype(jnp.float32)
        grad_block, grad_params = pull(weighting)
        totals = jax.tree.map(jnp.add, totals, grad_params)
        return (totals, (result.astype(jnp.bfloat16), grad_block))
    zeros = jax.tree.map(jnp.zeros_like, params)
    totals, (results, grads) = lax.scan(step, zeros, (blocks, masks, cots))
    return (results.reshape(CAPTIONS, LEN, D), grads.reshape(CAPTIONS, LEN, D), totals[0], totals[1], totals[2], totals[3], totals[4], totals[5], totals[6], totals[7], totals[8], totals[9], totals[10], totals[11], totals[12], totals[13], totals[14])
```

```python
import functools
import math

import jax
import jax.numpy as jnp
from jax import lax
from jax.experimental import pallas as pl
from jax.experimental.pallas import tpu as pltpu
from jax.sharding import PartitionSpec as P

HEADS = 12


def layer_norm(values, gain, shift):
    centre = jnp.mean(values, axis=-1, keepdims=True)
    centred = values - centre
    spread = jnp.mean(centred * centred, axis=-1, keepdims=True)
    return centred * lax.rsqrt(spread + 1e-06) * gain + shift


def smooth(values):
    return jax.nn.gelu(values, approximate=True)


def project(inputs, matrix):
    return jnp.einsum("cli,ij->clj", inputs, matrix, preferred_element_type=jnp.float32)


def project_back(grads, matrix):
    return jnp.einsum("clj,ij->cli", grads, matrix, preferred_element_type=jnp.float32)


def outer_sum(inputs, grads):
    return jnp.einsum("cli,clj->ij", inputs, grads, preferred_element_type=jnp.float32)


def token_sum(grads):
    return jnp.sum(grads.astype(jnp.float32), axis=(0, 1))


def masked_scores(query_low, keys_low, keymask, factor):
    raw = (
        jnp.einsum("clhd,cmhd->chlm", query_low, keys_low, preferred_element_type=jnp.float32)
        * factor
    )
    return jnp.where(keymask[:, None, None, :], raw, -1e30)


def per_device(
    hidden,
    lengths,
    cotangent,
    attgain,
    attshift,
    querymat,
    querybias,
    keymat,
    valuemat,
    valuebias,
    mixmat,
    mixbias,
    mlpgain,
    mlpshift,
    upmat_w,
    upbias,
    downmat,
    downbias,
):
    captions, length, width = hidden.shape
    head_size = width // HEADS
    factor = 1.0 / math.sqrt(head_size)
    positions = lax.broadcasted_iota(jnp.int32, (captions, length), 1)
    keymask = positions < lengths[:, None]
    rowmask = keymask.astype(jnp.float32)[..., None]
    gathered = (
        lax.all_gather(attgain, ("dp", "fsdp"), axis=0, tiled=True),
        lax.all_gather(attshift, ("dp", "fsdp"), axis=0, tiled=True),
        lax.all_gather(querymat, ("dp", "fsdp"), axis=1, tiled=True),
        lax.all_gather(querybias, ("dp", "fsdp"), axis=0, tiled=True),
        lax.all_gather(keymat, ("dp", "fsdp"), axis=1, tiled=True),
        lax.all_gather(valuemat, ("dp", "fsdp"), axis=1, tiled=True),
        lax.all_gather(valuebias, ("dp", "fsdp"), axis=0, tiled=True),
        lax.all_gather(mixmat, ("dp", "fsdp"), axis=1, tiled=True),
        lax.all_gather(mixbias, ("dp", "fsdp"), axis=0, tiled=True),
        lax.all_gather(mlpgain, ("dp", "fsdp"), axis=0, tiled=True),
        lax.all_gather(mlpshift, ("dp", "fsdp"), axis=0, tiled=True),
        lax.all_gather(upmat_w, ("dp", "fsdp"), axis=1, tiled=True),
        lax.all_gather(upbias, ("dp", "fsdp"), axis=0, tiled=True),
        lax.all_gather(downmat, ("dp", "fsdp"), axis=1, tiled=True),
        lax.all_gather(downbias, ("dp", "fsdp"), axis=0, tiled=True),
    )
    (
        gain_one,
        shift_one,
        query_w,
        query_b,
        keys_w,
        values_w,
        values_b,
        mixer_w,
        mixer_b,
        gain_two,
        shift_two,
        upper_w,
        upper_b,
        lower_w,
        lower_b,
    ) = gathered
    gain_one = gain_one.astype(jnp.float32)
    shift_one = shift_one.astype(jnp.float32)
    gain_two = gain_two.astype(jnp.float32)
    shift_two = shift_two.astype(jnp.float32)
    source = hidden.astype(jnp.float32)
    normed_low = layer_norm(source, gain_one, shift_one).astype(jnp.bfloat16)
    query_low = (project(normed_low, query_w) + query_b.astype(jnp.float32)).astype(jnp.bfloat16)
    keys_low = project(normed_low, keys_w).astype(jnp.bfloat16)
    values_low = (project(normed_low, values_w) + values_b.astype(jnp.float32)).astype(jnp.bfloat16)
    query_heads = query_low.reshape(captions, length, HEADS, head_size)
    keys_heads = keys_low.reshape(captions, length, HEADS, head_size)
    values_heads = values_low.reshape(captions, length, HEADS, head_size)
    scores = masked_scores(query_heads, keys_heads, keymask, factor)
    peak = jnp.max(scores, axis=-1, keepdims=True)
    logsum = peak + jnp.log(jnp.sum(jnp.exp(scores - peak), axis=-1, keepdims=True))
    probs_low = jnp.exp(scores - logsum).astype(jnp.bfloat16)
    mixed_low = (
        jnp.einsum("chlm,cmhd->clhd", probs_low, values_heads, preferred_element_type=jnp.float32)
        .reshape(captions, length, width)
        .astype(jnp.bfloat16)
    )
    middle = source + project(mixed_low, mixer_w) + mixer_b.astype(jnp.float32)
    normed2_low = layer_norm(middle, gain_two, shift_two).astype(jnp.bfloat16)
    upper = project(normed2_low, upper_w) + upper_b.astype(jnp.float32)
    active_low = smooth(upper).astype(jnp.bfloat16)
    result = middle + project(active_low, lower_w) + lower_b.astype(jnp.float32)
    block_out = result.astype(jnp.bfloat16)
    again = (
        lax.all_gather(attgain, ("dp", "fsdp"), axis=0, tiled=True),
        lax.all_gather(attshift, ("dp", "fsdp"), axis=0, tiled=True),
        lax.all_gather(querymat, ("dp", "fsdp"), axis=1, tiled=True),
        lax.all_gather(querybias, ("dp", "fsdp"), axis=0, tiled=True),
        lax.all_gather(keymat, ("dp", "fsdp"), axis=1, tiled=True),
        lax.all_gather(valuemat, ("dp", "fsdp"), axis=1, tiled=True),
        lax.all_gather(valuebias, ("dp", "fsdp"), axis=0, tiled=True),
        lax.all_gather(mixmat, ("dp", "fsdp"), axis=1, tiled=True),
        lax.all_gather(mixbias, ("dp", "fsdp"), axis=0, tiled=True),
        lax.all_gather(mlpgain, ("dp", "fsdp"), axis=0, tiled=True),
        lax.all_gather(mlpshift, ("dp", "fsdp"), axis=0, tiled=True),
        lax.all_gather(upmat_w, ("dp", "fsdp"), axis=1, tiled=True),
        lax.all_gather(upbias, ("dp", "fsdp"), axis=0, tiled=True),
        lax.all_gather(downmat, ("dp", "fsdp"), axis=1, tiled=True),
        lax.all_gather(downbias, ("dp", "fsdp"), axis=0, tiled=True),
    )
    (
        gain_one,
        shift_one,
        query_w,
        query_b,
        keys_w,
        values_w,
        values_b,
        mixer_w,
        mixer_b,
        gain_two,
        shift_two,
        upper_w,
        upper_b,
        lower_w,
        lower_b,
    ) = again
    gain_one = gain_one.astype(jnp.float32)
    shift_one = shift_one.astype(jnp.float32)
    gain_two = gain_two.astype(jnp.float32)
    shift_two = shift_two.astype(jnp.float32)
    grad_out = cotangent.astype(jnp.float32) * rowmask
    grad_low = grad_out.astype(jnp.bfloat16)
    downmat_grad = outer_sum(active_low, grad_low)
    downbias_grad = token_sum(grad_low)
    grad_active = project_back(grad_low, lower_w)
    gelu_pull = jax.vjp(smooth, upper)[1]
    grad_upper_low = gelu_pull(grad_active)[0].astype(jnp.bfloat16)
    upmat_grad = outer_sum(normed2_low, grad_upper_low)
    upbias_grad = token_sum(grad_upper_low)
    grad_normed2 = project_back(grad_upper_low, upper_w)
    norm_pull = jax.vjp(layer_norm, middle, gain_two, shift_two)[1]
    grad_ln_two, mlpgain_grad, mlpshift_grad = norm_pull(grad_normed2)
    grad_middle = grad_out + grad_ln_two
    mlpgain_grad, mlpshift_grad, upmat_grad, upbias_grad, downmat_grad, downbias_grad = (
        lax.psum_scatter(mlpgain_grad, ("dp", "fsdp"), scatter_dimension=0, tiled=True),
        lax.psum_scatter(mlpshift_grad, ("dp", "fsdp"), scatter_dimension=0, tiled=True),
        lax.psum_scatter(upmat_grad, ("dp", "fsdp"), scatter_dimension=1, tiled=True),
        lax.psum_scatter(upbias_grad, ("dp", "fsdp"), scatter_dimension=0, tiled=True),
        lax.psum_scatter(downmat_grad, ("dp", "fsdp"), scatter_dimension=1, tiled=True),
        lax.psum_scatter(downbias_grad, ("dp", "fsdp"), scatter_dimension=0, tiled=True),
    )
    grad_branch_low = grad_middle.astype(jnp.bfloat16)
    mixmat_grad = outer_sum(mixed_low, grad_branch_low)
    mixbias_grad = token_sum(grad_branch_low)
    grad_mixed_low = (
        project_back(grad_branch_low, mixer_w)
        .astype(jnp.bfloat16)
        .reshape(captions, length, HEADS, head_size)
    )
    scores_again = masked_scores(query_heads, keys_heads, keymask, factor)
    probs = jnp.exp(scores_again - logsum)
    probs_again = probs.astype(jnp.bfloat16)
    grad_values_low = jnp.einsum(
        "chlm,clhd->cmhd", probs_again, grad_mixed_low, preferred_element_type=jnp.float32
    ).astype(jnp.bfloat16)
    grad_probs = jnp.einsum(
        "clhd,cmhd->chlm", grad_mixed_low, values_heads, preferred_element_type=jnp.float32
    )
    weighted = jnp.sum(probs * grad_probs, axis=-1, keepdims=True)
    grad_scores_low = (probs * (grad_probs - weighted)).astype(jnp.bfloat16)
    grad_query_low = (
        jnp.einsum(
            "chlm,cmhd->clhd", grad_scores_low, keys_heads, preferred_element_type=jnp.float32
        )
        * factor
    ).astype(jnp.bfloat16)
    grad_keys_low = (
        jnp.einsum(
            "chlm,clhd->cmhd", grad_scores_low, query_heads, preferred_element_type=jnp.float32
        )
        * factor
    ).astype(jnp.bfloat16)
    grad_query_low = grad_query_low.reshape(captions, length, width)
    grad_keys_low = grad_keys_low.reshape(captions, length, width)
    grad_values_low = grad_values_low.reshape(captions, length, width)
    querymat_grad = outer_sum(normed_low, grad_query_low)
    querybias_grad = token_sum(grad_query_low)
    keymat_grad = outer_sum(normed_low, grad_keys_low)
    valuemat_grad = outer_sum(normed_low, grad_values_low)
    valuebias_grad = token_sum(grad_values_low)
    grad_normed = (
        project_back(grad_query_low, query_w)
        + project_back(grad_keys_low, keys_w)
        + project_back(grad_values_low, values_w)
    )
    first_pull = jax.vjp(layer_norm, source, gain_one, shift_one)[1]
    grad_ln_one, attgain_grad, attshift_grad = first_pull(grad_normed)
    input_grad = grad_middle + grad_ln_one
    (
        attgain_grad,
        attshift_grad,
        querymat_grad,
        querybias_grad,
        keymat_grad,
        valuemat_grad,
        valuebias_grad,
        mixmat_grad,
        mixbias_grad,
    ) = (
        lax.psum_scatter(attgain_grad, ("dp", "fsdp"), scatter_dimension=0, tiled=True),
        lax.psum_scatter(attshift_grad, ("dp", "fsdp"), scatter_dimension=0, tiled=True),
        lax.psum_scatter(querymat_grad, ("dp", "fsdp"), scatter_dimension=1, tiled=True),
        lax.psum_scatter(querybias_grad, ("dp", "fsdp"), scatter_dimension=0, tiled=True),
        lax.psum_scatter(keymat_grad, ("dp", "fsdp"), scatter_dimension=1, tiled=True),
        lax.psum_scatter(valuemat_grad, ("dp", "fsdp"), scatter_dimension=1, tiled=True),
        lax.psum_scatter(valuebias_grad, ("dp", "fsdp"), scatter_dimension=0, tiled=True),
        lax.psum_scatter(mixmat_grad, ("dp", "fsdp"), scatter_dimension=1, tiled=True),
        lax.psum_scatter(mixbias_grad, ("dp", "fsdp"), scatter_dimension=0, tiled=True),
    )
    return (
        block_out,
        input_grad,
        attgain_grad,
        attshift_grad,
        querymat_grad,
        querybias_grad,
        keymat_grad,
        valuemat_grad,
        valuebias_grad,
        mixmat_grad,
        mixbias_grad,
        mlpgain_grad,
        mlpshift_grad,
        upmat_grad,
        upbias_grad,
        downmat_grad,
        downbias_grad,
    )


NT = (((1,), (1,)), ((), ()))
NN = (((1,), (0,)), ((), ()))
TN = (((0,), (0,)), ((), ()))
F32 = jnp.float32
BF16 = jnp.bfloat16
AXES = ("dp", "fsdp")
QUAD = 4
VMEM_LIMIT = 56 * 1024 * 1024


def dot(left, right, dims):
    return lax.dot_general(left, right, dims, preferred_element_type=F32)


class Grid3:
    def __init__(self, dp, fsdp):
        self.c = 2
        self.y = fsdp // 2
        self.x = self.y
        self.z = dp // self.x
        self.count = dp * fsdp

    def index(self, z, x, y, c):
        return ((z * self.x + x) * self.y + y) * self.c + c

    def shift(self, values, kz=0, kx=0, ky=0, kc=0):
        pairs = []
        for z in range(self.z):
            for x in range(self.x):
                for y in range(self.y):
                    for c in range(self.c):
                        target = self.index(
                            (z + kz) % self.z, (x + kx) % self.x, (y + ky) % self.y, (c + kc) % self.c
                        )
                        pairs.append((self.index(z, x, y, c), target))
        return lax.ppermute(values, AXES, pairs)

    def here(self):
        dp, fsdp = lax.axis_index("dp"), lax.axis_index("fsdp")
        return lax.div(dp, self.x), lax.rem(dp, self.x), lax.div(fsdp, self.c), lax.rem(fsdp, self.c)

    def away(self, kz, kx, ky, kc):
        z, x, y, c = self.here()
        return self.index(
            lax.rem(z + (kz % self.z), self.z),
            lax.rem(x + (kx % self.x), self.x),
            lax.rem(y + (ky % self.y), self.y),
            lax.rem(c + (kc % self.c), self.c),
        )


def gather(grid, own):
    rows = [own]
    for _ in range(grid.z - 1):
        rows.append(grid.shift(rows[-1], kz=1))
    half = grid.z // 2
    first = jnp.stack(rows[:half])
    second = jnp.stack(rows[half:])
    first_x = grid.shift(first, kx=1)
    second_y = grid.shift(second, ky=1)
    first_y = grid.shift(first, ky=1)
    second_x = grid.shift(second, kx=1)
    first_xy = grid.shift(first_x, ky=1)
    second_xy = grid.shift(second_y, kx=1)
    arrays, places = [], []
    for array, start, kx, ky in (
        (first, 0, 0, 0),
        (second, half, 0, 0),
        (first_x, 0, 1, 0),
        (second_y, half, 0, 1),
        (first_y, 0, 0, 1),
        (second_x, half, 1, 0),
        (first_xy, 0, 1, 1),
        (second_xy, half, 1, 1),
    ):
        arrays.append(array)
        places.append([(-(start + k), -kx, -ky, 0) for k in range(half)])
        arrays.append(grid.shift(array, kc=1))
        places.append([(-(start + k), -kx, -ky, -1) for k in range(half)])
    return arrays, places


def place(grid, places, refs, held, sems):
    copies = []
    for ref, spots in zip(refs, places):
        for slot, spot in enumerate(spots):
            copies.append(
                pltpu.make_async_copy(ref.at[slot], held.at[grid.away(*spot)], sems.at[len(copies)])
            )
    for copy in copies:
        copy.start()
    for copy in copies:
        copy.wait()


def outgoing(grid, core):
    half = grid.z // 2
    slots = []
    for which in range(2):
        for one in range(2):
            for two in range(2):
                for low in range(half):
                    kx, ky = (one, two) if which == 0 else (two, one)
                    slots.append((which * half + low, kx, ky, core))
    return slots


def scatter(grid, own, other):
    half = grid.z // 2

    def plus(left, right):
        return (left.astype(F32) + right.astype(F32)).astype(BF16)

    arrived = grid.shift(other, kc=1)
    tail = own.shape[1:]
    shape = (2, 2, 2, half) + tail
    own = own.reshape(shape)
    arrived = arrived.reshape(shape)
    send_a = plus(own[0, 1], arrived[0, 1])
    send_b = plus(own[1, 1], arrived[1, 1])
    got_a = grid.shift(send_a, kx=1)
    got_b = grid.shift(send_b, ky=1)
    keep_a = plus(own[0, 0], arrived[0, 0])
    keep_b = plus(own[1, 0], arrived[1, 0])
    next_a = plus(keep_a[1], got_a[1])
    next_b = plus(keep_b[1], got_b[1])
    last_a = grid.shift(next_a, ky=1)
    last_b = grid.shift(next_b, kx=1)
    rest_a = keep_a[0].astype(F32) + got_a[0].astype(F32) + last_a.astype(F32)
    rest_b = keep_b[0].astype(F32) + got_b[0].astype(F32) + last_b.astype(F32)
    parts = [rest_a[k] for k in range(half)] + [rest_b[k] for k in range(half)]
    total = parts[0]
    for k in range(1, grid.z):
        total = total + grid.shift(parts[k].astype(BF16), kz=k).astype(F32)
    return total


def lanes_of(rows):
    return lax.broadcasted_iota(jnp.int32, (rows, 256), 1) // 64


def spread(block):
    head = lanes_of(block.shape[0])
    zero = jnp.zeros_like(block)
    return jnp.concatenate([jnp.where(head == g, block, zero) for g in range(QUAD)], axis=0)


def collect(square):
    head = lanes_of(64)
    total = jnp.where(head == 0, square[0:64], 0.0)
    for g in range(1, QUAD):
        total = jnp.where(head == g, square[64 * g : 64 * g + 64], total)
    return total


def normal(values):
    centre = jnp.mean(values, axis=-1, keepdims=True)
    centred = values - centre
    spread_of = jnp.mean(centred * centred, axis=-1, keepdims=True)
    scale = lax.rsqrt(spread_of + 1e-06)
    return centred * scale, scale


def normal_back(hat, scale, gain, grads):
    weighted = grads * gain
    middle = jnp.mean(weighted, axis=-1, keepdims=True)
    along = jnp.mean(weighted * hat, axis=-1, keepdims=True)
    return scale * (weighted - middle - hat * along)


def row_mask(lengths_ref, step, captions, length):
    position = lax.broadcasted_iota(jnp.int32, (length, 1), 0)
    return jnp.concatenate(
        [(position < lengths_ref[step * captions + k]).astype(F32) for k in range(captions)], axis=0
    )


def pack_kernel(grid, small_ref, up_ref, q_ref, k_ref, v_ref, out_ref, wide):
    wide[...] = jnp.zeros_like(wide)
    wide[0:8, 0:24] = small_ref[...]
    wide[8:9, 0:96] = up_ref[...]
    me = lax.axis_index("dp") * (grid.y * grid.c) + lax.axis_index("fsdp")
    eight = pltpu.roll(wide[0:8, :], me * 24, 1)
    four = pltpu.roll(wide[8:16, :], lax.rem(me, 8) * 96, 1)
    row = lax.broadcasted_iota(jnp.int32, (8, 768), 0)
    four = jnp.where(row == lax.div(me, 8), jnp.broadcast_to(four[0:1], (8, 768)), 0.0)
    zero = jnp.zeros((8, 768), F32)
    out_ref[0] = jnp.concatenate([eight, four, zero], axis=0).astype(BF16)
    out_ref[1] = q_ref[...]
    out_ref[2] = k_ref[...]
    out_ref[3] = v_ref[...]


def attend_kernel(grid, places, length, lengths_ref, hidden_ref, *rest):
    count = len(places)
    refs, rest = rest[:count], rest[count:]
    normed_ref, q_ref, k_ref, v_ref, probs_ref, mixed_ref, vec_ref, held, sems = rest
    step = pl.program_id(0)

    @pl.when(step == 0)
    def _():
        place(grid, places, refs, held, sems)
        total = held[0, 0].astype(F32)
        for j in range(1, grid.count):
            total = total + held[j, 0].astype(F32)
        vec_ref[...] = total

    rows, width = hidden_ref.shape
    hat, _ = normal(hidden_ref[...].astype(F32))
    normed = (hat * vec_ref[0:1, :] + vec_ref[1:2, :]).astype(BF16)
    normed_ref[...] = normed
    q_ref[...] = (dot(normed, held[:, 1].reshape(width, width), NT) + vec_ref[2:3, :]).astype(BF16)
    k_ref[...] = dot(normed, held[:, 2].reshape(width, width), NT).astype(BF16)
    v_ref[...] = (dot(normed, held[:, 3].reshape(width, width), NT) + vec_ref[3:4, :]).astype(BF16)
    captions = rows // length
    quads = width // 256
    position = lax.broadcasted_iota(jnp.int32, (length, 256), 0)
    for cap in range(captions):
        keep = position < lengths_ref[step * captions + cap]
        for quad in range(quads):
            span = (slice(cap * length, (cap + 1) * length), slice(256 * quad, 256 * quad + 256))
            scores = dot(k_ref[span], spread(q_ref[span]), NT) * 0.125
            scores = jnp.where(keep, scores, -1e30)
            peak = jnp.max(scores, axis=0, keepdims=True)
            raised = jnp.exp(scores - peak)
            probs = (raised * (1.0 / jnp.sum(raised, axis=0, keepdims=True))).astype(BF16)
            probs_ref[cap * quads + quad] = probs
            mixed_ref[span] = collect(dot(probs, v_ref[span], TN)).astype(BF16)


def upper_kernel(grid, places, hidden_ref, mixed_ref, vec_ref, *rest):
    count = len(places)
    refs, rest = rest[:count], rest[count:]
    middle_ref, normed_ref, active_ref, slope_ref, held, sems = rest

    @pl.when(pl.program_id(0) == 0)
    def _():
        place(grid, places, refs, held, sems)

    width = hidden_ref.shape[1]
    middle = (
        hidden_ref[...].astype(F32)
        + dot(mixed_ref[...], held[:, 0].reshape(width, width), NT)
        + vec_ref[4:5, :]
    )
    middle_ref[...] = middle
    hat, _ = normal(middle)
    normed = (hat * vec_ref[5:6, :] + vec_ref[6:7, :]).astype(BF16)
    normed_ref[...] = normed
    per = grid.count // 4
    for part in range(4):
        weight = held[per * part : per * part + per, 1:5].reshape(width, width)
        upper = dot(normed, weight, NT) + vec_ref[8 + part : 9 + part, :]
        square = upper * upper
        root = math.sqrt(2.0 / math.pi)
        bend = jnp.tanh(upper * (root + (root * 0.044715) * square))
        half = 0.5 * bend + 0.5
        span = slice(width * part, width * part + width)
        active_ref[:, span] = (upper * half).astype(BF16)
        slope = half + (0.5 * upper) * (1.0 - bend * bend) * (root + (3.0 * root * 0.044715) * square)
        slope_ref[:, span] = slope.astype(BF16)


def mask_into(lengths_ref, cot_ref, low, length):
    rows = cot_ref.shape[0]
    captions = rows // length
    for k in range(captions):
        span = slice(k * length, (k + 1) * length)
        position = lax.broadcasted_iota(jnp.int32, (length, 1), 0)
        kept = jnp.where(position < lengths_ref[k], cot_ref[span, :].astype(F32), 0.0)
        low[span, :] = kept.astype(BF16)


def down_grad_kernel(grid, length, lengths_ref, cot_ref, active_ref, low_ref, vec_ref, own_ref, other_ref, total):
    @pl.when(pl.program_id(0) == 0)
    def _():
        mask_into(lengths_ref, cot_ref, low_ref, length)
        vec_ref[...] = jnp.broadcast_to(
            jnp.sum(low_ref[...].astype(F32), axis=0, keepdims=True), vec_ref.shape
        )

    total[...] = dot(low_ref[...], active_ref[...], TN)
    rows = total.shape[0] // grid.count
    for core, out_ref in ((0, own_ref), (1, other_ref)):
        for slot, spot in enumerate(outgoing(grid, core)):
            at = pl.multiple_of(grid.away(*spot) * rows, 8)
            out_ref[slot] = total[pl.ds(at, rows), :].astype(BF16)


def upper_grad_kernel(grid, places, low_ref, slope_ref, normed_ref, *rest):
    count = len(places)
    refs, rest = rest[:count], rest[count:]
    upper_ref, vec_ref, both_ref, held, sems, total = rest
    step = pl.program_id(0)

    @pl.when(step == 0)
    def _():
        place(grid, places, refs, held, sems)

    width = low_ref.shape[1]
    weight = held[:, :, pl.ds(pl.multiple_of(step * width, 128), width)].reshape(width, width)
    grads = (dot(low_ref[...], weight, NN) * slope_ref[...].astype(F32)).astype(BF16)
    upper_ref[...] = grads
    vec_ref[pl.ds(pl.multiple_of(step * 8, 8), 8), :] = jnp.broadcast_to(
        jnp.sum(grads.astype(F32), axis=0, keepdims=True), (8, width)
    )
    total[...] = dot(grads, normed_ref[...], TN)
    per = grid.count // 4
    rows = width // per
    z, x, y, c = grid.here()
    for k in range(per):
        owner = step * per + k
        kz = lax.rem(lax.div(owner, grid.x * grid.y * grid.c) - z + grid.z, grid.z)
        kx = lax.rem(lax.rem(lax.div(owner, grid.y * grid.c), grid.x) - x + grid.x, grid.x)
        ky = lax.rem(lax.rem(lax.div(owner, grid.c), grid.y) - y + grid.y, grid.y)
        kc = lax.rem(lax.rem(owner, grid.c) - c + grid.c, grid.c)
        half = grid.z // 2
        which = lax.div(kz, half)
        one = jnp.where(which == 0, kx, ky)
        two = jnp.where(which == 0, ky, kx)
        slot = ((which * 2 + one) * 2 + two) * half + lax.rem(kz, half)
        block = total[k * rows : (k + 1) * rows, :].astype(BF16)
        both_ref[kc * (grid.count // 2) + slot] = block.reshape(both_ref.shape[1:])


def middle_grad_kernel(grid, places, length, lengths_ref, upper_ref, middle_ref, cot_ref, q_ref, k_ref, v_ref, probs_ref, vec_in, *rest):
    count = len(places)
    refs, rest = rest[:count], rest[count:]
    grad_ref, branch_ref, dq_ref, dk_ref, dv_ref, vec_ref, held, sems, dm = rest
    step = pl.program_id(0)

    @pl.when(step == 0)
    def _():
        place(grid, places, refs, held, sems)
        vec_ref[...] = jnp.zeros_like(vec_ref)

    rows, width = middle_ref.shape
    captions = rows // length
    per = grid.count // 4
    grads = dot(upper_ref[:, 0:width], held[0:per, 1:5].reshape(width, width), NN)
    for part in range(1, 4):
        weight = held[per * part : per * part + per, 1:5].reshape(width, width)
        grads = grads + dot(upper_ref[:, width * part : width * part + width], weight, NN)
    hat, scale = normal(middle_ref[...])
    out = cot_ref[...].astype(F32) * row_mask(lengths_ref, step, captions, length)
    grad_middle = out + normal_back(hat, scale, vec_in[5:6, :], grads)
    grad_ref[...] = grad_middle
    branch = grad_middle.astype(BF16)
    branch_ref[...] = branch
    dm[...] = dot(branch, held[:, 0].reshape(width, width), NN).astype(BF16)
    vec_ref[0:1, :] += jnp.sum(grads * hat, axis=0, keepdims=True)
    vec_ref[1:2, :] += jnp.sum(grads, axis=0, keepdims=True)
    vec_ref[2:3, :] += jnp.sum(branch.astype(F32), axis=0, keepdims=True)
    quads = width // 256
    for cap in range(captions):
        for quad in range(quads):
            span = (slice(cap * length, (cap + 1) * length), slice(256 * quad, 256 * quad + 256))
            probs = probs_ref[cap * quads + quad]
            wide = spread(dm[span])
            dv_ref[span] = dot(probs, wide, NN).astype(BF16)
            grad_probs = dot(v_ref[span], wide, NT)
            probs = probs.astype(F32)
            along = jnp.sum(probs * grad_probs, axis=0, keepdims=True)
            grad_scores = (probs * (grad_probs - along)).astype(BF16)
            dk_ref[span] = (dot(grad_scores, spread(q_ref[span]), NN) * 0.125).astype(BF16)
            dq_ref[span] = (collect(dot(grad_scores, k_ref[span], TN)) * 0.125).astype(BF16)
    vec_ref[3:4, :] += jnp.sum(dq_ref[...].astype(F32), axis=0, keepdims=True)
    vec_ref[4:5, :] += jnp.sum(dv_ref[...].astype(F32), axis=0, keepdims=True)


def weight_grad_kernel(grid, dq_ref, dk_ref, dv_ref, branch_ref, normed_ref, mixed_ref, own_ref, other_ref, total):
    rows = total.shape[0] // grid.count
    for at, (grads, inputs) in enumerate(
        ((dq_ref, normed_ref), (dk_ref, normed_ref), (dv_ref, normed_ref), (branch_ref, mixed_ref))
    ):
        total[...] = dot(grads[...], inputs[...], TN)
        for core, out_ref in ((0, own_ref), (1, other_ref)):
            for slot, spot in enumerate(outgoing(grid, core)):
                start = pl.multiple_of(grid.away(*spot) * rows, 8)
                out_ref[slot, at] = total[pl.ds(start, rows), :].astype(BF16)


def input_grad_kernel(grid, places, hidden_ref, grad_ref, dq_ref, dk_ref, dv_ref, vec_in, down_vec, up_vec, mid_vec, *rest):
    count = len(places)
    refs, rest = rest[:count], rest[count:]
    out_ref, vec_ref, held, sems = rest

    @pl.when(pl.program_id(0) == 0)
    def _():
        place(grid, places, refs, held, sems)
        vec_ref[...] = jnp.zeros_like(vec_ref)
        vec_ref[2:3, :] = mid_vec[3:4, :]
        vec_ref[3:4, :] = mid_vec[4:5, :]
        vec_ref[4:5, :] = mid_vec[2:3, :]
        vec_ref[5:7, :] = mid_vec[0:2, :]
        vec_ref[7:8, :] = down_vec[0:1, :]
        for part in range(4):
            vec_ref[8 + part : 9 + part, :] = up_vec[8 * part : 8 * part + 1, :]

    width = hidden_ref.shape[1]
    grads = dot(dq_ref[...], held[:, 1].reshape(width, width), NN)
    grads = grads + dot(dk_ref[...], held[:, 2].reshape(width, width), NN)
    grads = grads + dot(dv_ref[...], held[:, 3].reshape(width, width), NN)
    hat, scale = normal(hidden_ref[...].astype(F32))
    out_ref[...] = grad_ref[...] + normal_back(hat, scale, vec_in[0:1, :], grads)
    vec_ref[0:1, :] += jnp.sum(grads * hat, axis=0, keepdims=True)
    vec_ref[1:2, :] += jnp.sum(grads, axis=0, keepdims=True)


def lower_kernel(grid, places, active_ref, middle_ref, vec_in, *rest):
    count = len(places)
    refs, rest = rest[:count], rest[count:]
    out_ref, held, sems = rest

    @pl.when(pl.program_id(0) == 0)
    def _():
        place(grid, places, refs, held, sems)

    width = middle_ref.shape[1]
    weight = held[...].reshape(width, held.shape[2])
    out = middle_ref[...] + dot(active_ref[...], weight, NT) + vec_in[7:8, :]
    out_ref[...] = out.astype(BF16)


def unpack_kernel(grid, vec_ref, *outs):
    me = lax.axis_index("dp") * (grid.y * grid.c) + lax.axis_index("fsdp")
    eight = pltpu.roll(vec_ref[0:8, :], lax.rem(768 - me * 24, 768), 1)
    for k in range(8):
        outs[k][...] = eight[k : k + 1, 0:24]
    row = lax.broadcasted_iota(jnp.int32, (8, 768), 0)
    four = jnp.sum(jnp.where(row == lax.div(me, 8), vec_ref[8:16, :], 0.0), axis=0, keepdims=True)
    four = jnp.broadcast_to(four, (8, 768))
    four = pltpu.roll(four, lax.rem(768 - lax.rem(me, 8) * 96, 768), 1)
    outs[8][...] = four[0:1, 0:96]


def whole(shape):
    return pl.BlockSpec(shape, lambda *_: (0,) * len(shape))


ANY = pl.BlockSpec(memory_space=pl.ANY)
SMEM = pl.BlockSpec(memory_space=pltpu.SMEM)


def call(kernel, steps, in_specs, out_specs, outs, scratch, flops, moved, name):
    return pl.pallas_call(
        kernel,
        grid=(steps,),
        in_specs=in_specs,
        out_specs=out_specs,
        out_shape=[jax.ShapeDtypeStruct(s, d) for s, d in outs],
        scratch_shapes=scratch,
        compiler_params=pltpu.CompilerParams(vmem_limit_bytes=VMEM_LIMIT),
        cost_estimate=pl.CostEstimate(flops=flops, bytes_accessed=moved, transcendentals=0),
        name=name,
    )


def fast_device(
    grid,
    hidden,
    lengths,
    cotangent,
    attgain,
    attshift,
    querymat,
    querybias,
    keymat,
    valuemat,
    valuebias,
    mixmat,
    mixbias,
    mlpgain,
    mlpshift,
    upmat_w,
    upbias,
    downmat,
    downbias,
):
    captions, length, width = hidden.shape
    tokens = captions * length
    hidden2 = hidden.reshape(tokens, width)
    cot2 = cotangent.reshape(tokens, width)
    share = width // grid.count
    ff = downmat.shape[0]
    small = jnp.stack(
        [attgain, attshift, querybias, valuebias, mixbias, mlpgain, mlpshift, downbias]
    ).astype(F32)
    upsmall = upbias.astype(F32).reshape(1, -1)
    first = call(
        functools.partial(pack_kernel, grid),
        1,
        [whole((8, share)), whole((1, 96))] + [whole((share, width))] * 3,
        [whole((4, share, width))],
        [((4, share, width), BF16)],
        [pltpu.VMEM((16, width), F32)],
        1000,
        1000,
        "pack",
    )(small, upsmall, querymat.T, keymat.T, valuemat.T)[0]
    second = jnp.concatenate([mixmat.T[None], upmat_w.T.reshape(4, share, width)], axis=0)
    third = downmat.T
    first_in, places = gather(grid, first)
    second_in, _ = gather(grid, second)
    third_in, _ = gather(grid, third)
    copies = pltpu.SemaphoreType.DMA((grid.count,))
    held_first = pltpu.VMEM((grid.count,) + first.shape, BF16)
    held_second = pltpu.VMEM((grid.count,) + second.shape, BF16)
    held_third = pltpu.VMEM((grid.count,) + third.shape, BF16)
    steps = 4
    rows = tokens // steps
    block = pl.BlockSpec((rows, width), lambda i: (i, 0))
    broad = pl.BlockSpec((rows, ff), lambda i: (i, 0))
    heads = (tokens // length) * (width // 256)
    probs_block = pl.BlockSpec((heads // steps, length, 256), lambda i: (i, 0, 0))
    unit = 2 * tokens * width * width
    row = (tokens, width)
    vec_block = whole((share, width))
    normed, query, keys, values, probs, mixed, vec = call(
        functools.partial(attend_kernel, grid, places, length),
        steps,
        [SMEM, block] + [ANY] * len(first_in),
        [block] * 4 + [probs_block, block, vec_block],
        [(row, BF16)] * 4 + [((heads, length, 256), BF16), (row, BF16), ((share, width), F32)],
        [held_first, copies],
        7 * unit,
        20_000_000,
        "attend",
    )(lengths, hidden2, *first_in)
    middle, normed2, active, slope = call(
        functools.partial(upper_kernel, grid, places),
        steps,
        [block, block, vec_block] + [ANY] * len(second_in),
        [block, block, broad, broad],
        [(row, F32), (row, BF16), ((tokens, ff), BF16), ((tokens, ff), BF16)],
        [held_second, copies],
        8 * unit,
        20_000_000,
        "upper",
    )(hidden2, mixed, vec, *second_in)
    column = pl.BlockSpec((tokens, width), lambda i: (0, i))
    half = grid.count // 2
    low, down_vec, down_own, down_other = call(
        functools.partial(down_grad_kernel, grid, length),
        ff // width,
        [SMEM, whole(row), column],
        [whole(row), whole((8, width))]
        + [pl.BlockSpec((half, share, width), lambda i: (0, 0, i))] * 2,
        [(row, BF16), ((8, width), F32)] + [((half, share, ff), BF16)] * 2,
        [pltpu.VMEM((width, width), F32)],
        4 * unit,
        10_000_000,
        "down_grad",
    )(lengths, cot2, active)
    grad_upper, up_vec, up_both = call(
        functools.partial(upper_grad_kernel, grid, places),
        ff // width,
        [whole(row), column, whole(row)] + [ANY] * len(third_in),
        [column, whole((32, width)), whole((grid.count, 4, share, width))],
        [((tokens, ff), BF16), ((32, width), F32), ((grid.count, 4, share, width), BF16)],
        [held_third, copies, pltpu.VMEM((width, width), F32)],
        8 * unit,
        20_000_000,
        "upper_grad",
    )(low, slope, normed2, *third_in)
    grad_middle, branch, dq, dk, dv, mid_vec = call(
        functools.partial(middle_grad_kernel, grid, places, length),
        steps,
        [SMEM, broad, block, block, block, block, block, probs_block, vec_block]
        + [ANY] * len(second_in),
        [block] * 5 + [whole((8, width))],
        [(row, F32)] + [(row, BF16)] * 4 + [((8, width), F32)],
        [held_second, copies, pltpu.VMEM((rows, width), BF16)],
        13 * unit,
        20_000_000,
        "middle_grad",
    )(lengths, grad_upper, middle, cot2, query, keys, values, probs, vec, *second_in)
    att_own, att_other = call(
        functools.partial(weight_grad_kernel, grid),
        1,
        [whole(row)] * 6,
        [whole((half, 4, share, width))] * 2,
        [((half, 4, share, width), BF16)] * 2,
        [pltpu.VMEM((width, width), F32)],
        4 * unit,
        10_000_000,
        "weight_grad",
    )(dq, dk, dv, branch, normed, mixed)
    input_grad, all_vec = call(
        functools.partial(input_grad_kernel, grid, places),
        steps,
        [block] * 5 + [vec_block, whole((8, width)), whole((32, width)), whole((8, width))]
        + [ANY] * len(first_in),
        [block, whole((16, width))],
        [(row, F32), ((16, width), F32)],
        [held_first, copies],
        4 * unit,
        20_000_000,
        "input_grad",
    )(hidden2, grad_middle, dq, dk, dv, vec, down_vec, up_vec, mid_vec, *first_in)
    (block_out,) = call(
        functools.partial(lower_kernel, grid, places),
        steps,
        [broad, block, vec_block] + [ANY] * len(third_in),
        [block],
        [(row, BF16)],
        [held_third, copies],
        4 * unit,
        20_000_000,
        "lower",
    )(active, middle, vec, *third_in)
    down_sum = scatter(grid, down_own, down_other)
    up_sum = scatter(grid, up_both[:half], up_both[half:])
    att_sum = scatter(grid, att_own, att_other)
    all_vec = all_vec + grid.shift(all_vec, kc=1)
    all_vec = all_vec + grid.shift(all_vec, kx=1)
    all_vec = all_vec + grid.shift(all_vec, ky=1)
    all_vec = (
        all_vec + grid.shift(all_vec, kz=1) + grid.shift(all_vec, kz=2) + grid.shift(all_vec, kz=3)
    )
    vecs = call(
        functools.partial(unpack_kernel, grid),
        1,
        [whole((16, width))],
        [whole((1, share))] * 8 + [whole((1, ff // grid.count))],
        [((1, share), F32)] * 8 + [((1, ff // grid.count), F32)],
        [],
        1000,
        1000,
        "unpack",
    )(all_vec)
    vecs = [v.reshape(-1) for v in vecs]
    return (
        block_out.reshape(hidden.shape),
        input_grad.reshape(hidden.shape),
        vecs[0],
        vecs[1],
        att_sum[0].T,
        vecs[2],
        att_sum[1].T,
        att_sum[2].T,
        vecs[3],
        att_sum[3].T,
        vecs[4],
        vecs[5],
        vecs[6],
        up_sum.reshape(ff // grid.count, width).T,
        vecs[8],
        down_sum.T,
        vecs[7],
    )


def fits(mesh):
    return mesh.shape["dp"] == 8 and mesh.shape["fsdp"] == 4


def solution(mesh):
    placed = (
        P(("dp", "fsdp"), None, None),
        P(("dp", "fsdp")),
        P(("dp", "fsdp"), None, None),
        P(("dp", "fsdp")),
        P(("dp", "fsdp")),
        P(None, ("dp", "fsdp")),
        P(("dp", "fsdp")),
        P(None, ("dp", "fsdp")),
        P(None, ("dp", "fsdp")),
        P(("dp", "fsdp")),
        P(None, ("dp", "fsdp")),
        P(("dp", "fsdp")),
        P(("dp", "fsdp")),
        P(("dp", "fsdp")),
        P(None, ("dp", "fsdp")),
        P(("dp", "fsdp")),
        P(None, ("dp", "fsdp")),
        P(("dp", "fsdp")),
    )
    body = per_device
    if fits(mesh):
        body = functools.partial(fast_device, Grid3(mesh.shape["dp"], mesh.shape["fsdp"]))
    return jax.shard_map(
        body,
        mesh=mesh,
        in_specs=placed,
        out_specs=(
            P(("dp", "fsdp"), None, None),
            P(("dp", "fsdp"), None, None),
            P(("dp", "fsdp")),
            P(("dp", "fsdp")),
            P(None, ("dp", "fsdp")),
            P(("dp", "fsdp")),
            P(None, ("dp", "fsdp")),
            P(None, ("dp", "fsdp")),
            P(("dp", "fsdp")),
            P(None, ("dp", "fsdp")),
            P(("dp", "fsdp")),
            P(("dp", "fsdp")),
            P(("dp", "fsdp")),
            P(None, ("dp", "fsdp")),
            P(("dp", "fsdp")),
            P(None, ("dp", "fsdp")),
            P(("dp", "fsdp")),
        ),
        check_vma=False,
    )
```

```python
import functools
import math

import jax
import jax.numpy as jnp
from jax import lax
from jax.experimental import pallas as pl
from jax.experimental.pallas import tpu as pltpu
from jax.sharding import PartitionSpec as P

HEADS = 12


def layer_norm(values, gain, shift):
    centre = jnp.mean(values, axis=-1, keepdims=True)
    centred = values - centre
    spread = jnp.mean(centred * centred, axis=-1, keepdims=True)
    return centred * lax.rsqrt(spread + 1e-06) * gain + shift


def smooth(values):
    return jax.nn.gelu(values, approximate=True)


def project(inputs, matrix):
    return jnp.einsum("cli,ij->clj", inputs, matrix, preferred_element_type=jnp.float32)


def project_back(grads, matrix):
    return jnp.einsum("clj,ij->cli", grads, matrix, preferred_element_type=jnp.float32)


def outer_sum(inputs, grads):
    return jnp.einsum("cli,clj->ij", inputs, grads, preferred_element_type=jnp.float32)


def token_sum(grads):
    return jnp.sum(grads.astype(jnp.float32), axis=(0, 1))


def masked_scores(query_low, keys_low, keymask, factor):
    raw = (
        jnp.einsum("clhd,cmhd->chlm", query_low, keys_low, preferred_element_type=jnp.float32)
        * factor
    )
    return jnp.where(keymask[:, None, None, :], raw, -1e30)


def per_device(
    hidden,
    lengths,
    cotangent,
    attgain,
    attshift,
    querymat,
    querybias,
    keymat,
    valuemat,
    valuebias,
    mixmat,
    mixbias,
    mlpgain,
    mlpshift,
    upmat_w,
    upbias,
    downmat,
    downbias,
):
    captions, length, width = hidden.shape
    head_size = width // HEADS
    factor = 1.0 / math.sqrt(head_size)
    positions = lax.broadcasted_iota(jnp.int32, (captions, length), 1)
    keymask = positions < lengths[:, None]
    rowmask = keymask.astype(jnp.float32)[..., None]
    gathered = (
        lax.all_gather(attgain, ("dp", "fsdp"), axis=0, tiled=True),
        lax.all_gather(attshift, ("dp", "fsdp"), axis=0, tiled=True),
        lax.all_gather(querymat, ("dp", "fsdp"), axis=1, tiled=True),
        lax.all_gather(querybias, ("dp", "fsdp"), axis=0, tiled=True),
        lax.all_gather(keymat, ("dp", "fsdp"), axis=1, tiled=True),
        lax.all_gather(valuemat, ("dp", "fsdp"), axis=1, tiled=True),
        lax.all_gather(valuebias, ("dp", "fsdp"), axis=0, tiled=True),
        lax.all_gather(mixmat, ("dp", "fsdp"), axis=1, tiled=True),
        lax.all_gather(mixbias, ("dp", "fsdp"), axis=0, tiled=True),
        lax.all_gather(mlpgain, ("dp", "fsdp"), axis=0, tiled=True),
        lax.all_gather(mlpshift, ("dp", "fsdp"), axis=0, tiled=True),
        lax.all_gather(upmat_w, ("dp", "fsdp"), axis=1, tiled=True),
        lax.all_gather(upbias, ("dp", "fsdp"), axis=0, tiled=True),
        lax.all_gather(downmat, ("dp", "fsdp"), axis=1, tiled=True),
        lax.all_gather(downbias, ("dp", "fsdp"), axis=0, tiled=True),
    )
    (
        gain_one,
        shift_one,
        query_w,
        query_b,
        keys_w,
        values_w,
        values_b,
        mixer_w,
        mixer_b,
        gain_two,
        shift_two,
        upper_w,
        upper_b,
        lower_w,
        lower_b,
    ) = gathered
    gain_one = gain_one.astype(jnp.float32)
    shift_one = shift_one.astype(jnp.float32)
    gain_two = gain_two.astype(jnp.float32)
    shift_two = shift_two.astype(jnp.float32)
    source = hidden.astype(jnp.float32)
    normed_low = layer_norm(source, gain_one, shift_one).astype(jnp.bfloat16)
    query_low = (project(normed_low, query_w) + query_b.astype(jnp.float32)).astype(jnp.bfloat16)
    keys_low = project(normed_low, keys_w).astype(jnp.bfloat16)
    values_low = (project(normed_low, values_w) + values_b.astype(jnp.float32)).astype(jnp.bfloat16)
    query_heads = query_low.reshape(captions, length, HEADS, head_size)
    keys_heads = keys_low.reshape(captions, length, HEADS, head_size)
    values_heads = values_low.reshape(captions, length, HEADS, head_size)
    scores = masked_scores(query_heads, keys_heads, keymask, factor)
    peak = jnp.max(scores, axis=-1, keepdims=True)
    logsum = peak + jnp.log(jnp.sum(jnp.exp(scores - peak), axis=-1, keepdims=True))
    probs_low = jnp.exp(scores - logsum).astype(jnp.bfloat16)
    mixed_low = (
        jnp.einsum("chlm,cmhd->clhd", probs_low, values_heads, preferred_element_type=jnp.float32)
        .reshape(captions, length, width)
        .astype(jnp.bfloat16)
    )
    middle = source + project(mixed_low, mixer_w) + mixer_b.astype(jnp.float32)
    normed2_low = layer_norm(middle, gain_two, shift_two).astype(jnp.bfloat16)
    upper = project(normed2_low, upper_w) + upper_b.astype(jnp.float32)
    active_low = smooth(upper).astype(jnp.bfloat16)
    result = middle + project(active_low, lower_w) + lower_b.astype(jnp.float32)
    block_out = result.astype(jnp.bfloat16)
    again = (
        lax.all_gather(attgain, ("dp", "fsdp"), axis=0, tiled=True),
        lax.all_gather(attshift, ("dp", "fsdp"), axis=0, tiled=True),
        lax.all_gather(querymat, ("dp", "fsdp"), axis=1, tiled=True),
        lax.all_gather(querybias, ("dp", "fsdp"), axis=0, tiled=True),
        lax.all_gather(keymat, ("dp", "fsdp"), axis=1, tiled=True),
        lax.all_gather(valuemat, ("dp", "fsdp"), axis=1, tiled=True),
        lax.all_gather(valuebias, ("dp", "fsdp"), axis=0, tiled=True),
        lax.all_gather(mixmat, ("dp", "fsdp"), axis=1, tiled=True),
        lax.all_gather(mixbias, ("dp", "fsdp"), axis=0, tiled=True),
        lax.all_gather(mlpgain, ("dp", "fsdp"), axis=0, tiled=True),
        lax.all_gather(mlpshift, ("dp", "fsdp"), axis=0, tiled=True),
        lax.all_gather(upmat_w, ("dp", "fsdp"), axis=1, tiled=True),
        lax.all_gather(upbias, ("dp", "fsdp"), axis=0, tiled=True),
        lax.all_gather(downmat, ("dp", "fsdp"), axis=1, tiled=True),
        lax.all_gather(downbias, ("dp", "fsdp"), axis=0, tiled=True),
    )
    (
        gain_one,
        shift_one,
        query_w,
        query_b,
        keys_w,
        values_w,
        values_b,
        mixer_w,
        mixer_b,
        gain_two,
        shift_two,
        upper_w,
        upper_b,
        lower_w,
        lower_b,
    ) = again
    gain_one = gain_one.astype(jnp.float32)
    shift_one = shift_one.astype(jnp.float32)
    gain_two = gain_two.astype(jnp.float32)
    shift_two = shift_two.astype(jnp.float32)
    grad_out = cotangent.astype(jnp.float32) * rowmask
    grad_low = grad_out.astype(jnp.bfloat16)
    downmat_grad = outer_sum(active_low, grad_low)
    downbias_grad = token_sum(grad_low)
    grad_active = project_back(grad_low, lower_w)
    gelu_pull = jax.vjp(smooth, upper)[1]
    grad_upper_low = gelu_pull(grad_active)[0].astype(jnp.bfloat16)
    upmat_grad = outer_sum(normed2_low, grad_upper_low)
    upbias_grad = token_sum(grad_upper_low)
    grad_normed2 = project_back(grad_upper_low, upper_w)
    norm_pull = jax.vjp(layer_norm, middle, gain_two, shift_two)[1]
    grad_ln_two, mlpgain_grad, mlpshift_grad = norm_pull(grad_normed2)
    grad_middle = grad_out + grad_ln_two
    mlpgain_grad, mlpshift_grad, upmat_grad, upbias_grad, downmat_grad, downbias_grad = (
        lax.psum_scatter(mlpgain_grad, ("dp", "fsdp"), scatter_dimension=0, tiled=True),
        lax.psum_scatter(mlpshift_grad, ("dp", "fsdp"), scatter_dimension=0, tiled=True),
        lax.psum_scatter(upmat_grad, ("dp", "fsdp"), scatter_dimension=1, tiled=True),
        lax.psum_scatter(upbias_grad, ("dp", "fsdp"), scatter_dimension=0, tiled=True),
        lax.psum_scatter(downmat_grad, ("dp", "fsdp"), scatter_dimension=1, tiled=True),
        lax.psum_scatter(downbias_grad, ("dp", "fsdp"), scatter_dimension=0, tiled=True),
    )
    grad_branch_low = grad_middle.astype(jnp.bfloat16)
    mixmat_grad = outer_sum(mixed_low, grad_branch_low)
    mixbias_grad = token_sum(grad_branch_low)
    grad_mixed_low = (
        project_back(grad_branch_low, mixer_w)
        .astype(jnp.bfloat16)
        .reshape(captions, length, HEADS, head_size)
    )
    scores_again = masked_scores(query_heads, keys_heads, keymask, factor)
    probs = jnp.exp(scores_again - logsum)
    probs_again = probs.astype(jnp.bfloat16)
    grad_values_low = jnp.einsum(
        "chlm,clhd->cmhd", probs_again, grad_mixed_low, preferred_element_type=jnp.float32
    ).astype(jnp.bfloat16)
    grad_probs = jnp.einsum(
        "clhd,cmhd->chlm", grad_mixed_low, values_heads, preferred_element_type=jnp.float32
    )
    weighted = jnp.sum(probs * grad_probs, axis=-1, keepdims=True)
    grad_scores_low = (probs * (grad_probs - weighted)).astype(jnp.bfloat16)
    grad_query_low = (
        jnp.einsum(
            "chlm,cmhd->clhd", grad_scores_low, keys_heads, preferred_element_type=jnp.float32
        )
        * factor
    ).astype(jnp.bfloat16)
    grad_keys_low = (
        jnp.einsum(
            "chlm,clhd->cmhd", grad_scores_low, query_heads, preferred_element_type=jnp.float32
        )
        * factor
    ).astype(jnp.bfloat16)
    grad_query_low = grad_query_low.reshape(captions, length, width)
    grad_keys_low = grad_keys_low.reshape(captions, length, width)
    grad_values_low = grad_values_low.reshape(captions, length, width)
    querymat_grad = outer_sum(normed_low, grad_query_low)
    querybias_grad = token_sum(grad_query_low)
    keymat_grad = outer_sum(normed_low, grad_keys_low)
    valuemat_grad = outer_sum(normed_low, grad_values_low)
    valuebias_grad = token_sum(grad_values_low)
    grad_normed = (
        project_back(grad_query_low, query_w)
        + project_back(grad_keys_low, keys_w)
        + project_back(grad_values_low, values_w)
    )
    first_pull = jax.vjp(layer_norm, source, gain_one, shift_one)[1]
    grad_ln_one, attgain_grad, attshift_grad = first_pull(grad_normed)
    input_grad = grad_middle + grad_ln_one
    (
        attgain_grad,
        attshift_grad,
        querymat_grad,
        querybias_grad,
        keymat_grad,
        valuemat_grad,
        valuebias_grad,
        mixmat_grad,
        mixbias_grad,
    ) = (
        lax.psum_scatter(attgain_grad, ("dp", "fsdp"), scatter_dimension=0, tiled=True),
        lax.psum_scatter(attshift_grad, ("dp", "fsdp"), scatter_dimension=0, tiled=True),
        lax.psum_scatter(querymat_grad, ("dp", "fsdp"), scatter_dimension=1, tiled=True),
        lax.psum_scatter(querybias_grad, ("dp", "fsdp"), scatter_dimension=0, tiled=True),
        lax.psum_scatter(keymat_grad, ("dp", "fsdp"), scatter_dimension=1, tiled=True),
        lax.psum_scatter(valuemat_grad, ("dp", "fsdp"), scatter_dimension=1, tiled=True),
        lax.psum_scatter(valuebias_grad, ("dp", "fsdp"), scatter_dimension=0, tiled=True),
        lax.psum_scatter(mixmat_grad, ("dp", "fsdp"), scatter_dimension=1, tiled=True),
        lax.psum_scatter(mixbias_grad, ("dp", "fsdp"), scatter_dimension=0, tiled=True),
    )
    return (
        block_out,
        input_grad,
        attgain_grad,
        attshift_grad,
        querymat_grad,
        querybias_grad,
        keymat_grad,
        valuemat_grad,
        valuebias_grad,
        mixmat_grad,
        mixbias_grad,
        mlpgain_grad,
        mlpshift_grad,
        upmat_grad,
        upbias_grad,
        downmat_grad,
        downbias_grad,
    )


NT = (((1,), (1,)), ((), ()))
NN = (((1,), (0,)), ((), ()))
TN = (((0,), (0,)), ((), ()))
F32 = jnp.float32
BF16 = jnp.bfloat16
AXES = ("z", "x", "y", "c")
QUAD = 4
VMEM_LIMIT = 56 * 1024 * 1024


def dot(left, right, dims):
    return lax.dot_general(left, right, dims, preferred_element_type=F32)


class Grid3:
    def __init__(self, dp, fsdp):
        self.c = 2
        self.y = fsdp // 2
        self.x = self.y
        self.z = dp // self.x
        self.count = dp * fsdp

    def index(self, z, x, y, c):
        return ((z * self.x + x) * self.y + y) * self.c + c

    def shift(self, values, kz=0, kx=0, ky=0, kc=0):
        pairs = []
        for z in range(self.z):
            for x in range(self.x):
                for y in range(self.y):
                    for c in range(self.c):
                        target = self.index(
                            (z + kz) % self.z, (x + kx) % self.x, (y + ky) % self.y, (c + kc) % self.c
                        )
                        pairs.append((self.index(z, x, y, c), target))
        return lax.ppermute(values, AXES, pairs)

    def here(self):
        return tuple(lax.axis_index(name) for name in AXES)

    def me(self):
        return self.index(*self.here())

    def away(self, kz, kx, ky, kc):
        z, x, y, c = self.here()
        return self.index(
            lax.rem(z + (kz % self.z), self.z),
            lax.rem(x + (kx % self.x), self.x),
            lax.rem(y + (ky % self.y), self.y),
            lax.rem(c + (kc % self.c), self.c),
        )


def tie(values, gate):
    return lax.optimization_barrier((values, gate))[0]


def gather_begin(grid, own):
    rows = [own]
    for k in range(1, grid.z):
        rows.append(grid.shift(own, kz=k))
    half = grid.z // 2
    first = jnp.stack(rows[:half])
    second = jnp.stack(rows[half:])
    return first, second


def gather_middle(grid, begun):
    first, second = begun
    return first, second, grid.shift(first, kx=1), grid.shift(second, ky=1)


def gather_end(grid, begun):
    first, second, first_x, second_y = begun
    half = grid.z // 2
    first_y = grid.shift(first, ky=1)
    second_x = grid.shift(second, kx=1)
    first_xy = grid.shift(first_x, ky=1)
    second_xy = grid.shift(second_y, kx=1)
    arrays, places = [], []
    for array, start, kx, ky in (
        (first, 0, 0, 0),
        (second, half, 0, 0),
        (first_x, 0, 1, 0),
        (second_y, half, 0, 1),
        (first_y, 0, 0, 1),
        (second_x, half, 1, 0),
        (first_xy, 0, 1, 1),
        (second_xy, half, 1, 1),
    ):
        arrays.append(array)
        places.append([(-(start + k), -kx, -ky, 0) for k in range(half)])
        arrays.append(grid.shift(array, kc=1))
        places.append([(-(start + k), -kx, -ky, -1) for k in range(half)])
    return arrays, places


def place(grid, places, refs, held):
    for ref, spots in zip(refs, places):
        for slot, spot in enumerate(spots):
            held[grid.away(*spot)] = ref[slot]


def outgoing(grid, core):
    half = grid.z // 2
    slots = []
    for which in range(2):
        for one in range(2):
            for two in range(2):
                for low in range(half):
                    kx, ky = (one, two) if which == 0 else (two, one)
                    slots.append((which * half + low, kx, ky, core))
    return slots


def plus(left, right):
    return (left.astype(F32) + right.astype(F32)).astype(BF16)


def scatter_core(grid, other):
    return grid.shift(other, kc=1)


def scatter_first(grid, own, arrived):
    shape = (2, 2, 2, grid.z // 2) + own.shape[1:]
    own = own.reshape(shape)
    arrived = arrived.reshape(shape)
    send_a = plus(own[0, 1], arrived[0, 1])
    send_b = plus(own[1, 1], arrived[1, 1])
    keep_a = plus(own[0, 0], arrived[0, 0])
    keep_b = plus(own[1, 0], arrived[1, 0])
    return send_a, send_b, keep_a, keep_b, grid.shift(send_a, kx=1), grid.shift(send_b, ky=1)


def scatter_second(grid, state, gate):
    _, _, keep_a, keep_b, got_a, got_b = state
    got_a, got_b = tie((got_a, got_b), gate)
    next_a = plus(keep_a[1], got_a[1])
    next_b = plus(keep_b[1], got_b[1])
    rest_a = plus(keep_a[0], got_a[0])
    rest_b = plus(keep_b[0], got_b[0])
    return next_a, rest_a, rest_b, grid.shift(next_a, ky=1), grid.shift(next_b, kx=1)


def scatter_third(grid, state, gate):
    _, rest_a, rest_b, last_a, last_b = state
    last_a, last_b = tie((last_a, last_b), gate)
    half = grid.z // 2
    parts = [plus(rest_a[k], last_a[k]) for k in range(half)] + [plus(rest_b[k], last_b[k]) for k in range(half)]
    return parts + [grid.shift(parts[k], kz=k) for k in range(1, grid.z)]


def scatter_last(state, gate):
    count = (len(state) + 1) // 2
    came = tie(list(state[count:]), gate)
    total = state[0].astype(F32)
    for part in came:
        total = total + part.astype(F32)
    return total


def lanes_of(rows):
    return lax.broadcasted_iota(jnp.int32, (rows, 256), 1) // 64


def spread(block):
    head = lanes_of(block.shape[0])
    zero = jnp.zeros_like(block)
    return jnp.concatenate([jnp.where(head == g, block, zero) for g in range(QUAD)], axis=0)


def collect(square):
    head = lanes_of(64)
    total = jnp.where(head == 0, square[0:64], 0.0)
    for g in range(1, QUAD):
        total = jnp.where(head == g, square[64 * g : 64 * g + 64], total)
    return total


def normal(values):
    centre = jnp.mean(values, axis=-1, keepdims=True)
    centred = values - centre
    spread_of = jnp.mean(centred * centred, axis=-1, keepdims=True)
    scale = lax.rsqrt(spread_of + 1e-06)
    return centred * scale, scale


def normal_back(hat, scale, gain, grads):
    weighted = grads * gain
    middle = jnp.mean(weighted, axis=-1, keepdims=True)
    along = jnp.mean(weighted * hat, axis=-1, keepdims=True)
    return scale * (weighted - middle - hat * along)


TILE = 16
SIZES = (384, 512, 640, 768, 896, 1024)


def order_of(lengths, length):
    captions = lengths.shape[0]
    tiles = length // TILE
    real = (lengths + (TILE - 1)) // TILE
    before = jnp.tril(jnp.ones((captions, captions), jnp.int32), -1)
    start = jnp.sum(before * real[None, :], axis=1)
    total = jnp.sum(real)
    late = total + jnp.sum(before * (tiles - real)[None, :], axis=1)
    at = jnp.arange(tiles, dtype=jnp.int32)[None, :]
    spots = jnp.where(at < real[:, None], start[:, None] + at, late[:, None] + at - real[:, None])
    sizes = jnp.array(SIZES, jnp.int32)
    size = jnp.min(jnp.where(sizes >= total * TILE, sizes, SIZES[-1]))
    return jnp.concatenate([spots.reshape(-1), start, jnp.stack([size, total])]).astype(jnp.int32)


def tile_rows(place_ref, index):
    return pl.ds(pl.multiple_of(place_ref[index] * TILE, TILE), TILE)


def by_size(size, body):
    for rows in SIZES:
        pl.when(size == rows)(functools.partial(body, rows))


def rows_at(step, rows):
    return pl.ds(pl.multiple_of(step * rows, rows), rows)


def pack_kernel(grid, small_ref, up_ref, q_ref, k_ref, v_ref, out_ref, wide):
    wide[...] = jnp.zeros_like(wide)
    wide[0:8, 0:24] = small_ref[...]
    wide[8:9, 0:96] = up_ref[...]
    me = grid.me()
    eight = pltpu.roll(wide[0:8, :], me * 24, 1)
    four = pltpu.roll(wide[8:16, :], lax.rem(me, 8) * 96, 1)
    row = lax.broadcasted_iota(jnp.int32, (8, 768), 0)
    four = jnp.where(row == lax.div(me, 8), jnp.broadcast_to(four[0:1], (8, 768)), 0.0)
    zero = jnp.zeros((8, 768), F32)
    out_ref[0] = jnp.concatenate([eight, four, zero], axis=0).astype(BF16)
    out_ref[1] = q_ref[...]
    out_ref[2] = k_ref[...]
    out_ref[3] = v_ref[...]


def project_kernel(grid, places, place_ref, hidden_ref, *rest):
    count = len(places)
    refs, rest = rest[:count], rest[count:]
    moved_ref, normed_out, q_ref, k_ref, v_ref, vec_ref, held = rest
    place(grid, places, refs, held)
    width = hidden_ref.shape[1]
    total = held[0, 0].astype(F32)
    for j in range(1, grid.count):
        total = total + held[j, 0].astype(F32)
    vec_ref[...] = total
    rows = 256

    def block(step, carry):
        at = rows_at(step, rows)
        hidden = hidden_ref[at, :]
        hat, _ = normal(hidden.astype(F32))
        normed = (hat * vec_ref[0:1, :] + vec_ref[1:2, :]).astype(BF16)
        q_ref[at, :] = (dot(normed, held[:, 1].reshape(width, width), NT) + vec_ref[2:3, :]).astype(BF16)
        k_ref[at, :] = dot(normed, held[:, 2].reshape(width, width), NT).astype(BF16)
        v_ref[at, :] = (dot(normed, held[:, 3].reshape(width, width), NT) + vec_ref[3:4, :]).astype(BF16)
        for t in range(rows // TILE):
            to = tile_rows(place_ref, step * (rows // TILE) + t)
            part = slice(t * TILE, (t + 1) * TILE)
            normed_out[to, :] = normed[part, :]
            moved_ref[to, :] = hidden[part, :]
        return carry

    lax.fori_loop(0, hidden_ref.shape[0] // rows, block, 0)


def attend_kernel(length, group, lengths_ref, place_ref, q_ref, k_ref, v_ref, probs_ref, mixed_out):
    width = q_ref.shape[1]
    captions = q_ref.shape[0] // length
    tiles = length // TILE
    quads = width // 256
    position = lax.broadcasted_iota(jnp.int32, (length, 256), 0)

    def several(step, carry):
        items = [
            (step * group + g, quad, rows_at(step * group + g, length), slice(256 * quad, 256 * quad + 256))
            for g in range(group)
            for quad in range(quads)
        ]
        scores = [dot(k_ref[rows, lanes], spread(q_ref[rows, lanes]), NT) for _, _, rows, lanes in items]
        probs = []
        for (cap, _, _, _), score in zip(items, scores):
            score = jnp.where(position < lengths_ref[cap], score * 0.125, -1e30)
            raised = jnp.exp(score - jnp.max(score, axis=0, keepdims=True))
            probs.append((raised * (1.0 / jnp.sum(raised, axis=0, keepdims=True))).astype(BF16))
        for (cap, quad, _, _), prob in zip(items, probs):
            probs_ref[cap * quads + quad] = prob
        mixed = [
            collect(dot(prob, v_ref[rows, lanes], TN)).astype(BF16)
            for (_, _, rows, lanes), prob in zip(items, probs)
        ]
        for (cap, _, _, lanes), value in zip(items, mixed):
            for t in range(tiles):
                to = tile_rows(place_ref, cap * tiles + t)
                mixed_out[to, lanes] = value[t * TILE : (t + 1) * TILE, :]
        return carry

    lax.fori_loop(0, captions // group, several, 0)


def upper_kernel(grid, places, moved_ref, mixed_ref, vec_ref, *rest):
    count = len(places)
    refs, rest = rest[:count], rest[count:]
    middle_ref, normed_ref, active_ref, slope_ref, held = rest
    place(grid, places, refs, held)
    width = moved_ref.shape[1]
    per = grid.count // 4
    rows = 256
    root = math.sqrt(2.0 / math.pi)

    def block(step, carry):
        at = rows_at(step, rows)
        middle = (
            moved_ref[at, :].astype(F32)
            + dot(mixed_ref[at, :], held[:, 0].reshape(width, width), NT)
            + vec_ref[4:5, :]
        )
        middle_ref[at, :] = middle
        hat, _ = normal(middle)
        normed = (hat * vec_ref[5:6, :] + vec_ref[6:7, :]).astype(BF16)
        normed_ref[at, :] = normed
        for part in range(4):
            weight = held[per * part : per * part + per, 1:5].reshape(width, width)
            upper = dot(normed, weight, NT) + vec_ref[8 + part : 9 + part, :]
            square = upper * upper
            bend = jnp.tanh(upper * (root + (root * 0.044715) * square))
            half = 0.5 * bend + 0.5
            span = slice(width * part, width * part + width)
            active = upper * half
            active_ref[at, span] = active.astype(BF16)
            slope = half + active * ((1.0 - bend) * (root + (3.0 * root * 0.044715) * square))
            slope_ref[at, span] = slope.astype(BF16)
        return carry

    lax.fori_loop(0, moved_ref.shape[0] // rows, block, 0)


def down_grad_kernel(grid, length, size_at, lengths_ref, place_ref, cot_ref, active_ref, low_ref, vec_ref, own_ref, other_ref, total):
    width = cot_ref.shape[1]
    captions = cot_ref.shape[0] // length
    tiles = length // TILE
    position = lax.broadcasted_iota(jnp.int32, (length, 1), 0)
    vec_ref[...] = jnp.zeros_like(vec_ref)

    def caption(cap, carry):
        part = cot_ref[rows_at(cap, length), :].astype(F32)
        part = jnp.where(position < lengths_ref[cap], part, 0.0)
        vec_ref[0:1, :] += jnp.sum(part, axis=0, keepdims=True)
        part = part.astype(BF16)
        for t in range(tiles):
            low_ref[tile_rows(place_ref, cap * tiles + t), :] = part[t * TILE : (t + 1) * TILE, :]
        return carry

    lax.fori_loop(0, captions, caption, 0)
    share = width // grid.count
    core = lax.axis_index("c")

    def column(step, carry):
        lanes = rows_at(step, width)

        def product(rows):
            total[...] = dot(low_ref[0:rows, :], active_ref[0:rows, lanes], TN)

        by_size(place_ref[size_at], product)
        for out_ref, owner in ((own_ref, core), (other_ref, 1 - core)):
            slot = 0
            for x in range(grid.x):
                for y in range(grid.y):
                    for z in range(grid.z):
                        at = pl.multiple_of(grid.index(z, x, y, owner) * share, 8)
                        out_ref[slot, :, lanes] = total[pl.ds(at, share), :].astype(BF16)
                        slot += 1
        return carry

    lax.fori_loop(0, active_ref.shape[1] // width, column, 0)


def upper_grad_kernel(grid, places, size_at, place_ref, low_ref, slope_ref, normed_ref, *rest):
    count = len(places)
    refs, rest = rest[:count], rest[count:]
    upper_ref, vec_ref, own_ref, other_ref, held, total = rest
    place(grid, places, refs, held)
    width = low_ref.shape[1]
    per = grid.count // 4
    share = width // per
    half = grid.z // 2
    z, x, y, c = grid.here()
    shape = own_ref.shape[1:]
    mine = jnp.where(c == 0, 0, share)

    def column(step, carry):
        lanes = rows_at(step, width)

        def product(rows):
            grads = dot(low_ref[0:rows, :], held[:, :, lanes].reshape(width, width), NN) * slope_ref[0:rows, lanes].astype(F32)
            vec_ref[rows_at(step, 8), :] = jnp.broadcast_to(jnp.sum(grads, axis=0, keepdims=True), (8, width))
            grads = grads.astype(BF16)
            upper_ref[0:rows, lanes] = grads
            total[...] = dot(grads, normed_ref[0:rows, :], TN)

        by_size(place_ref[size_at], product)
        for k in range(per // 2):
            chip = step * (per // 2) + k
            kz = lax.rem(lax.div(chip, grid.x * grid.y) - z + grid.z, grid.z)
            kx = lax.rem(lax.rem(lax.div(chip, grid.y), grid.x) - x + grid.x, grid.x)
            ky = lax.rem(lax.rem(chip, grid.y) - y + grid.y, grid.y)
            which = lax.div(kz, half)
            one = jnp.where(which == 0, kx, ky)
            two = jnp.where(which == 0, ky, kx)
            slot = ((which * 2 + one) * 2 + two) * half + lax.rem(kz, half)
            own_at = pl.multiple_of(2 * share * k + mine, 8)
            other_at = pl.multiple_of(2 * share * k + (share - mine), 8)
            own_ref[slot] = total[pl.ds(own_at, share), :].astype(BF16).reshape(shape)
            other_ref[slot] = total[pl.ds(other_at, share), :].astype(BF16).reshape(shape)
        return carry

    lax.fori_loop(0, upper_ref.shape[1] // width, column, 0)


def middle_grad_kernel(grid, size_at, place_ref, upper_ref, middle_ref, low_ref, vec_in, held, grad_ref, branch_ref, dm_ref, vec_ref):
    width = middle_ref.shape[1]
    per = grid.count // 4
    rows = 128
    vec_ref[...] = jnp.zeros_like(vec_ref)

    def block(step, carry):
        at = rows_at(step, rows)
        grads = dot(upper_ref[at, 0:width], held[0:per, 1:5].reshape(width, width), NN)
        for part in range(1, 4):
            weight = held[per * part : per * part + per, 1:5].reshape(width, width)
            grads = grads + dot(upper_ref[at, width * part : width * part + width], weight, NN)
        hat, scale = normal(middle_ref[at, :])
        grad_middle = low_ref[at, :].astype(F32) + normal_back(hat, scale, vec_in[5:6, :], grads)
        grad_ref[at, :] = grad_middle
        branch = grad_middle.astype(BF16)
        branch_ref[at, :] = branch
        dm_ref[at, :] = dot(branch, held[:, 0].reshape(width, width), NN).astype(BF16)
        vec_ref[0:1, :] += jnp.sum(grads * hat, axis=0, keepdims=True)
        vec_ref[1:2, :] += jnp.sum(grads, axis=0, keepdims=True)
        vec_ref[2:3, :] += jnp.sum(grad_middle, axis=0, keepdims=True)
        return carry

    lax.fori_loop(0, lax.div(place_ref[size_at], rows), block, 0)


def attend_grad_kernel(length, group, lengths_ref, place_ref, dm_ref, q_ref, k_ref, v_ref, probs_ref, grads_ref, vec_ref):
    width = dm_ref.shape[1]
    quads = width // 256
    tiles = length // TILE
    captions = probs_ref.shape[0] // quads
    starts = captions * tiles
    end = place_ref[starts + captions + 1]
    clear = pl.ds(pl.multiple_of(end * TILE, TILE), 256)
    for which in range(3):
        grads_ref[which, clear, :] = jnp.zeros((256, width), BF16)
    vec_ref[...] = jnp.zeros_like(vec_ref)
    row = lax.broadcasted_iota(jnp.int32, (length, 1), 0)

    def several(step, carry):
        items = []
        for g in range(group):
            cap = step * group + g
            packed = pl.ds(pl.multiple_of(place_ref[starts + cap] * TILE, TILE), length)
            plain = pl.ds(pl.multiple_of(cap * length, length), length)
            for quad in range(quads):
                items.append((cap, quad, packed, plain, slice(256 * quad, 256 * quad + 256)))
        probs = [probs_ref[cap * quads + quad] for cap, quad, _, _, _ in items]
        wide = []
        for cap, _, packed, _, lanes in items:
            dm = dm_ref[packed, lanes]
            wide.append(spread(jnp.where(row < lengths_ref[cap], dm, jnp.zeros_like(dm))))
        grad_probs = [dot(v_ref[plain, lanes], w, NT) for (_, _, _, plain, lanes), w in zip(items, wide)]
        grad_values = [dot(p, w, NN) for p, w in zip(probs, wide)]
        grad_scores = []
        for p, grad in zip(probs, grad_probs):
            p = p.astype(F32)
            along = p * grad
            grad_scores.append((along - p * jnp.sum(along, axis=0, keepdims=True)).astype(BF16))
        grad_keys = [
            dot(g, spread(q_ref[plain, lanes]), NN) * 0.125 for (_, _, _, plain, lanes), g in zip(items, grad_scores)
        ]
        grad_query = [
            collect(dot(g, k_ref[plain, lanes], TN)) * 0.125 for (_, _, _, plain, lanes), g in zip(items, grad_scores)
        ]
        for at, (_, _, packed, _, lanes) in enumerate(items):
            grads_ref[0, packed, lanes] = grad_query[at].astype(BF16)
            grads_ref[1, packed, lanes] = grad_keys[at].astype(BF16)
            grads_ref[2, packed, lanes] = grad_values[at].astype(BF16)
        for quad in range(quads):
            lanes = slice(256 * quad, 256 * quad + 256)
            vec_ref[0:1, lanes] += sum(jnp.sum(v, axis=0, keepdims=True) for v in grad_query[quad::quads])
            vec_ref[1:2, lanes] += sum(jnp.sum(v, axis=0, keepdims=True) for v in grad_values[quad::quads])
        return carry

    lax.fori_loop(0, captions // group, several, 0)


def weight_grad_kernel(grid, size_at, place_ref, grads_ref, branch_ref, normed_ref, mixed_ref, own_ref, other_ref, total):
    share = total.shape[0] // grid.count

    def send(at):
        for core, out_ref in ((0, own_ref), (1, other_ref)):
            for slot, spot in enumerate(outgoing(grid, core)):
                start = pl.multiple_of(grid.away(*spot) * share, 8)
                out_ref[slot, at] = total[pl.ds(start, share), :].astype(BF16)

    def matrix(at, carry):
        def product(rows):
            total[...] = dot(grads_ref[at, 0:rows, :], normed_ref[0:rows, :], TN)

        by_size(place_ref[size_at], product)
        send(at)
        return carry

    lax.fori_loop(0, 3, matrix, 0)

    def product(rows):
        total[...] = dot(branch_ref[0:rows, :], mixed_ref[0:rows, :], TN)

    by_size(place_ref[size_at], product)
    send(3)


def input_grad_kernel(grid, size_at, place_ref, moved_ref, grad_ref, grads_ref, vec_in, down_vec, up_vec, mid_vec, att_vec, held, out_ref, vec_ref, found):
    rows = 128
    width = moved_ref.shape[1]
    vec_ref[...] = jnp.zeros_like(vec_ref)
    vec_ref[2:4, :] = att_vec[0:2, :]
    vec_ref[4:5, :] = mid_vec[2:3, :]
    vec_ref[5:7, :] = mid_vec[0:2, :]
    vec_ref[7:8, :] = down_vec[0:1, :]
    for part in range(4):
        vec_ref[8 + part : 9 + part, :] = up_vec[8 * part : 8 * part + 1, :]

    def block(step, carry):
        at = rows_at(step, rows)
        grads = dot(grads_ref[0, at, :], held[:, 1].reshape(width, width), NN)
        grads = grads + dot(grads_ref[1, at, :], held[:, 2].reshape(width, width), NN)
        grads = grads + dot(grads_ref[2, at, :], held[:, 3].reshape(width, width), NN)
        hat, scale = normal(moved_ref[at, :].astype(F32))
        found[at, :] = grad_ref[at, :] + normal_back(hat, scale, vec_in[0:1, :], grads)
        vec_ref[0:1, :] += jnp.sum(grads * hat, axis=0, keepdims=True)
        vec_ref[1:2, :] += jnp.sum(grads, axis=0, keepdims=True)
        return carry

    lax.fori_loop(0, lax.div(place_ref[size_at], rows), block, 0)
    total = place_ref[size_at + 1]

    def tile(index, carry):
        values = found[tile_rows(place_ref, index), :]
        out_ref[rows_at(index, TILE), :] = jnp.where(place_ref[index] < total, values, 0.0)
        return carry

    lax.fori_loop(0, out_ref.shape[0] // TILE, tile, 0)


def lower_kernel(place_ref, active_ref, middle_ref, vec_in, weight_ref, out_ref, found):
    step = pl.program_id(0)
    rows = middle_ref.shape[0]
    weight = weight_ref[...].reshape(middle_ref.shape[1], active_ref.shape[1])
    out = middle_ref[...] + dot(active_ref[...], weight, NT) + vec_in[7:8, :]
    found[rows_at(step, rows), :] = out.astype(BF16)

    @pl.when(step == pl.num_programs(0) - 1)
    def _():
        for index in range(out_ref.shape[0] // TILE):
            out_ref[index * TILE : (index + 1) * TILE, :] = found[tile_rows(place_ref, index), :]


def unpack_kernel(grid, vec_ref, *outs):
    me = grid.me()
    eight = pltpu.roll(vec_ref[0:8, :], lax.rem(768 - me * 24, 768), 1)
    for k in range(8):
        outs[k][...] = eight[k : k + 1, 0:24]
    row = lax.broadcasted_iota(jnp.int32, (8, 768), 0)
    four = jnp.sum(jnp.where(row == lax.div(me, 8), vec_ref[8:16, :], 0.0), axis=0, keepdims=True)
    four = jnp.broadcast_to(four, (8, 768))
    four = pltpu.roll(four, lax.rem(768 - lax.rem(me, 8) * 96, 768), 1)
    outs[8][...] = four[0:1, 0:96]


def whole(shape):
    return pl.BlockSpec(shape, lambda *_: (0,) * len(shape))


ANY = pl.BlockSpec(memory_space=pl.ANY)
SMEM = pl.BlockSpec(memory_space=pltpu.SMEM)


FAST = pl.BlockSpec(memory_space=pltpu.VMEM)


def call(kernel, steps, in_specs, out_specs, outs, scratch, flops, moved, name, limit=10):
    return pl.pallas_call(
        kernel,
        grid=(steps,),
        in_specs=in_specs,
        out_specs=out_specs,
        out_shape=[jax.ShapeDtypeStruct(s, d) for s, d in outs],
        scratch_shapes=scratch,
        compiler_params=pltpu.CompilerParams(vmem_limit_bytes=limit * 1024 * 1024),
        cost_estimate=pl.CostEstimate(flops=flops, bytes_accessed=moved, transcendentals=0),
        name=name,
    )


def call_near(kernel, in_specs, outs, scratch, flops, name, limit=10):
    return pl.pallas_call(
        kernel,
        in_specs=in_specs,
        out_specs=[FAST] * len(outs),
        out_shape=[jax.ShapeDtypeStruct(s, d) for s, d in outs],
        scratch_shapes=scratch,
        compiler_params=pltpu.CompilerParams(vmem_limit_bytes=limit * 1024 * 1024),
        cost_estimate=pl.CostEstimate(flops=flops, bytes_accessed=1_000_000, transcendentals=0),
        name=name,
    )


def fast_device(
    grid,
    hidden,
    lengths,
    cotangent,
    attgain,
    attshift,
    querymat,
    querybias,
    keymat,
    valuemat,
    valuebias,
    mixmat,
    mixbias,
    mlpgain,
    mlpshift,
    upmat_w,
    upbias,
    downmat,
    downbias,
):
    captions, length, width = hidden.shape
    tokens = captions * length
    hidden2 = hidden.reshape(tokens, width)
    cot2 = cotangent.reshape(tokens, width)
    share = width // grid.count
    ff = downmat.shape[0]
    small = jnp.stack(
        [attgain, attshift, querybias, valuebias, mixbias, mlpgain, mlpshift, downbias]
    ).astype(F32)
    upsmall = upbias.astype(F32).reshape(1, -1)
    first = call(
        functools.partial(pack_kernel, grid),
        1,
        [whole((8, share)), whole((1, 96))] + [whole((share, width))] * 3,
        [whole((4, share, width))],
        [((4, share, width), BF16)],
        [pltpu.VMEM((16, width), F32)],
        1000,
        1000,
        "pack",
    )(small, upsmall, querymat.T, keymat.T, valuemat.T)[0]
    second = jnp.concatenate([mixmat.T[None], upmat_w.T.reshape(4, share, width)], axis=0)
    third = downmat.T
    where = order_of(lengths, length)
    size_at = captions * (length // TILE) + captions
    begun = lax.optimization_barrier(gather_begin(grid, first))
    second_begun = lax.optimization_barrier(gather_begin(grid, tie(second, begun)))
    third_begun = lax.optimization_barrier(gather_begin(grid, tie(third, second_begun)))
    begun = lax.optimization_barrier(gather_middle(grid, begun))
    first_in, places = gather_end(grid, begun)
    second_begun = gather_middle(grid, tie(second_begun, first_in))
    half = grid.count // 2
    unit = 2 * tokens * width * width
    row = (tokens, width)
    heads = captions * (width // 256)
    tall = (tokens + 64, width)
    square = pltpu.VMEM((width, width), F32)
    moved, normed, query, keys, values, vec, held_one = call_near(
        functools.partial(project_kernel, grid, places),
        [SMEM] + [FAST] * (1 + len(first_in)),
        [(row, BF16)] * 5 + [((share, width), F32), ((grid.count,) + first.shape, BF16)],
        [],
        5 * unit,
        "project",
    )(where, hidden2, *first_in)
    second_begun, third_begun = tie((second_begun, third_begun), vec)
    second_in, _ = gather_end(grid, second_begun)
    third_begun = gather_middle(grid, third_begun)
    probs, mixed = call_near(
        functools.partial(attend_kernel, length, 4),
        [SMEM] * 2 + [FAST] * 3,
        [((heads, length, 256), BF16), (row, BF16)],
        [],
        5 * unit,
        "attend",
    )(lengths, where, query, keys, values)
    third_in, _ = gather_end(grid, tie(third_begun, second_in))
    middle, normed2, active, slope, held_two = call_near(
        functools.partial(upper_kernel, grid, places),
        [FAST] * (3 + len(second_in)),
        [(row, F32), (row, BF16), ((tokens, ff), BF16), ((tokens, ff), BF16), ((grid.count,) + second.shape, BF16)],
        [],
        9 * unit,
        "upper",
    )(moved, mixed, vec, *second_in)
    low, down_vec, down_own, down_other = call_near(
        functools.partial(down_grad_kernel, grid, length, size_at),
        [SMEM] * 2 + [FAST] * 2,
        [(row, BF16), ((8, width), F32)] + [((half, share, ff), BF16)] * 2,
        [square],
        5 * unit,
        "down_grad",
    )(lengths, where, cot2, active)
    down_came = grid.shift(down_other, kc=1)
    grad_upper, up_vec, up_own, up_other, lower_w = call_near(
        functools.partial(upper_grad_kernel, grid, places, size_at),
        [SMEM] + [FAST] * (3 + len(third_in)),
        [((tokens, ff), BF16), ((32, width), F32)]
        + [((half, 4, share, width), BF16)] * 2
        + [((grid.count, share, ff), BF16)],
        [square],
        8 * unit,
        "upper_grad",
    )(where, low, slope, normed2, *third_in)
    down_came = tie(down_came, up_vec)
    down_part = down_own.astype(F32) + down_came.astype(F32)
    down_part = down_part.astype(BF16).reshape(half * share, ff)
    down_part = lax.psum_scatter(down_part, ("x", "y"), scatter_dimension=0, tiled=True)
    up_one = scatter_core(grid, up_other)
    grad_middle, branch, dm, mid_vec = call_near(
        functools.partial(middle_grad_kernel, grid, size_at),
        [SMEM] + [FAST] * 5,
        [(row, F32), (row, BF16), (tall, BF16), ((8, width), F32)],
        [],
        6 * unit,
        "middle_grad",
    )(where, grad_upper, middle, low, vec, held_two)
    up_two = scatter_first(grid, up_own, tie(up_one, mid_vec))
    dm = tie(dm, up_two[0])
    grads, att_vec = call_near(
        functools.partial(attend_grad_kernel, length, 4),
        [SMEM] * 2 + [FAST] * 5,
        [((3, tokens + 256, width), BF16), ((8, width), F32)],
        [],
        7 * unit,
        "attend_grad",
    )(lengths, where, dm, query, keys, values, probs)
    up_three = scatter_second(grid, up_two, att_vec)
    grads = tie(grads, up_three[0])
    att_own, att_other = call_near(
        functools.partial(weight_grad_kernel, grid, size_at),
        [SMEM] + [FAST] * 4,
        [((half, 4, share, width), BF16)] * 2,
        [square],
        5 * unit,
        "weight_grad",
    )(where, grads, branch, normed, mixed)
    up_four = scatter_third(grid, up_three, att_own[0, 0, 0:8, 0:128])
    att_one = scatter_core(grid, att_other)
    grad_middle = tie(grad_middle, up_four[0])
    input_grad, all_vec = call_near(
        functools.partial(input_grad_kernel, grid, size_at),
        [SMEM] + [FAST] * 9,
        [(row, F32), ((16, width), F32)],
        [pltpu.VMEM(row, F32)],
        5 * unit,
        "input_grad",
    )(where, moved, grad_middle, grads, vec, down_vec, up_vec, mid_vec, att_vec, held_one)
    att_two = scatter_first(grid, att_own, tie(att_one, all_vec))
    up_sum = scatter_last(up_four, all_vec)
    middle = tie(middle, att_two[0])
    steps = 4
    rows = tokens // steps
    block = pl.BlockSpec((rows, width), lambda i: (i, 0))
    (block_out,) = call(
        lower_kernel,
        steps,
        [SMEM, pl.BlockSpec((rows, ff), lambda i: (i, 0)), block, whole((share, width)), whole((grid.count, share, ff))],
        [whole(row)],
        [(row, BF16)],
        [pltpu.VMEM(row, BF16)],
        4 * unit,
        20_000_000,
        "lower",
        24,
    )(where, active, middle, vec, lower_w)
    att_three = scatter_second(grid, att_two, block_out[0:8, 0:128])
    att_four = scatter_third(grid, att_three, block_out[0:8, 0:128])
    att_sum = scatter_last(att_four, block_out[0:8, 0:128])
    down_sum = lax.psum_scatter(down_part, "z", scatter_dimension=0, tiled=True).astype(F32)
    all_vec = all_vec + grid.shift(all_vec, kc=1)
    all_vec = all_vec + grid.shift(all_vec, kx=1)
    all_vec = all_vec + grid.shift(all_vec, ky=1)
    all_vec = (
        all_vec + grid.shift(all_vec, kz=1) + grid.shift(all_vec, kz=2) + grid.shift(all_vec, kz=3)
    )
    vecs = call(
        functools.partial(unpack_kernel, grid),
        1,
        [whole((16, width))],
        [whole((1, share))] * 8 + [whole((1, ff // grid.count))],
        [((1, share), F32)] * 8 + [((1, ff // grid.count), F32)],
        [],
        1000,
        1000,
        "unpack",
    )(all_vec)
    vecs = [v.reshape(-1) for v in vecs]
    return (
        block_out.reshape(hidden.shape),
        input_grad.reshape(hidden.shape),
        vecs[0],
        vecs[1],
        att_sum[0].T,
        vecs[2],
        att_sum[1].T,
        att_sum[2].T,
        vecs[3],
        att_sum[3].T,
        vecs[4],
        vecs[5],
        vecs[6],
        up_sum.reshape(ff // grid.count, width).T,
        vecs[8],
        down_sum.T,
        vecs[7],
    )


def fits(mesh):
    return mesh.shape["dp"] == 8 and mesh.shape["fsdp"] == 4


def solution(mesh):
    axes = ("dp", "fsdp")
    body = per_device
    if fits(mesh):
        axes = AXES
        grid = Grid3(mesh.shape["dp"], mesh.shape["fsdp"])
        mesh = jax.sharding.Mesh(mesh.devices.reshape(grid.z, grid.x, grid.y, grid.c), AXES)
        body = functools.partial(fast_device, grid)
    placed = (
        P(axes, None, None),
        P(axes),
        P(axes, None, None),
        P(axes),
        P(axes),
        P(None, axes),
        P(axes),
        P(None, axes),
        P(None, axes),
        P(axes),
        P(None, axes),
        P(axes),
        P(axes),
        P(axes),
        P(None, axes),
        P(axes),
        P(None, axes),
        P(axes),
    )
    return jax.shard_map(
        body,
        mesh=mesh,
        in_specs=placed,
        out_specs=(
            P(axes, None, None),
            P(axes, None, None),
            P(axes),
            P(axes),
            P(None, axes),
            P(axes),
            P(None, axes),
            P(None, axes),
            P(axes),
            P(None, axes),
            P(axes),
            P(axes),
            P(axes),
            P(None, axes),
            P(axes),
            P(None, axes),
            P(axes),
        ),
        check_vma=False,
    )
```

```python
import functools
import math

import jax
import jax.numpy as jnp
from jax import lax
from jax.experimental import pallas as pl
from jax.experimental.pallas import tpu as pltpu
from jax.sharding import PartitionSpec as P

HEADS = 12


def layer_norm(values, gain, shift):
    centre = jnp.mean(values, axis=-1, keepdims=True)
    centred = values - centre
    spread = jnp.mean(centred * centred, axis=-1, keepdims=True)
    return centred * lax.rsqrt(spread + 1e-06) * gain + shift


def smooth(values):
    return jax.nn.gelu(values, approximate=True)


def project(inputs, matrix):
    return jnp.einsum("cli,ij->clj", inputs, matrix, preferred_element_type=jnp.float32)


def project_back(grads, matrix):
    return jnp.einsum("clj,ij->cli", grads, matrix, preferred_element_type=jnp.float32)


def outer_sum(inputs, grads):
    return jnp.einsum("cli,clj->ij", inputs, grads, preferred_element_type=jnp.float32)


def token_sum(grads):
    return jnp.sum(grads.astype(jnp.float32), axis=(0, 1))


def masked_scores(query_low, keys_low, keymask, factor):
    raw = (
        jnp.einsum("clhd,cmhd->chlm", query_low, keys_low, preferred_element_type=jnp.float32)
        * factor
    )
    return jnp.where(keymask[:, None, None, :], raw, -1e30)


def per_device(
    hidden,
    lengths,
    cotangent,
    attgain,
    attshift,
    querymat,
    querybias,
    keymat,
    valuemat,
    valuebias,
    mixmat,
    mixbias,
    mlpgain,
    mlpshift,
    upmat_w,
    upbias,
    downmat,
    downbias,
):
    captions, length, width = hidden.shape
    head_size = width // HEADS
    factor = 1.0 / math.sqrt(head_size)
    positions = lax.broadcasted_iota(jnp.int32, (captions, length), 1)
    keymask = positions < lengths[:, None]
    rowmask = keymask.astype(jnp.float32)[..., None]
    gathered = (
        lax.all_gather(attgain, ("dp", "fsdp"), axis=0, tiled=True),
        lax.all_gather(attshift, ("dp", "fsdp"), axis=0, tiled=True),
        lax.all_gather(querymat, ("dp", "fsdp"), axis=1, tiled=True),
        lax.all_gather(querybias, ("dp", "fsdp"), axis=0, tiled=True),
        lax.all_gather(keymat, ("dp", "fsdp"), axis=1, tiled=True),
        lax.all_gather(valuemat, ("dp", "fsdp"), axis=1, tiled=True),
        lax.all_gather(valuebias, ("dp", "fsdp"), axis=0, tiled=True),
        lax.all_gather(mixmat, ("dp", "fsdp"), axis=1, tiled=True),
        lax.all_gather(mixbias, ("dp", "fsdp"), axis=0, tiled=True),
        lax.all_gather(mlpgain, ("dp", "fsdp"), axis=0, tiled=True),
        lax.all_gather(mlpshift, ("dp", "fsdp"), axis=0, tiled=True),
        lax.all_gather(upmat_w, ("dp", "fsdp"), axis=1, tiled=True),
        lax.all_gather(upbias, ("dp", "fsdp"), axis=0, tiled=True),
        lax.all_gather(downmat, ("dp", "fsdp"), axis=1, tiled=True),
        lax.all_gather(downbias, ("dp", "fsdp"), axis=0, tiled=True),
    )
    (
        gain_one,
        shift_one,
        query_w,
        query_b,
        keys_w,
        values_w,
        values_b,
        mixer_w,
        mixer_b,
        gain_two,
        shift_two,
        upper_w,
        upper_b,
        lower_w,
        lower_b,
    ) = gathered
    gain_one = gain_one.astype(jnp.float32)
    shift_one = shift_one.astype(jnp.float32)
    gain_two = gain_two.astype(jnp.float32)
    shift_two = shift_two.astype(jnp.float32)
    source = hidden.astype(jnp.float32)
    normed_low = layer_norm(source, gain_one, shift_one).astype(jnp.bfloat16)
    query_low = (project(normed_low, query_w) + query_b.astype(jnp.float32)).astype(jnp.bfloat16)
    keys_low = project(normed_low, keys_w).astype(jnp.bfloat16)
    values_low = (project(normed_low, values_w) + values_b.astype(jnp.float32)).astype(jnp.bfloat16)
    query_heads = query_low.reshape(captions, length, HEADS, head_size)
    keys_heads = keys_low.reshape(captions, length, HEADS, head_size)
    values_heads = values_low.reshape(captions, length, HEADS, head_size)
    scores = masked_scores(query_heads, keys_heads, keymask, factor)
    peak = jnp.max(scores, axis=-1, keepdims=True)
    logsum = peak + jnp.log(jnp.sum(jnp.exp(scores - peak), axis=-1, keepdims=True))
    probs_low = jnp.exp(scores - logsum).astype(jnp.bfloat16)
    mixed_low = (
        jnp.einsum("chlm,cmhd->clhd", probs_low, values_heads, preferred_element_type=jnp.float32)
        .reshape(captions, length, width)
        .astype(jnp.bfloat16)
    )
    middle = source + project(mixed_low, mixer_w) + mixer_b.astype(jnp.float32)
    normed2_low = layer_norm(middle, gain_two, shift_two).astype(jnp.bfloat16)
    upper = project(normed2_low, upper_w) + upper_b.astype(jnp.float32)
    active_low = smooth(upper).astype(jnp.bfloat16)
    result = middle + project(active_low, lower_w) + lower_b.astype(jnp.float32)
    block_out = result.astype(jnp.bfloat16)
    again = (
        lax.all_gather(attgain, ("dp", "fsdp"), axis=0, tiled=True),
        lax.all_gather(attshift, ("dp", "fsdp"), axis=0, tiled=True),
        lax.all_gather(querymat, ("dp", "fsdp"), axis=1, tiled=True),
        lax.all_gather(querybias, ("dp", "fsdp"), axis=0, tiled=True),
        lax.all_gather(keymat, ("dp", "fsdp"), axis=1, tiled=True),
        lax.all_gather(valuemat, ("dp", "fsdp"), axis=1, tiled=True),
        lax.all_gather(valuebias, ("dp", "fsdp"), axis=0, tiled=True),
        lax.all_gather(mixmat, ("dp", "fsdp"), axis=1, tiled=True),
        lax.all_gather(mixbias, ("dp", "fsdp"), axis=0, tiled=True),
        lax.all_gather(mlpgain, ("dp", "fsdp"), axis=0, tiled=True),
        lax.all_gather(mlpshift, ("dp", "fsdp"), axis=0, tiled=True),
        lax.all_gather(upmat_w, ("dp", "fsdp"), axis=1, tiled=True),
        lax.all_gather(upbias, ("dp", "fsdp"), axis=0, tiled=True),
        lax.all_gather(downmat, ("dp", "fsdp"), axis=1, tiled=True),
        lax.all_gather(downbias, ("dp", "fsdp"), axis=0, tiled=True),
    )
    (
        gain_one,
        shift_one,
        query_w,
        query_b,
        keys_w,
        values_w,
        values_b,
        mixer_w,
        mixer_b,
        gain_two,
        shift_two,
        upper_w,
        upper_b,
        lower_w,
        lower_b,
    ) = again
    gain_one = gain_one.astype(jnp.float32)
    shift_one = shift_one.astype(jnp.float32)
    gain_two = gain_two.astype(jnp.float32)
    shift_two = shift_two.astype(jnp.float32)
    grad_out = cotangent.astype(jnp.float32) * rowmask
    grad_low = grad_out.astype(jnp.bfloat16)
    downmat_grad = outer_sum(active_low, grad_low)
    downbias_grad = token_sum(grad_low)
    grad_active = project_back(grad_low, lower_w)
    gelu_pull = jax.vjp(smooth, upper)[1]
    grad_upper_low = gelu_pull(grad_active)[0].astype(jnp.bfloat16)
    upmat_grad = outer_sum(normed2_low, grad_upper_low)
    upbias_grad = token_sum(grad_upper_low)
    grad_normed2 = project_back(grad_upper_low, upper_w)
    norm_pull = jax.vjp(layer_norm, middle, gain_two, shift_two)[1]
    grad_ln_two, mlpgain_grad, mlpshift_grad = norm_pull(grad_normed2)
    grad_middle = grad_out + grad_ln_two
    mlpgain_grad, mlpshift_grad, upmat_grad, upbias_grad, downmat_grad, downbias_grad = (
        lax.psum_scatter(mlpgain_grad, ("dp", "fsdp"), scatter_dimension=0, tiled=True),
        lax.psum_scatter(mlpshift_grad, ("dp", "fsdp"), scatter_dimension=0, tiled=True),
        lax.psum_scatter(upmat_grad, ("dp", "fsdp"), scatter_dimension=1, tiled=True),
        lax.psum_scatter(upbias_grad, ("dp", "fsdp"), scatter_dimension=0, tiled=True),
        lax.psum_scatter(downmat_grad, ("dp", "fsdp"), scatter_dimension=1, tiled=True),
        lax.psum_scatter(downbias_grad, ("dp", "fsdp"), scatter_dimension=0, tiled=True),
    )
    grad_branch_low = grad_middle.astype(jnp.bfloat16)
    mixmat_grad = outer_sum(mixed_low, grad_branch_low)
    mixbias_grad = token_sum(grad_branch_low)
    grad_mixed_low = (
        project_back(grad_branch_low, mixer_w)
        .astype(jnp.bfloat16)
        .reshape(captions, length, HEADS, head_size)
    )
    scores_again = masked_scores(query_heads, keys_heads, keymask, factor)
    probs = jnp.exp(scores_again - logsum)
    probs_again = probs.astype(jnp.bfloat16)
    grad_values_low = jnp.einsum(
        "chlm,clhd->cmhd", probs_again, grad_mixed_low, preferred_element_type=jnp.float32
    ).astype(jnp.bfloat16)
    grad_probs = jnp.einsum(
        "clhd,cmhd->chlm", grad_mixed_low, values_heads, preferred_element_type=jnp.float32
    )
    weighted = jnp.sum(probs * grad_probs, axis=-1, keepdims=True)
    grad_scores_low = (probs * (grad_probs - weighted)).astype(jnp.bfloat16)
    grad_query_low = (
        jnp.einsum(
            "chlm,cmhd->clhd", grad_scores_low, keys_heads, preferred_element_type=jnp.float32
        )
        * factor
    ).astype(jnp.bfloat16)
    grad_keys_low = (
        jnp.einsum(
            "chlm,clhd->cmhd", grad_scores_low, query_heads, preferred_element_type=jnp.float32
        )
        * factor
    ).astype(jnp.bfloat16)
    grad_query_low = grad_query_low.reshape(captions, length, width)
    grad_keys_low = grad_keys_low.reshape(captions, length, width)
    grad_values_low = grad_values_low.reshape(captions, length, width)
    querymat_grad = outer_sum(normed_low, grad_query_low)
    querybias_grad = token_sum(grad_query_low)
    keymat_grad = outer_sum(normed_low, grad_keys_low)
    valuemat_grad = outer_sum(normed_low, grad_values_low)
    valuebias_grad = token_sum(grad_values_low)
    grad_normed = (
        project_back(grad_query_low, query_w)
        + project_back(grad_keys_low, keys_w)
        + project_back(grad_values_low, values_w)
    )
    first_pull = jax.vjp(layer_norm, source, gain_one, shift_one)[1]
    grad_ln_one, attgain_grad, attshift_grad = first_pull(grad_normed)
    input_grad = grad_middle + grad_ln_one
    (
        attgain_grad,
        attshift_grad,
        querymat_grad,
        querybias_grad,
        keymat_grad,
        valuemat_grad,
        valuebias_grad,
        mixmat_grad,
        mixbias_grad,
    ) = (
        lax.psum_scatter(attgain_grad, ("dp", "fsdp"), scatter_dimension=0, tiled=True),
        lax.psum_scatter(attshift_grad, ("dp", "fsdp"), scatter_dimension=0, tiled=True),
        lax.psum_scatter(querymat_grad, ("dp", "fsdp"), scatter_dimension=1, tiled=True),
        lax.psum_scatter(querybias_grad, ("dp", "fsdp"), scatter_dimension=0, tiled=True),
        lax.psum_scatter(keymat_grad, ("dp", "fsdp"), scatter_dimension=1, tiled=True),
        lax.psum_scatter(valuemat_grad, ("dp", "fsdp"), scatter_dimension=1, tiled=True),
        lax.psum_scatter(valuebias_grad, ("dp", "fsdp"), scatter_dimension=0, tiled=True),
        lax.psum_scatter(mixmat_grad, ("dp", "fsdp"), scatter_dimension=1, tiled=True),
        lax.psum_scatter(mixbias_grad, ("dp", "fsdp"), scatter_dimension=0, tiled=True),
    )
    return (
        block_out,
        input_grad,
        attgain_grad,
        attshift_grad,
        querymat_grad,
        querybias_grad,
        keymat_grad,
        valuemat_grad,
        valuebias_grad,
        mixmat_grad,
        mixbias_grad,
        mlpgain_grad,
        mlpshift_grad,
        upmat_grad,
        upbias_grad,
        downmat_grad,
        downbias_grad,
    )


NT = (((1,), (1,)), ((), ()))
NN = (((1,), (0,)), ((), ()))
TN = (((0,), (0,)), ((), ()))
F32 = jnp.float32
BF16 = jnp.bfloat16
AXES = ("z", "x", "y", "c")
QUAD = 4
VMEM_LIMIT = 56 * 1024 * 1024


def dot(left, right, dims):
    return lax.dot_general(left, right, dims, preferred_element_type=F32)


class Grid3:
    def __init__(self, dp, fsdp):
        self.c = 2
        self.y = fsdp // 2
        self.x = self.y
        self.z = dp // self.x
        self.count = dp * fsdp

    def index(self, z, x, y, c):
        return ((z * self.x + x) * self.y + y) * self.c + c

    def shift(self, values, kz=0, kx=0, ky=0, kc=0):
        pairs = []
        for z in range(self.z):
            for x in range(self.x):
                for y in range(self.y):
                    for c in range(self.c):
                        pairs.append((self.index(z, x, y, c), self.index(z ^ kz, x ^ kx, y ^ ky, c ^ kc)))
        return lax.ppermute(values, AXES, pairs)

    def here(self):
        return tuple(lax.axis_index(name) for name in AXES)

    def me(self):
        return self.index(*self.here())

    def away(self, *bits):
        return self.index(*(lax.bitwise_xor(at, jnp.int32(bit)) for at, bit in zip(self.here(), bits)))


def tie(values, gate):
    return lax.optimization_barrier((values, gate))[0]


def together(values):
    return lax.optimization_barrier(values)


COLUMN = (0, 3, 1, 2)


def gather_one(grid, first, second):
    return first, second, grid.shift(first, kx=1), grid.shift(second, ky=1)


def gather_two(grid, four):
    first, second, first_x, second_y = four
    one = jnp.concatenate([first, first_x])
    two = jnp.concatenate([second, second_y])
    return one, two, grid.shift(one, ky=1), grid.shift(two, kx=1)


def gather_core(grid, arrays):
    return tuple(grid.shift(array, kc=1) for array in arrays)


def gather_places():
    first, second = COLUMN[:2], COLUMN[2:]
    one = [(z, x, 0) for x in range(2) for z in first]
    two = [(z, 0, y) for y in range(2) for z in second]
    one_y = [(z, x, 1) for z, x, _ in one]
    two_x = [(z, 1, y) for z, _, y in two]
    return [[spot + (core,) for spot in group] for core, pair in ((0, 0), (0, 1), (1, 0), (1, 1)) for group in ((one, two), (one_y, two_x))[pair]]


def place(grid, places, refs, held):
    for ref, spots in zip(refs, places):
        for slot, spot in enumerate(spots):
            held[grid.away(*spot)] = ref[slot]


def outgoing(grid, core):
    half = grid.z // 2
    slots = []
    for which in range(2):
        for one in range(2):
            for two in range(2):
                for low in range(half):
                    kx, ky = (one, two) if which == 0 else (two, one)
                    slots.append((COLUMN[which * half + low], kx, ky, core))
    return slots


def plus(left, right):
    return (left.astype(F32) + right.astype(F32)).astype(BF16)


def scatter_core(grid, other):
    return grid.shift(other, kc=1)


def join(values, extra):
    values = values.reshape(-1, 8, values.shape[-1])
    return values if extra is None else jnp.concatenate([values, extra])


def part(values, shape):
    count = math.prod(shape[:-1]) // 8
    return values[:count].reshape(shape), values[count:]


def scatter_first(grid, own, arrived, extra=None):
    shape = (2, 2, 2, grid.z // 2) + own.shape[1:]
    own = own.reshape(shape)
    arrived = arrived.reshape(shape)
    send_a = plus(own[0, 1], arrived[0, 1])
    send_b = plus(own[1, 1], arrived[1, 1])
    keep_a = plus(own[0, 0], arrived[0, 0])
    keep_b = plus(own[1, 0], arrived[1, 0])
    if extra is not None:
        send_a = join(send_a, extra.astype(BF16))
    return keep_a, keep_b, grid.shift(send_a, kx=1), grid.shift(send_b, ky=1), extra


def scatter_second(grid, state, gate):
    keep_a, keep_b, got_a, got_b, extra = state
    got_a, got_b = tie((got_a, got_b), gate)
    if extra is not None:
        got_a, more = part(got_a, keep_a.shape)
        extra = extra + more.astype(F32)
    next_a = plus(keep_a[1], got_a[1])
    next_b = plus(keep_b[1], got_b[1])
    rest_a = plus(keep_a[0], got_a[0])
    rest_b = plus(keep_b[0], got_b[0])
    if extra is not None:
        next_a = join(next_a, extra.astype(BF16))
    return rest_a, rest_b, grid.shift(next_a, ky=1), grid.shift(next_b, kx=1), extra


def scatter_third(grid, state, gate):
    rest_a, rest_b, last_a, last_b, extra = state
    last_a, last_b = tie((last_a, last_b), gate)
    if extra is not None:
        last_a, more = part(last_a, rest_a.shape)
        extra = extra + more.astype(F32)
    half = grid.z // 2
    parts = [plus(rest_a[k], last_a[k]) for k in range(half)] + [plus(rest_b[k], last_b[k]) for k in range(half)]
    sends = parts[1:]
    if extra is not None:
        sends = [join(send, extra.astype(BF16)) for send in sends]
    return parts[0], [grid.shift(send, kz=k) for send, k in zip(sends, COLUMN[1:])], extra


def scatter_last(state, gate):
    total, came, extra = state
    shape = total.shape
    came = tie(came, gate)
    total = total.astype(F32)
    for values in came:
        if extra is not None:
            values, more = part(values, shape)
            extra = extra + more.astype(F32)
        total = total + values.astype(F32)
    return total if extra is None else (total, extra)


def lanes_of(rows):
    return lax.broadcasted_iota(jnp.int32, (rows, 256), 1) // 64


def spread(block):
    head = lanes_of(block.shape[0])
    zero = jnp.zeros_like(block)
    return jnp.concatenate([jnp.where(head == g, block, zero) for g in range(QUAD)], axis=0)


def collect(square):
    head = lanes_of(64)
    total = jnp.where(head == 0, square[0:64], 0.0)
    for g in range(1, QUAD):
        total = jnp.where(head == g, square[64 * g : 64 * g + 64], total)
    return total


def normal(values):
    centre = jnp.mean(values, axis=-1, keepdims=True)
    centred = values - centre
    spread_of = jnp.mean(centred * centred, axis=-1, keepdims=True)
    scale = lax.rsqrt(spread_of + 1e-06)
    return centred * scale, scale


def normal_back(hat, scale, gain, grads):
    weighted = grads * gain
    middle = jnp.mean(weighted, axis=-1, keepdims=True)
    along = jnp.mean(weighted * hat, axis=-1, keepdims=True)
    return scale * (weighted - middle - hat * along)


TILE = 16
SIZES = (384, 512, 640, 768, 896, 1024)


def order_of(lengths, length):
    captions = lengths.shape[0]
    tiles = length // TILE
    real = (lengths + (TILE - 1)) // TILE
    before = jnp.tril(jnp.ones((captions, captions), jnp.int32), -1)
    start = jnp.sum(before * real[None, :], axis=1)
    total = jnp.sum(real)
    late = total + jnp.sum(before * (tiles - real)[None, :], axis=1)
    at = jnp.arange(tiles, dtype=jnp.int32)[None, :]
    spots = jnp.where(at < real[:, None], start[:, None] + at, late[:, None] + at - real[:, None])
    sizes = jnp.array(SIZES, jnp.int32)
    size = jnp.min(jnp.where(sizes >= total * TILE, sizes, SIZES[-1]))
    return jnp.concatenate([spots.reshape(-1), start, jnp.stack([size, total])]).astype(jnp.int32)


def tile_rows(place_ref, index):
    return pl.ds(pl.multiple_of(place_ref[index] * TILE, TILE), TILE)


def by_size(size, body):
    for rows in SIZES:
        pl.when(size == rows)(functools.partial(body, rows))


def rows_at(step, rows):
    return pl.ds(pl.multiple_of(step * rows, rows), rows)


def pack_kernel(grid, small_ref, up_ref, q_ref, k_ref, v_ref, out_ref, wide):
    wide[...] = jnp.zeros_like(wide)
    wide[0:8, 0:24] = small_ref[...]
    wide[8:9, 0:96] = up_ref[...]
    me = grid.me()
    eight = pltpu.roll(wide[0:8, :], me * 24, 1)
    four = pltpu.roll(wide[8:16, :], lax.rem(me, 8) * 96, 1)
    row = lax.broadcasted_iota(jnp.int32, (8, 768), 0)
    four = jnp.where(row == lax.div(me, 8), jnp.broadcast_to(four[0:1], (8, 768)), 0.0)
    zero = jnp.zeros((8, 768), F32)
    out_ref[0] = jnp.concatenate([eight, four, zero], axis=0).astype(BF16)
    out_ref[1] = q_ref[...]
    out_ref[2] = k_ref[...]
    out_ref[3] = v_ref[...]


def project_kernel(grid, places, place_ref, hidden_ref, *rest):
    count = len(places)
    refs, rest = rest[:count], rest[count:]
    moved_ref, normed_out, q_ref, k_ref, v_ref, vec_ref, held = rest
    total = jnp.zeros(vec_ref.shape, F32)
    for ref, spots in zip(refs, places):
        for slot, spot in enumerate(spots):
            total = total + ref[slot, 0].astype(F32)
            held[grid.away(*spot)] = ref[slot, 1:4]
    vec_ref[...] = total
    width = hidden_ref.shape[1]
    rows = 256

    def block(step, carry):
        at = rows_at(step, rows)
        hidden = hidden_ref[at, :]
        hat, _ = normal(hidden.astype(F32))
        normed = (hat * vec_ref[0:1, :] + vec_ref[1:2, :]).astype(BF16)
        q_ref[at, :] = (dot(normed, held[:, 0].reshape(width, width), NT) + vec_ref[2:3, :]).astype(BF16)
        k_ref[at, :] = dot(normed, held[:, 1].reshape(width, width), NT).astype(BF16)
        v_ref[at, :] = (dot(normed, held[:, 2].reshape(width, width), NT) + vec_ref[3:4, :]).astype(BF16)
        for t in range(rows // TILE):
            to = tile_rows(place_ref, step * (rows // TILE) + t)
            part = slice(t * TILE, (t + 1) * TILE)
            normed_out[to, :] = normed[part, :]
            moved_ref[to, :] = hidden[part, :]
        return carry

    lax.fori_loop(0, hidden_ref.shape[0] // rows, block, 0)


def attend_kernel(length, group, lengths_ref, place_ref, q_ref, k_ref, v_ref, probs_ref, mixed_out):
    width = q_ref.shape[1]
    captions = q_ref.shape[0] // length
    tiles = length // TILE
    quads = width // 256
    position = lax.broadcasted_iota(jnp.int32, (length, 256), 0)

    def several(step, carry):
        items = [
            (step * group + g, quad, rows_at(step * group + g, length), slice(256 * quad, 256 * quad + 256))
            for g in range(group)
            for quad in range(quads)
        ]
        scores = [dot(k_ref[rows, lanes], spread(q_ref[rows, lanes]), NT) for _, _, rows, lanes in items]
        probs = []
        for (cap, _, _, _), score in zip(items, scores):
            score = jnp.where(position < lengths_ref[cap], score * 0.125, -1e30)
            raised = jnp.exp(score - jnp.max(score, axis=0, keepdims=True))
            probs.append((raised * (1.0 / jnp.sum(raised, axis=0, keepdims=True))).astype(BF16))
        for (cap, quad, _, _), prob in zip(items, probs):
            probs_ref[cap * quads + quad] = prob
        mixed = [
            collect(dot(prob, v_ref[rows, lanes], TN)).astype(BF16)
            for (_, _, rows, lanes), prob in zip(items, probs)
        ]
        for (cap, _, _, lanes), value in zip(items, mixed):
            for t in range(tiles):
                to = tile_rows(place_ref, cap * tiles + t)
                mixed_out[to, lanes] = value[t * TILE : (t + 1) * TILE, :]
        return carry

    lax.fori_loop(0, captions // group, several, 0)


def upper_kernel(grid, places, moved_ref, mixed_ref, vec_ref, *rest):
    count = len(places)
    refs, rest = rest[:count], rest[count:]
    middle_ref, normed_ref, active_ref, slope_ref, held = rest
    place(grid, places, refs, held)
    width = moved_ref.shape[1]
    per = grid.count // 4
    rows = 256
    root = math.sqrt(2.0 / math.pi)

    def block(step, carry):
        at = rows_at(step, rows)
        middle = (
            moved_ref[at, :].astype(F32)
            + dot(mixed_ref[at, :], held[:, 0].reshape(width, width), NT)
            + vec_ref[4:5, :]
        )
        middle_ref[at, :] = middle
        hat, _ = normal(middle)
        normed = (hat * vec_ref[5:6, :] + vec_ref[6:7, :]).astype(BF16)
        normed_ref[at, :] = normed
        for part in range(4):
            weight = held[per * part : per * part + per, 1:5].reshape(width, width)
            upper = dot(normed, weight, NT) + vec_ref[8 + part : 9 + part, :]
            square = upper * upper
            bend = jnp.tanh(upper * (root + (root * 0.044715) * square))
            half = 0.5 * bend + 0.5
            span = slice(width * part, width * part + width)
            active = upper * half
            active_ref[at, span] = active.astype(BF16)
            slope = half + active * ((1.0 - bend) * (root + (3.0 * root * 0.044715) * square))
            slope_ref[at, span] = slope.astype(BF16)
        return carry

    lax.fori_loop(0, moved_ref.shape[0] // rows, block, 0)


def down_grad_kernel(grid, length, size_at, lengths_ref, place_ref, cot_ref, active_ref, low_ref, vec_ref, own_ref, other_ref, total):
    width = cot_ref.shape[1]
    captions = cot_ref.shape[0] // length
    tiles = length // TILE
    position = lax.broadcasted_iota(jnp.int32, (length, 1), 0)
    vec_ref[...] = jnp.zeros_like(vec_ref)

    def caption(cap, carry):
        part = cot_ref[rows_at(cap, length), :].astype(F32)
        part = jnp.where(position < lengths_ref[cap], part, 0.0)
        vec_ref[0:1, :] += jnp.sum(part, axis=0, keepdims=True)
        part = part.astype(BF16)
        for t in range(tiles):
            low_ref[tile_rows(place_ref, cap * tiles + t), :] = part[t * TILE : (t + 1) * TILE, :]
        return carry

    lax.fori_loop(0, captions, caption, 0)
    share = width // grid.count

    def column(step, carry):
        lanes = rows_at(step, width)

        def product(rows):
            total[...] = dot(low_ref[0:rows, :], active_ref[0:rows, lanes], TN)

        by_size(place_ref[size_at], product)
        for core, out_ref in ((0, own_ref), (1, other_ref)):
            for slot, spot in enumerate(outgoing(grid, core)):
                at = pl.multiple_of(grid.away(*spot) * share, 8)
                out_ref[slot, :, lanes] = total[pl.ds(at, share), :].astype(BF16)
        return carry

    lax.fori_loop(0, active_ref.shape[1] // width, column, 0)


def upper_grad_kernel(grid, places, size_at, place_ref, low_ref, slope_ref, normed_ref, *rest):
    count = len(places)
    refs, rest = rest[:count], rest[count:]
    upper_ref, vec_ref, own_ref, other_ref, held, total = rest
    place(grid, places, refs, held)
    width = low_ref.shape[1]
    per = grid.count // 4
    share = width // per
    half = grid.z // 2
    z, x, y, c = grid.here()
    shape = own_ref.shape[1:]
    mine = jnp.where(c == 0, 0, share)

    def column(step, carry):
        lanes = rows_at(step, width)

        def product(rows):
            grads = dot(low_ref[0:rows, :], held[:, :, lanes].reshape(width, width), NN) * slope_ref[0:rows, lanes].astype(F32)
            vec_ref[rows_at(step, 8), :] = jnp.broadcast_to(jnp.sum(grads, axis=0, keepdims=True), (8, width))
            grads = grads.astype(BF16)
            upper_ref[0:rows, lanes] = grads
            total[...] = dot(grads, normed_ref[0:rows, :], TN)

        by_size(place_ref[size_at], product)
        for k in range(per // 2):
            chip = step * (per // 2) + k
            kz = lax.bitwise_xor(lax.div(chip, grid.x * grid.y), z)
            kx = lax.bitwise_xor(lax.rem(lax.div(chip, grid.y), grid.x), x)
            ky = lax.bitwise_xor(lax.rem(chip, grid.y), y)
            low = lax.div(kz, 2)
            which = lax.bitwise_xor(low, lax.rem(kz, 2))
            one = jnp.where(which == 0, kx, ky)
            two = jnp.where(which == 0, ky, kx)
            slot = ((which * 2 + one) * 2 + two) * half + low
            own_at = pl.multiple_of(2 * share * k + mine, 8)
            other_at = pl.multiple_of(2 * share * k + (share - mine), 8)
            own_ref[slot] = total[pl.ds(own_at, share), :].astype(BF16).reshape(shape)
            other_ref[slot] = total[pl.ds(other_at, share), :].astype(BF16).reshape(shape)
        return carry

    lax.fori_loop(0, upper_ref.shape[1] // width, column, 0)


def middle_grad_kernel(grid, size_at, place_ref, upper_ref, middle_ref, low_ref, vec_in, held, grad_ref, branch_ref, dm_ref, vec_ref):
    width = middle_ref.shape[1]
    per = grid.count // 4
    rows = 128
    vec_ref[...] = jnp.zeros_like(vec_ref)

    def block(step, carry):
        at = rows_at(step, rows)
        grads = dot(upper_ref[at, 0:width], held[0:per, 1:5].reshape(width, width), NN)
        for part in range(1, 4):
            weight = held[per * part : per * part + per, 1:5].reshape(width, width)
            grads = grads + dot(upper_ref[at, width * part : width * part + width], weight, NN)
        hat, scale = normal(middle_ref[at, :])
        grad_middle = low_ref[at, :].astype(F32) + normal_back(hat, scale, vec_in[5:6, :], grads)
        grad_ref[at, :] = grad_middle
        branch = grad_middle.astype(BF16)
        branch_ref[at, :] = branch
        dm_ref[at, :] = dot(branch, held[:, 0].reshape(width, width), NN).astype(BF16)
        vec_ref[0:1, :] += jnp.sum(grads * hat, axis=0, keepdims=True)
        vec_ref[1:2, :] += jnp.sum(grads, axis=0, keepdims=True)
        vec_ref[2:3, :] += jnp.sum(grad_middle, axis=0, keepdims=True)
        return carry

    lax.fori_loop(0, lax.div(place_ref[size_at], rows), block, 0)


def attend_grad_kernel(length, group, lengths_ref, place_ref, dm_ref, q_ref, k_ref, v_ref, probs_ref, grads_ref, vec_ref):
    width = dm_ref.shape[1]
    quads = width // 256
    tiles = length // TILE
    captions = probs_ref.shape[0] // quads
    starts = captions * tiles
    end = place_ref[starts + captions + 1]
    clear = pl.ds(pl.multiple_of(end * TILE, TILE), 256)
    for which in range(3):
        grads_ref[which, clear, :] = jnp.zeros((256, width), BF16)
    vec_ref[...] = jnp.zeros_like(vec_ref)
    row = lax.broadcasted_iota(jnp.int32, (length, 1), 0)

    def several(step, carry):
        items = []
        for g in range(group):
            cap = step * group + g
            packed = pl.ds(pl.multiple_of(place_ref[starts + cap] * TILE, TILE), length)
            plain = pl.ds(pl.multiple_of(cap * length, length), length)
            for quad in range(quads):
                items.append((cap, quad, packed, plain, slice(256 * quad, 256 * quad + 256)))
        probs = [probs_ref[cap * quads + quad] for cap, quad, _, _, _ in items]
        wide = []
        for cap, _, packed, _, lanes in items:
            dm = dm_ref[packed, lanes]
            wide.append(spread(jnp.where(row < lengths_ref[cap], dm, jnp.zeros_like(dm))))
        grad_probs = [dot(v_ref[plain, lanes], w, NT) for (_, _, _, plain, lanes), w in zip(items, wide)]
        grad_values = [dot(p, w, NN) for p, w in zip(probs, wide)]
        grad_scores = []
        for p, grad in zip(probs, grad_probs):
            p = p.astype(F32)
            along = p * grad
            grad_scores.append((along - p * jnp.sum(along, axis=0, keepdims=True)).astype(BF16))
        grad_keys = [
            dot(g, spread(q_ref[plain, lanes]), NN) * 0.125 for (_, _, _, plain, lanes), g in zip(items, grad_scores)
        ]
        grad_query = [
            collect(dot(g, k_ref[plain, lanes], TN)) * 0.125 for (_, _, _, plain, lanes), g in zip(items, grad_scores)
        ]
        for at, (_, _, packed, _, lanes) in enumerate(items):
            grads_ref[0, packed, lanes] = grad_query[at].astype(BF16)
            grads_ref[1, packed, lanes] = grad_keys[at].astype(BF16)
            grads_ref[2, packed, lanes] = grad_values[at].astype(BF16)
        for quad in range(quads):
            lanes = slice(256 * quad, 256 * quad + 256)
            vec_ref[0:1, lanes] += sum(jnp.sum(v, axis=0, keepdims=True) for v in grad_query[quad::quads])
            vec_ref[1:2, lanes] += sum(jnp.sum(v, axis=0, keepdims=True) for v in grad_values[quad::quads])
        return carry

    lax.fori_loop(0, captions // group, several, 0)


def weight_grad_kernel(grid, size_at, place_ref, grads_ref, branch_ref, normed_ref, mixed_ref, own_ref, other_ref, total):
    share = total.shape[0] // grid.count

    def send(at):
        for core, out_ref in ((0, own_ref), (1, other_ref)):
            for slot, spot in enumerate(outgoing(grid, core)):
                start = pl.multiple_of(grid.away(*spot) * share, 8)
                out_ref[slot, at] = total[pl.ds(start, share), :].astype(BF16)

    def matrix(at, carry):
        def product(rows):
            total[...] = dot(grads_ref[at, 0:rows, :], normed_ref[0:rows, :], TN)

        by_size(place_ref[size_at], product)
        send(at)
        return carry

    lax.fori_loop(0, 3, matrix, 0)

    def product(rows):
        total[...] = dot(branch_ref[0:rows, :], mixed_ref[0:rows, :], TN)

    by_size(place_ref[size_at], product)
    send(3)


def input_grad_kernel(grid, size_at, place_ref, moved_ref, grad_ref, grads_ref, vec_in, down_vec, up_vec, mid_vec, att_vec, held, out_ref, vec_ref, found):
    rows = 128
    width = moved_ref.shape[1]
    vec_ref[...] = jnp.zeros_like(vec_ref)
    vec_ref[2:4, :] = att_vec[0:2, :]
    vec_ref[4:5, :] = mid_vec[2:3, :]
    vec_ref[5:7, :] = mid_vec[0:2, :]
    vec_ref[7:8, :] = down_vec[0:1, :]
    for part in range(4):
        vec_ref[8 + part : 9 + part, :] = up_vec[8 * part : 8 * part + 1, :]

    def block(step, carry):
        at = rows_at(step, rows)
        grads = dot(grads_ref[0, at, :], held[:, 0].reshape(width, width), NN)
        grads = grads + dot(grads_ref[1, at, :], held[:, 1].reshape(width, width), NN)
        grads = grads + dot(grads_ref[2, at, :], held[:, 2].reshape(width, width), NN)
        hat, scale = normal(moved_ref[at, :].astype(F32))
        found[at, :] = grad_ref[at, :] + normal_back(hat, scale, vec_in[0:1, :], grads)
        vec_ref[0:1, :] += jnp.sum(grads * hat, axis=0, keepdims=True)
        vec_ref[1:2, :] += jnp.sum(grads, axis=0, keepdims=True)
        return carry

    lax.fori_loop(0, lax.div(place_ref[size_at], rows), block, 0)
    total = place_ref[size_at + 1]

    def tile(index, carry):
        values = found[tile_rows(place_ref, index), :]
        out_ref[rows_at(index, TILE), :] = jnp.where(place_ref[index] < total, values, 0.0)
        return carry

    lax.fori_loop(0, out_ref.shape[0] // TILE, tile, 0)


def lower_kernel(place_ref, active_ref, middle_ref, vec_in, weight_ref, out_ref, found):
    step = pl.program_id(0)
    rows = middle_ref.shape[0]
    weight = weight_ref[...].reshape(middle_ref.shape[1], active_ref.shape[1])
    out = middle_ref[...] + dot(active_ref[...], weight, NT) + vec_in[7:8, :]
    found[rows_at(step, rows), :] = out.astype(BF16)

    @pl.when(step == pl.num_programs(0) - 1)
    def _():
        for index in range(out_ref.shape[0] // TILE):
            out_ref[index * TILE : (index + 1) * TILE, :] = found[tile_rows(place_ref, index), :]


def unpack_kernel(grid, vec_ref, *outs):
    me = grid.me()
    eight = pltpu.roll(vec_ref[0:8, :], lax.rem(768 - me * 24, 768), 1)
    for k in range(8):
        outs[k][...] = eight[k : k + 1, 0:24]
    row = lax.broadcasted_iota(jnp.int32, (8, 768), 0)
    four = jnp.sum(jnp.where(row == lax.div(me, 8), vec_ref[8:16, :], 0.0), axis=0, keepdims=True)
    four = jnp.broadcast_to(four, (8, 768))
    four = pltpu.roll(four, lax.rem(768 - lax.rem(me, 8) * 96, 768), 1)
    outs[8][...] = four[0:1, 0:96]


def whole(shape):
    return pl.BlockSpec(shape, lambda *_: (0,) * len(shape))


ANY = pl.BlockSpec(memory_space=pl.ANY)
SMEM = pl.BlockSpec(memory_space=pltpu.SMEM)


FAST = pl.BlockSpec(memory_space=pltpu.VMEM)


def call(kernel, steps, in_specs, out_specs, outs, scratch, flops, moved, name, limit=8):
    return pl.pallas_call(
        kernel,
        grid=(steps,),
        in_specs=in_specs,
        out_specs=out_specs,
        out_shape=[jax.ShapeDtypeStruct(s, d) for s, d in outs],
        scratch_shapes=scratch,
        compiler_params=pltpu.CompilerParams(vmem_limit_bytes=limit * 1024 * 1024),
        cost_estimate=pl.CostEstimate(flops=flops, bytes_accessed=moved, transcendentals=0),
        name=name,
    )


def call_near(kernel, in_specs, outs, scratch, flops, name, limit=8, aliases=None):
    return pl.pallas_call(
        kernel,
        in_specs=in_specs,
        out_specs=[FAST] * len(outs),
        input_output_aliases=aliases or {},
        out_shape=[jax.ShapeDtypeStruct(s, d) for s, d in outs],
        scratch_shapes=scratch,
        compiler_params=pltpu.CompilerParams(vmem_limit_bytes=limit * 1024 * 1024),
        cost_estimate=pl.CostEstimate(flops=flops, bytes_accessed=1_000_000, transcendentals=0),
        name=name,
    )


def fast_device(
    grid,
    hidden,
    lengths,
    cotangent,
    attgain,
    attshift,
    querymat,
    querybias,
    keymat,
    valuemat,
    valuebias,
    mixmat,
    mixbias,
    mlpgain,
    mlpshift,
    upmat_w,
    upbias,
    downmat,
    downbias,
):
    captions, length, width = hidden.shape
    tokens = captions * length
    hidden2 = hidden.reshape(tokens, width)
    cot2 = cotangent.reshape(tokens, width)
    share = width // grid.count
    ff = downmat.shape[0]
    small = jnp.stack(
        [attgain, attshift, querybias, valuebias, mixbias, mlpgain, mlpshift, downbias]
    ).astype(F32)
    upsmall = upbias.astype(F32).reshape(1, -1)
    first = call(
        functools.partial(pack_kernel, grid),
        1,
        [whole((8, share)), whole((1, 96))] + [whole((share, width))] * 3,
        [whole((4, share, width))],
        [((4, share, width), BF16)],
        [pltpu.VMEM((16, width), F32)],
        1000,
        1000,
        "pack",
    )(small, upsmall, querymat.T, keymat.T, valuemat.T)[0]
    second = jnp.concatenate([mixmat.T[None], upmat_w.T.reshape(4, share, width)], axis=0)
    third = downmat.T
    where = order_of(lengths, length)
    size_at = captions * (length // TILE) + captions
    places = gather_places()
    first_a = jnp.stack([first, grid.shift(first, kz=3)])
    first_a, second = together((first_a, second))
    first_z = grid.shift(first_a, kz=1)
    second_a = jnp.stack([second, grid.shift(second, kz=3)])
    first_a, first_z, second_a = together((first_a, first_z, second_a))
    first_a = gather_one(grid, first_a, first_z)
    second_z = grid.shift(second_a, kz=1)
    first_a, second_z, third = together((first_a, second_z, third))
    first_b = gather_two(grid, first_a)
    first_c = gather_core(grid, first_b[:2])
    third_a = jnp.stack([third, grid.shift(third, kz=3)])
    first_b, first_c, third_a = together((first_b, first_c, third_a))
    first_in = first_b + first_c + gather_core(grid, first_b[2:])
    second_a = gather_one(grid, second_a, tie(second_z, first_b))
    third_z = grid.shift(third_a, kz=1)
    half = grid.count // 2
    unit = 2 * tokens * width * width
    row = (tokens, width)
    heads = captions * (width // 256)
    tall = (tokens + 64, width)
    square = pltpu.VMEM((width, width), F32)
    moved, normed, query, keys, values, vec, held_one = call_near(
        functools.partial(project_kernel, grid, places),
        [SMEM] + [FAST] * (1 + len(first_in)),
        [(row, BF16)] * 5 + [((share, width), F32), ((grid.count, 3, share, width), BF16)],
        [],
        5 * unit,
        "project",
    )(where, hidden2, *first_in)
    second_a, third_z, query = together((second_a, third_z, query))
    second_b = gather_two(grid, second_a)
    second_c = gather_core(grid, second_b[:2])
    probs, mixed = call_near(
        functools.partial(attend_kernel, length, 4),
        [SMEM] * 2 + [FAST] * 3,
        [((heads, length, 256), BF16), (row, BF16)],
        [],
        5 * unit,
        "attend",
    )(lengths, where, query, keys, values)
    second_b, second_c, third_z, mixed = together((second_b, second_c, third_z, mixed))
    second_in = second_b + second_c + gather_core(grid, second_b[2:])
    third_a = gather_one(grid, third_a, third_z)
    middle, normed2, active, slope, held_two = call_near(
        functools.partial(upper_kernel, grid, places),
        [FAST] * (3 + len(second_in)),
        [(row, F32), (row, BF16), ((tokens, ff), BF16), ((tokens, ff), BF16), ((grid.count,) + second.shape, BF16)],
        [],
        9 * unit,
        "upper",
    )(moved, mixed, vec, *second_in)
    third_a, active = together((third_a, active))
    third_b = gather_two(grid, third_a)
    third_c = gather_core(grid, third_b[:2])
    low, down_vec, down_own, down_other = call_near(
        functools.partial(down_grad_kernel, grid, length, size_at),
        [SMEM] * 2 + [FAST] * 2,
        [(row, BF16), ((8, width), F32)] + [((half, share, ff), BF16)] * 2,
        [square],
        5 * unit,
        "down_grad",
    )(lengths, where, cot2, active)
    third_b, third_c, down_own = together((third_b, third_c, down_own))
    third_in = third_b + third_c + gather_core(grid, third_b[2:])
    down_two = scatter_first(grid, down_own, scatter_core(grid, down_other))
    low = tie(low, down_two[0])
    grad_upper, up_vec, up_own, up_other, lower_w = call_near(
        functools.partial(upper_grad_kernel, grid, places, size_at),
        [SMEM] + [FAST] * (3 + len(third_in)),
        [((tokens, ff), BF16), ((32, width), F32)]
        + [((half, 4, share, width), BF16)] * 2
        + [((grid.count, share, ff), BF16)],
        [square],
        8 * unit,
        "upper_grad",
        aliases={2: 0},
    )(where, low, slope, normed2, *third_in)
    down_three = scatter_second(grid, down_two, up_vec)
    up_one = scatter_core(grid, up_other)
    grad_upper = tie(grad_upper, down_three[0])
    grad_middle, branch, dm, mid_vec = call_near(
        functools.partial(middle_grad_kernel, grid, size_at),
        [SMEM] + [FAST] * 5,
        [(row, F32), (row, BF16), (tall, BF16), ((8, width), F32)],
        [],
        6 * unit,
        "middle_grad",
    )(where, grad_upper, middle, low, vec, held_two)
    down_four = scatter_third(grid, down_three, mid_vec)
    up_two = scatter_first(grid, up_own, tie(up_one, mid_vec))
    dm = tie(dm, (up_two[0], down_four[0]))
    grads, att_vec = call_near(
        functools.partial(attend_grad_kernel, length, 4),
        [SMEM] * 2 + [FAST] * 5,
        [((3, tokens + 256, width), BF16), ((8, width), F32)],
        [],
        7 * unit,
        "attend_grad",
    )(lengths, where, dm, query, keys, values, probs)
    up_three = scatter_second(grid, up_two, att_vec)
    grads = tie(grads, up_three[0])
    att_own, att_other = call_near(
        functools.partial(weight_grad_kernel, grid, size_at),
        [SMEM] + [FAST] * 4,
        [((half, 4, share, width), BF16)] * 2,
        [square],
        5 * unit,
        "weight_grad",
    )(where, grads, branch, normed, mixed)
    att_gate = att_own[0, 0, 0:8, 0:128]
    up_four = scatter_third(grid, up_three, att_gate)
    att_one = scatter_core(grid, att_other)
    grad_middle = tie(grad_middle, up_four[0])
    input_grad, all_vec = call_near(
        functools.partial(input_grad_kernel, grid, size_at),
        [SMEM] + [FAST] * 9,
        [(row, F32), ((16, width), F32)],
        [pltpu.VMEM(row, F32)],
        5 * unit,
        "input_grad",
    )(where, moved, grad_middle, grads, vec, down_vec, up_vec, mid_vec, att_vec, held_one)
    down_sum = scatter_last(down_four, all_vec)
    up_sum = scatter_last(up_four, all_vec)
    all_vec = (all_vec + grid.shift(all_vec, kc=1)).reshape(2, 8, width)
    att_two = scatter_first(grid, att_own, tie(att_one, all_vec), all_vec)
    middle = tie(middle, att_two[0])
    steps = 4
    rows = tokens // steps
    block = pl.BlockSpec((rows, width), lambda i: (i, 0))
    (block_out,) = call(
        lower_kernel,
        steps,
        [SMEM, pl.BlockSpec((rows, ff), lambda i: (i, 0)), block, whole((share, width)), whole((grid.count, share, ff))],
        [whole(row)],
        [(row, BF16)],
        [pltpu.VMEM(row, BF16)],
        4 * unit,
        20_000_000,
        "lower",
        24,
    )(where, active, middle, vec, lower_w)
    out_gate = block_out[0:8, 0:128]
    att_three = scatter_second(grid, att_two, out_gate)
    att_four = scatter_third(grid, att_three, out_gate)
    att_sum, all_vec = scatter_last(att_four, out_gate)
    all_vec = all_vec.reshape(16, width)
    vecs = call(
        functools.partial(unpack_kernel, grid),
        1,
        [whole((16, width))],
        [whole((1, share))] * 8 + [whole((1, ff // grid.count))],
        [((1, share), F32)] * 8 + [((1, ff // grid.count), F32)],
        [],
        1000,
        1000,
        "unpack",
    )(all_vec)
    vecs = [v.reshape(-1) for v in vecs]
    return (
        block_out.reshape(hidden.shape),
        input_grad.reshape(hidden.shape),
        vecs[0],
        vecs[1],
        att_sum[0].T,
        vecs[2],
        att_sum[1].T,
        att_sum[2].T,
        vecs[3],
        att_sum[3].T,
        vecs[4],
        vecs[5],
        vecs[6],
        up_sum.reshape(ff // grid.count, width).T,
        vecs[8],
        down_sum.T,
        vecs[7],
    )


def fits(mesh):
    return mesh.shape["dp"] == 8 and mesh.shape["fsdp"] == 4


def solution(mesh):
    axes = ("dp", "fsdp")
    body = per_device
    if fits(mesh):
        axes = AXES
        grid = Grid3(mesh.shape["dp"], mesh.shape["fsdp"])
        mesh = jax.sharding.Mesh(mesh.devices.reshape(grid.z, grid.x, grid.y, grid.c), AXES)
        body = functools.partial(fast_device, grid)
    placed = (
        P(axes, None, None),
        P(axes),
        P(axes, None, None),
        P(axes),
        P(axes),
        P(None, axes),
        P(axes),
        P(None, axes),
        P(None, axes),
        P(axes),
        P(None, axes),
        P(axes),
        P(axes),
        P(axes),
        P(None, axes),
        P(axes),
        P(None, axes),
        P(axes),
    )
    return jax.shard_map(
        body,
        mesh=mesh,
        in_specs=placed,
        out_specs=(
            P(axes, None, None),
            P(axes, None, None),
            P(axes),
            P(axes),
            P(None, axes),
            P(axes),
            P(None, axes),
            P(None, axes),
            P(axes),
            P(None, axes),
            P(axes),
            P(axes),
            P(axes),
            P(None, axes),
            P(axes),
            P(None, axes),
            P(axes),
        ),
        check_vma=False,
    )
```

```python
import functools
import math

import jax
import jax.numpy as jnp
from jax import lax
from jax.experimental import pallas as pl
from jax.experimental.pallas import tpu as pltpu
from jax.sharding import PartitionSpec as P

HEADS = 12


def layer_norm(values, gain, shift):
    centre = jnp.mean(values, axis=-1, keepdims=True)
    centred = values - centre
    spread = jnp.mean(centred * centred, axis=-1, keepdims=True)
    return centred * lax.rsqrt(spread + 1e-06) * gain + shift


def smooth(values):
    return jax.nn.gelu(values, approximate=True)


def project(inputs, matrix):
    return jnp.einsum("cli,ij->clj", inputs, matrix, preferred_element_type=jnp.float32)


def project_back(grads, matrix):
    return jnp.einsum("clj,ij->cli", grads, matrix, preferred_element_type=jnp.float32)


def outer_sum(inputs, grads):
    return jnp.einsum("cli,clj->ij", inputs, grads, preferred_element_type=jnp.float32)


def token_sum(grads):
    return jnp.sum(grads.astype(jnp.float32), axis=(0, 1))


def masked_scores(query_low, keys_low, keymask, factor):
    raw = (
        jnp.einsum("clhd,cmhd->chlm", query_low, keys_low, preferred_element_type=jnp.float32)
        * factor
    )
    return jnp.where(keymask[:, None, None, :], raw, -1e30)


def per_device(
    hidden,
    lengths,
    cotangent,
    attgain,
    attshift,
    querymat,
    querybias,
    keymat,
    valuemat,
    valuebias,
    mixmat,
    mixbias,
    mlpgain,
    mlpshift,
    upmat_w,
    upbias,
    downmat,
    downbias,
):
    captions, length, width = hidden.shape
    head_size = width // HEADS
    factor = 1.0 / math.sqrt(head_size)
    positions = lax.broadcasted_iota(jnp.int32, (captions, length), 1)
    keymask = positions < lengths[:, None]
    rowmask = keymask.astype(jnp.float32)[..., None]
    gathered = (
        lax.all_gather(attgain, ("dp", "fsdp"), axis=0, tiled=True),
        lax.all_gather(attshift, ("dp", "fsdp"), axis=0, tiled=True),
        lax.all_gather(querymat, ("dp", "fsdp"), axis=1, tiled=True),
        lax.all_gather(querybias, ("dp", "fsdp"), axis=0, tiled=True),
        lax.all_gather(keymat, ("dp", "fsdp"), axis=1, tiled=True),
        lax.all_gather(valuemat, ("dp", "fsdp"), axis=1, tiled=True),
        lax.all_gather(valuebias, ("dp", "fsdp"), axis=0, tiled=True),
        lax.all_gather(mixmat, ("dp", "fsdp"), axis=1, tiled=True),
        lax.all_gather(mixbias, ("dp", "fsdp"), axis=0, tiled=True),
        lax.all_gather(mlpgain, ("dp", "fsdp"), axis=0, tiled=True),
        lax.all_gather(mlpshift, ("dp", "fsdp"), axis=0, tiled=True),
        lax.all_gather(upmat_w, ("dp", "fsdp"), axis=1, tiled=True),
        lax.all_gather(upbias, ("dp", "fsdp"), axis=0, tiled=True),
        lax.all_gather(downmat, ("dp", "fsdp"), axis=1, tiled=True),
        lax.all_gather(downbias, ("dp", "fsdp"), axis=0, tiled=True),
    )
    (
        gain_one,
        shift_one,
        query_w,
        query_b,
        keys_w,
        values_w,
        values_b,
        mixer_w,
        mixer_b,
        gain_two,
        shift_two,
        upper_w,
        upper_b,
        lower_w,
        lower_b,
    ) = gathered
    gain_one = gain_one.astype(jnp.float32)
    shift_one = shift_one.astype(jnp.float32)
    gain_two = gain_two.astype(jnp.float32)
    shift_two = shift_two.astype(jnp.float32)
    source = hidden.astype(jnp.float32)
    normed_low = layer_norm(source, gain_one, shift_one).astype(jnp.bfloat16)
    query_low = (project(normed_low, query_w) + query_b.astype(jnp.float32)).astype(jnp.bfloat16)
    keys_low = project(normed_low, keys_w).astype(jnp.bfloat16)
    values_low = (project(normed_low, values_w) + values_b.astype(jnp.float32)).astype(jnp.bfloat16)
    query_heads = query_low.reshape(captions, length, HEADS, head_size)
    keys_heads = keys_low.reshape(captions, length, HEADS, head_size)
    values_heads = values_low.reshape(captions, length, HEADS, head_size)
    scores = masked_scores(query_heads, keys_heads, keymask, factor)
    peak = jnp.max(scores, axis=-1, keepdims=True)
    logsum = peak + jnp.log(jnp.sum(jnp.exp(scores - peak), axis=-1, keepdims=True))
    probs_low = jnp.exp(scores - logsum).astype(jnp.bfloat16)
    mixed_low = (
        jnp.einsum("chlm,cmhd->clhd", probs_low, values_heads, preferred_element_type=jnp.float32)
        .reshape(captions, length, width)
        .astype(jnp.bfloat16)
    )
    middle = source + project(mixed_low, mixer_w) + mixer_b.astype(jnp.float32)
    normed2_low = layer_norm(middle, gain_two, shift_two).astype(jnp.bfloat16)
    upper = project(normed2_low, upper_w) + upper_b.astype(jnp.float32)
    active_low = smooth(upper).astype(jnp.bfloat16)
    result = middle + project(active_low, lower_w) + lower_b.astype(jnp.float32)
    block_out = result.astype(jnp.bfloat16)
    again = (
        lax.all_gather(attgain, ("dp", "fsdp"), axis=0, tiled=True),
        lax.all_gather(attshift, ("dp", "fsdp"), axis=0, tiled=True),
        lax.all_gather(querymat, ("dp", "fsdp"), axis=1, tiled=True),
        lax.all_gather(querybias, ("dp", "fsdp"), axis=0, tiled=True),
        lax.all_gather(keymat, ("dp", "fsdp"), axis=1, tiled=True),
        lax.all_gather(valuemat, ("dp", "fsdp"), axis=1, tiled=True),
        lax.all_gather(valuebias, ("dp", "fsdp"), axis=0, tiled=True),
        lax.all_gather(mixmat, ("dp", "fsdp"), axis=1, tiled=True),
        lax.all_gather(mixbias, ("dp", "fsdp"), axis=0, tiled=True),
        lax.all_gather(mlpgain, ("dp", "fsdp"), axis=0, tiled=True),
        lax.all_gather(mlpshift, ("dp", "fsdp"), axis=0, tiled=True),
        lax.all_gather(upmat_w, ("dp", "fsdp"), axis=1, tiled=True),
        lax.all_gather(upbias, ("dp", "fsdp"), axis=0, tiled=True),
        lax.all_gather(downmat, ("dp", "fsdp"), axis=1, tiled=True),
        lax.all_gather(downbias, ("dp", "fsdp"), axis=0, tiled=True),
    )
    (
        gain_one,
        shift_one,
        query_w,
        query_b,
        keys_w,
        values_w,
        values_b,
        mixer_w,
        mixer_b,
        gain_two,
        shift_two,
        upper_w,
        upper_b,
        lower_w,
        lower_b,
    ) = again
    gain_one = gain_one.astype(jnp.float32)
    shift_one = shift_one.astype(jnp.float32)
    gain_two = gain_two.astype(jnp.float32)
    shift_two = shift_two.astype(jnp.float32)
    grad_out = cotangent.astype(jnp.float32) * rowmask
    grad_low = grad_out.astype(jnp.bfloat16)
    downmat_grad = outer_sum(active_low, grad_low)
    downbias_grad = token_sum(grad_low)
    grad_active = project_back(grad_low, lower_w)
    gelu_pull = jax.vjp(smooth, upper)[1]
    grad_upper_low = gelu_pull(grad_active)[0].astype(jnp.bfloat16)
    upmat_grad = outer_sum(normed2_low, grad_upper_low)
    upbias_grad = token_sum(grad_upper_low)
    grad_normed2 = project_back(grad_upper_low, upper_w)
    norm_pull = jax.vjp(layer_norm, middle, gain_two, shift_two)[1]
    grad_ln_two, mlpgain_grad, mlpshift_grad = norm_pull(grad_normed2)
    grad_middle = grad_out + grad_ln_two
    mlpgain_grad, mlpshift_grad, upmat_grad, upbias_grad, downmat_grad, downbias_grad = (
        lax.psum_scatter(mlpgain_grad, ("dp", "fsdp"), scatter_dimension=0, tiled=True),
        lax.psum_scatter(mlpshift_grad, ("dp", "fsdp"), scatter_dimension=0, tiled=True),
        lax.psum_scatter(upmat_grad, ("dp", "fsdp"), scatter_dimension=1, tiled=True),
        lax.psum_scatter(upbias_grad, ("dp", "fsdp"), scatter_dimension=0, tiled=True),
        lax.psum_scatter(downmat_grad, ("dp", "fsdp"), scatter_dimension=1, tiled=True),
        lax.psum_scatter(downbias_grad, ("dp", "fsdp"), scatter_dimension=0, tiled=True),
    )
    grad_branch_low = grad_middle.astype(jnp.bfloat16)
    mixmat_grad = outer_sum(mixed_low, grad_branch_low)
    mixbias_grad = token_sum(grad_branch_low)
    grad_mixed_low = (
        project_back(grad_branch_low, mixer_w)
        .astype(jnp.bfloat16)
        .reshape(captions, length, HEADS, head_size)
    )
    scores_again = masked_scores(query_heads, keys_heads, keymask, factor)
    probs = jnp.exp(scores_again - logsum)
    probs_again = probs.astype(jnp.bfloat16)
    grad_values_low = jnp.einsum(
        "chlm,clhd->cmhd", probs_again, grad_mixed_low, preferred_element_type=jnp.float32
    ).astype(jnp.bfloat16)
    grad_probs = jnp.einsum(
        "clhd,cmhd->chlm", grad_mixed_low, values_heads, preferred_element_type=jnp.float32
    )
    weighted = jnp.sum(probs * grad_probs, axis=-1, keepdims=True)
    grad_scores_low = (probs * (grad_probs - weighted)).astype(jnp.bfloat16)
    grad_query_low = (
        jnp.einsum(
            "chlm,cmhd->clhd", grad_scores_low, keys_heads, preferred_element_type=jnp.float32
        )
        * factor
    ).astype(jnp.bfloat16)
    grad_keys_low = (
        jnp.einsum(
            "chlm,clhd->cmhd", grad_scores_low, query_heads, preferred_element_type=jnp.float32
        )
        * factor
    ).astype(jnp.bfloat16)
    grad_query_low = grad_query_low.reshape(captions, length, width)
    grad_keys_low = grad_keys_low.reshape(captions, length, width)
    grad_values_low = grad_values_low.reshape(captions, length, width)
    querymat_grad = outer_sum(normed_low, grad_query_low)
    querybias_grad = token_sum(grad_query_low)
    keymat_grad = outer_sum(normed_low, grad_keys_low)
    valuemat_grad = outer_sum(normed_low, grad_values_low)
    valuebias_grad = token_sum(grad_values_low)
    grad_normed = (
        project_back(grad_query_low, query_w)
        + project_back(grad_keys_low, keys_w)
        + project_back(grad_values_low, values_w)
    )
    first_pull = jax.vjp(layer_norm, source, gain_one, shift_one)[1]
    grad_ln_one, attgain_grad, attshift_grad = first_pull(grad_normed)
    input_grad = grad_middle + grad_ln_one
    (
        attgain_grad,
        attshift_grad,
        querymat_grad,
        querybias_grad,
        keymat_grad,
        valuemat_grad,
        valuebias_grad,
        mixmat_grad,
        mixbias_grad,
    ) = (
        lax.psum_scatter(attgain_grad, ("dp", "fsdp"), scatter_dimension=0, tiled=True),
        lax.psum_scatter(attshift_grad, ("dp", "fsdp"), scatter_dimension=0, tiled=True),
        lax.psum_scatter(querymat_grad, ("dp", "fsdp"), scatter_dimension=1, tiled=True),
        lax.psum_scatter(querybias_grad, ("dp", "fsdp"), scatter_dimension=0, tiled=True),
        lax.psum_scatter(keymat_grad, ("dp", "fsdp"), scatter_dimension=1, tiled=True),
        lax.psum_scatter(valuemat_grad, ("dp", "fsdp"), scatter_dimension=1, tiled=True),
        lax.psum_scatter(valuebias_grad, ("dp", "fsdp"), scatter_dimension=0, tiled=True),
        lax.psum_scatter(mixmat_grad, ("dp", "fsdp"), scatter_dimension=1, tiled=True),
        lax.psum_scatter(mixbias_grad, ("dp", "fsdp"), scatter_dimension=0, tiled=True),
    )
    return (
        block_out,
        input_grad,
        attgain_grad,
        attshift_grad,
        querymat_grad,
        querybias_grad,
        keymat_grad,
        valuemat_grad,
        valuebias_grad,
        mixmat_grad,
        mixbias_grad,
        mlpgain_grad,
        mlpshift_grad,
        upmat_grad,
        upbias_grad,
        downmat_grad,
        downbias_grad,
    )


NT = (((1,), (1,)), ((), ()))
NN = (((1,), (0,)), ((), ()))
TN = (((0,), (0,)), ((), ()))
F32 = jnp.float32
BF16 = jnp.bfloat16
AXES = ("z", "x", "y", "c")
QUAD = 4
VMEM_LIMIT = 56 * 1024 * 1024


def dot(left, right, dims):
    return lax.dot_general(left, right, dims, preferred_element_type=F32)


class Grid3:
    def __init__(self, dp, fsdp):
        self.c = 2
        self.y = fsdp // 2
        self.x = self.y
        self.z = dp // self.x
        self.count = dp * fsdp

    def index(self, z, x, y, c):
        return ((z * self.x + x) * self.y + y) * self.c + c

    def shift(self, values, kz=0, kx=0, ky=0, kc=0):
        pairs = []
        for z in range(self.z):
            for x in range(self.x):
                for y in range(self.y):
                    for c in range(self.c):
                        pairs.append((self.index(z, x, y, c), self.index(z ^ kz, x ^ kx, y ^ ky, c ^ kc)))
        return lax.ppermute(values, AXES, pairs)

    def here(self):
        return tuple(lax.axis_index(name) for name in AXES)

    def me(self):
        return self.index(*self.here())

    def away(self, *bits):
        return self.index(*(lax.bitwise_xor(at, jnp.int32(bit)) for at, bit in zip(self.here(), bits)))


def tie(values, gate):
    return lax.optimization_barrier((values, gate))[0]


def together(values):
    return lax.optimization_barrier(values)


COLUMN = (0, 3, 1, 2)


def gather_one(grid, first, second):
    return first, second, grid.shift(first, kx=1), grid.shift(second, ky=1)


def gather_two(grid, four):
    first, second, first_x, second_y = four
    one = jnp.concatenate([first, first_x])
    two = jnp.concatenate([second, second_y])
    return one, two, grid.shift(one, ky=1), grid.shift(two, kx=1)


def gather_core(grid, arrays):
    return tuple(grid.shift(array, kc=1) for array in arrays)


def gather_places():
    first, second = COLUMN[:2], COLUMN[2:]
    one = [(z, x, 0) for x in range(2) for z in first]
    two = [(z, 0, y) for y in range(2) for z in second]
    one_y = [(z, x, 1) for z, x, _ in one]
    two_x = [(z, 1, y) for z, _, y in two]
    return [[spot + (core,) for spot in group] for core, pair in ((0, 0), (0, 1), (1, 0), (1, 1)) for group in ((one, two), (one_y, two_x))[pair]]


def place(grid, places, refs, held):
    for ref, spots in zip(refs, places):
        for slot, spot in enumerate(spots):
            held[grid.away(*spot)] = ref[slot]


def outgoing(grid, core):
    half = grid.z // 2
    slots = []
    for which in range(2):
        for one in range(2):
            for two in range(2):
                for low in range(half):
                    kx, ky = (one, two) if which == 0 else (two, one)
                    slots.append((COLUMN[which * half + low], kx, ky, core))
    return slots


def plus(left, right):
    return (left.astype(F32) + right.astype(F32)).astype(BF16)


def scatter_core(grid, other):
    return grid.shift(other, kc=1)


def join(values, extra):
    values = values.reshape(-1, 8, values.shape[-1])
    return values if extra is None else jnp.concatenate([values, extra])


def part(values, shape):
    count = math.prod(shape[:-1]) // 8
    return values[:count].reshape(shape), values[count:]


def scatter_first(grid, own, arrived, extra=None):
    shape = (2, 2, 2, grid.z // 2) + own.shape[1:]
    own = own.reshape(shape)
    arrived = arrived.reshape(shape)
    send_a = plus(own[0, 1], arrived[0, 1])
    send_b = plus(own[1, 1], arrived[1, 1])
    keep_a = plus(own[0, 0], arrived[0, 0])
    keep_b = plus(own[1, 0], arrived[1, 0])
    if extra is not None:
        send_a = join(send_a, extra.astype(BF16))
    return keep_a, keep_b, grid.shift(send_a, kx=1), grid.shift(send_b, ky=1), extra, (send_a, send_b)


def scatter_second(grid, state, gate):
    keep_a, keep_b, got_a, got_b, extra, _ = state
    got_a, got_b = tie((got_a, got_b), gate)
    if extra is not None:
        got_a, more = part(got_a, keep_a.shape)
        extra = extra + more.astype(F32)
    next_a = plus(keep_a[1], got_a[1])
    next_b = plus(keep_b[1], got_b[1])
    rest_a = plus(keep_a[0], got_a[0])
    rest_b = plus(keep_b[0], got_b[0])
    if extra is not None:
        next_a = join(next_a, extra.astype(BF16))
    return rest_a, rest_b, grid.shift(next_a, ky=1), grid.shift(next_b, kx=1), extra, (next_a, next_b)


def scatter_third(grid, state, gate):
    rest_a, rest_b, last_a, last_b, extra, _ = state
    last_a, last_b = tie((last_a, last_b), gate)
    if extra is not None:
        last_a, more = part(last_a, rest_a.shape)
        extra = extra + more.astype(F32)
    half = grid.z // 2
    parts = [plus(rest_a[k], last_a[k]) for k in range(half)] + [plus(rest_b[k], last_b[k]) for k in range(half)]
    sends = parts[1:]
    if extra is not None:
        sends = [join(send, extra.astype(BF16)) for send in sends]
    return parts[0], [grid.shift(send, kz=k) for send, k in zip(sends, COLUMN[1:])], extra, sends


def scatter_last(state, gate):
    total, came, extra, _ = state
    shape = total.shape
    came = tie(came, gate)
    total = total.astype(F32)
    for values in came:
        if extra is not None:
            values, more = part(values, shape)
            extra = extra + more.astype(F32)
        total = total + values.astype(F32)
    return total if extra is None else (total, extra)


def lanes_of(rows):
    return lax.broadcasted_iota(jnp.int32, (rows, 256), 1) // 64


def spread(block):
    head = lanes_of(block.shape[0])
    zero = jnp.zeros_like(block)
    return jnp.concatenate([jnp.where(head == g, block, zero) for g in range(QUAD)], axis=0)


def collect(square):
    head = lanes_of(64)
    total = jnp.where(head == 0, square[0:64], 0.0)
    for g in range(1, QUAD):
        total = jnp.where(head == g, square[64 * g : 64 * g + 64], total)
    return total


def normal(values):
    centre = jnp.mean(values, axis=-1, keepdims=True)
    centred = values - centre
    spread_of = jnp.mean(centred * centred, axis=-1, keepdims=True)
    scale = lax.rsqrt(spread_of + 1e-06)
    return centred * scale, scale


def normal_back(hat, scale, gain, grads):
    weighted = grads * gain
    middle = jnp.mean(weighted, axis=-1, keepdims=True)
    along = jnp.mean(weighted * hat, axis=-1, keepdims=True)
    return scale * (weighted - middle - hat * along)


TILE = 16
SIZES = (384, 512, 640, 768, 896, 1024)


def order_of(lengths, length):
    captions = lengths.shape[0]
    tiles = length // TILE
    real = (lengths + (TILE - 1)) // TILE
    before = jnp.tril(jnp.ones((captions, captions), jnp.int32), -1)
    start = jnp.sum(before * real[None, :], axis=1)
    total = jnp.sum(real)
    late = total + jnp.sum(before * (tiles - real)[None, :], axis=1)
    at = jnp.arange(tiles, dtype=jnp.int32)[None, :]
    spots = jnp.where(at < real[:, None], start[:, None] + at, late[:, None] + at - real[:, None])
    sizes = jnp.array(SIZES, jnp.int32)
    size = jnp.min(jnp.where(sizes >= total * TILE, sizes, SIZES[-1]))
    return jnp.concatenate([spots.reshape(-1), start, jnp.stack([size, total])]).astype(jnp.int32)


def tile_rows(place_ref, index):
    return pl.ds(pl.multiple_of(place_ref[index] * TILE, TILE), TILE)


def by_size(size, body):
    for rows in SIZES:
        pl.when(size == rows)(functools.partial(body, rows))


def rows_at(step, rows):
    return pl.ds(pl.multiple_of(step * rows, rows), rows)


def pack_kernel(grid, small_ref, up_ref, q_ref, k_ref, v_ref, out_ref, wide):
    wide[...] = jnp.zeros_like(wide)
    wide[0:8, 0:24] = small_ref[...]
    wide[8:9, 0:96] = up_ref[...]
    me = grid.me()
    eight = pltpu.roll(wide[0:8, :], me * 24, 1)
    four = pltpu.roll(wide[8:16, :], lax.rem(me, 8) * 96, 1)
    row = lax.broadcasted_iota(jnp.int32, (8, 768), 0)
    four = jnp.where(row == lax.div(me, 8), jnp.broadcast_to(four[0:1], (8, 768)), 0.0)
    zero = jnp.zeros((8, 768), F32)
    out_ref[0] = jnp.concatenate([eight, four, zero], axis=0).astype(BF16)
    out_ref[1] = q_ref[...]
    out_ref[2] = k_ref[...]
    out_ref[3] = v_ref[...]


def project_kernel(grid, places, place_ref, hidden_ref, *rest):
    count = len(places)
    refs, rest = rest[:count], rest[count:]
    moved_ref, normed_out, q_ref, k_ref, v_ref, vec_ref, held = rest
    total = jnp.zeros(vec_ref.shape, F32)
    for ref, spots in zip(refs, places):
        for slot, spot in enumerate(spots):
            total = total + ref[slot, 0].astype(F32)
            held[grid.away(*spot)] = ref[slot, 1:4]
    vec_ref[...] = total
    width = hidden_ref.shape[1]
    rows = 256

    def block(step, carry):
        at = rows_at(step, rows)
        hidden = hidden_ref[at, :]
        hat, _ = normal(hidden.astype(F32))
        normed = (hat * vec_ref[0:1, :] + vec_ref[1:2, :]).astype(BF16)
        q_ref[at, :] = (dot(normed, held[:, 0].reshape(width, width), NT) + vec_ref[2:3, :]).astype(BF16)
        k_ref[at, :] = dot(normed, held[:, 1].reshape(width, width), NT).astype(BF16)
        v_ref[at, :] = (dot(normed, held[:, 2].reshape(width, width), NT) + vec_ref[3:4, :]).astype(BF16)
        for t in range(rows // TILE):
            to = tile_rows(place_ref, step * (rows // TILE) + t)
            part = slice(t * TILE, (t + 1) * TILE)
            normed_out[to, :] = normed[part, :]
            moved_ref[to, :] = hidden[part, :]
        return carry

    lax.fori_loop(0, hidden_ref.shape[0] // rows, block, 0)


def attend_kernel(length, group, lengths_ref, place_ref, q_ref, k_ref, v_ref, probs_ref, mixed_out):
    width = q_ref.shape[1]
    captions = q_ref.shape[0] // length
    tiles = length // TILE
    quads = width // 256
    position = lax.broadcasted_iota(jnp.int32, (length, 256), 0)

    def several(step, carry):
        items = [
            (step * group + g, quad, rows_at(step * group + g, length), slice(256 * quad, 256 * quad + 256))
            for g in range(group)
            for quad in range(quads)
        ]
        scores = [dot(k_ref[rows, lanes], spread(q_ref[rows, lanes]), NT) for _, _, rows, lanes in items]
        probs = []
        for (cap, _, _, _), score in zip(items, scores):
            score = jnp.where(position < lengths_ref[cap], score * 0.125, -1e30)
            raised = jnp.exp(score - jnp.max(score, axis=0, keepdims=True))
            probs.append((raised * (1.0 / jnp.sum(raised, axis=0, keepdims=True))).astype(BF16))
        for (cap, quad, _, _), prob in zip(items, probs):
            probs_ref[cap * quads + quad] = prob
        mixed = [
            collect(dot(prob, v_ref[rows, lanes], TN)).astype(BF16)
            for (_, _, rows, lanes), prob in zip(items, probs)
        ]
        for (cap, _, _, lanes), value in zip(items, mixed):
            for t in range(tiles):
                to = tile_rows(place_ref, cap * tiles + t)
                mixed_out[to, lanes] = value[t * TILE : (t + 1) * TILE, :]
        return carry

    lax.fori_loop(0, captions // group, several, 0)


def upper_kernel(grid, places, moved_ref, mixed_ref, vec_ref, *rest):
    count = len(places)
    refs, rest = rest[:count], rest[count:]
    middle_ref, normed_ref, active_ref, slope_ref, held = rest
    place(grid, places, refs, held)
    width = moved_ref.shape[1]
    per = grid.count // 4
    rows = 256
    root = math.sqrt(2.0 / math.pi)

    def block(step, carry):
        at = rows_at(step, rows)
        middle = (
            moved_ref[at, :].astype(F32)
            + dot(mixed_ref[at, :], held[:, 0].reshape(width, width), NT)
            + vec_ref[4:5, :]
        )
        middle_ref[at, :] = middle
        hat, _ = normal(middle)
        normed = (hat * vec_ref[5:6, :] + vec_ref[6:7, :]).astype(BF16)
        normed_ref[at, :] = normed
        for part in range(4):
            weight = held[per * part : per * part + per, 1:5].reshape(width, width)
            upper = dot(normed, weight, NT) + vec_ref[8 + part : 9 + part, :]
            square = upper * upper
            bend = jnp.tanh(upper * (root + (root * 0.044715) * square))
            half = 0.5 * bend + 0.5
            span = slice(width * part, width * part + width)
            active = upper * half
            active_ref[at, span] = active.astype(BF16)
            slope = half + active * ((1.0 - bend) * (root + (3.0 * root * 0.044715) * square))
            slope_ref[at, span] = slope.astype(BF16)
        return carry

    lax.fori_loop(0, moved_ref.shape[0] // rows, block, 0)


def down_grad_kernel(grid, length, size_at, lengths_ref, place_ref, cot_ref, active_ref, low_ref, vec_ref, own_ref, other_ref, far_ref, total, sem):
    keep = pltpu.make_async_copy(active_ref, far_ref, sem)
    keep.start()
    width = cot_ref.shape[1]
    captions = cot_ref.shape[0] // length
    tiles = length // TILE
    position = lax.broadcasted_iota(jnp.int32, (length, 1), 0)
    vec_ref[...] = jnp.zeros_like(vec_ref)

    def caption(cap, carry):
        part = cot_ref[rows_at(cap, length), :].astype(F32)
        part = jnp.where(position < lengths_ref[cap], part, 0.0)
        vec_ref[0:1, :] += jnp.sum(part, axis=0, keepdims=True)
        part = part.astype(BF16)
        for t in range(tiles):
            low_ref[tile_rows(place_ref, cap * tiles + t), :] = part[t * TILE : (t + 1) * TILE, :]
        return carry

    lax.fori_loop(0, captions, caption, 0)
    share = width // grid.count

    def column(step, carry):
        lanes = rows_at(step, width)

        def product(rows):
            total[...] = dot(low_ref[0:rows, :], active_ref[0:rows, lanes], TN)

        by_size(place_ref[size_at], product)
        for core, out_ref in ((0, own_ref), (1, other_ref)):
            for slot, spot in enumerate(outgoing(grid, core)):
                at = pl.multiple_of(grid.away(*spot) * share, 8)
                out_ref[slot, :, lanes] = total[pl.ds(at, share), :].astype(BF16)
        return carry

    lax.fori_loop(0, active_ref.shape[1] // width, column, 0)
    keep.wait()


def upper_grad_kernel(grid, places, size_at, place_ref, low_ref, slope_ref, normed_ref, *rest):
    count = len(places)
    refs, rest = rest[:count], rest[count:]
    upper_ref, vec_ref, own_ref, other_ref, far_ref, held, total, sem = rest
    place(grid, places, refs, held)
    keep = pltpu.make_async_copy(held, far_ref, sem)
    keep.start()
    width = low_ref.shape[1]
    per = grid.count // 4
    share = width // per
    half = grid.z // 2
    z, x, y, c = grid.here()
    shape = own_ref.shape[1:]
    mine = jnp.where(c == 0, 0, share)

    def column(step, carry):
        lanes = rows_at(step, width)

        def product(rows):
            grads = dot(low_ref[0:rows, :], held[:, :, lanes].reshape(width, width), NN) * slope_ref[0:rows, lanes].astype(F32)
            vec_ref[rows_at(step, 8), :] = jnp.broadcast_to(jnp.sum(grads, axis=0, keepdims=True), (8, width))
            grads = grads.astype(BF16)
            upper_ref[0:rows, lanes] = grads
            total[...] = dot(grads, normed_ref[0:rows, :], TN)

        by_size(place_ref[size_at], product)
        for k in range(per // 2):
            chip = step * (per // 2) + k
            kz = lax.bitwise_xor(lax.div(chip, grid.x * grid.y), z)
            kx = lax.bitwise_xor(lax.rem(lax.div(chip, grid.y), grid.x), x)
            ky = lax.bitwise_xor(lax.rem(chip, grid.y), y)
            low = lax.div(kz, 2)
            which = lax.bitwise_xor(low, lax.rem(kz, 2))
            one = jnp.where(which == 0, kx, ky)
            two = jnp.where(which == 0, ky, kx)
            slot = ((which * 2 + one) * 2 + two) * half + low
            own_at = pl.multiple_of(2 * share * k + mine, 8)
            other_at = pl.multiple_of(2 * share * k + (share - mine), 8)
            own_ref[slot] = total[pl.ds(own_at, share), :].astype(BF16).reshape(shape)
            other_ref[slot] = total[pl.ds(other_at, share), :].astype(BF16).reshape(shape)
        return carry

    lax.fori_loop(0, upper_ref.shape[1] // width, column, 0)
    keep.wait()


def middle_grad_kernel(grid, size_at, place_ref, upper_ref, middle_ref, low_ref, vec_in, held, grad_ref, branch_ref, dm_ref, vec_ref):
    width = middle_ref.shape[1]
    per = grid.count // 4
    rows = 128
    vec_ref[...] = jnp.zeros_like(vec_ref)

    def block(step, carry):
        at = rows_at(step, rows)
        grads = dot(upper_ref[at, 0:width], held[0:per, 1:5].reshape(width, width), NN)
        for part in range(1, 4):
            weight = held[per * part : per * part + per, 1:5].reshape(width, width)
            grads = grads + dot(upper_ref[at, width * part : width * part + width], weight, NN)
        hat, scale = normal(middle_ref[at, :])
        grad_middle = low_ref[at, :].astype(F32) + normal_back(hat, scale, vec_in[5:6, :], grads)
        grad_ref[at, :] = grad_middle
        branch = grad_middle.astype(BF16)
        branch_ref[at, :] = branch
        dm_ref[at, :] = dot(branch, held[:, 0].reshape(width, width), NN).astype(BF16)
        vec_ref[0:1, :] += jnp.sum(grads * hat, axis=0, keepdims=True)
        vec_ref[1:2, :] += jnp.sum(grads, axis=0, keepdims=True)
        vec_ref[2:3, :] += jnp.sum(grad_middle, axis=0, keepdims=True)
        return carry

    lax.fori_loop(0, lax.div(place_ref[size_at], rows), block, 0)


def attend_grad_kernel(length, group, lengths_ref, place_ref, dm_ref, q_ref, k_ref, v_ref, probs_ref, grads_ref, vec_ref):
    width = dm_ref.shape[1]
    quads = width // 256
    tiles = length // TILE
    captions = probs_ref.shape[0] // quads
    starts = captions * tiles
    end = place_ref[starts + captions + 1]
    clear = pl.ds(pl.multiple_of(end * TILE, TILE), 256)
    for which in range(3):
        grads_ref[which, clear, :] = jnp.zeros((256, width), BF16)
    vec_ref[...] = jnp.zeros_like(vec_ref)
    row = lax.broadcasted_iota(jnp.int32, (length, 1), 0)

    def several(step, carry):
        items = []
        for g in range(group):
            cap = step * group + g
            packed = pl.ds(pl.multiple_of(place_ref[starts + cap] * TILE, TILE), length)
            plain = pl.ds(pl.multiple_of(cap * length, length), length)
            for quad in range(quads):
                items.append((cap, quad, packed, plain, slice(256 * quad, 256 * quad + 256)))
        probs = [probs_ref[cap * quads + quad] for cap, quad, _, _, _ in items]
        wide = []
        for cap, _, packed, _, lanes in items:
            dm = dm_ref[packed, lanes]
            wide.append(spread(jnp.where(row < lengths_ref[cap], dm, jnp.zeros_like(dm))))
        grad_probs = [dot(v_ref[plain, lanes], w, NT) for (_, _, _, plain, lanes), w in zip(items, wide)]
        grad_values = [dot(p, w, NN) for p, w in zip(probs, wide)]
        grad_scores = []
        for p, grad in zip(probs, grad_probs):
            p = p.astype(F32)
            along = p * grad
            grad_scores.append((along - p * jnp.sum(along, axis=0, keepdims=True)).astype(BF16))
        grad_keys = [
            dot(g, spread(q_ref[plain, lanes]), NN) * 0.125 for (_, _, _, plain, lanes), g in zip(items, grad_scores)
        ]
        grad_query = [
            collect(dot(g, k_ref[plain, lanes], TN)) * 0.125 for (_, _, _, plain, lanes), g in zip(items, grad_scores)
        ]
        for at, (_, _, packed, _, lanes) in enumerate(items):
            grads_ref[0, packed, lanes] = grad_query[at].astype(BF16)
            grads_ref[1, packed, lanes] = grad_keys[at].astype(BF16)
            grads_ref[2, packed, lanes] = grad_values[at].astype(BF16)
        for quad in range(quads):
            lanes = slice(256 * quad, 256 * quad + 256)
            vec_ref[0:1, lanes] += sum(jnp.sum(v, axis=0, keepdims=True) for v in grad_query[quad::quads])
            vec_ref[1:2, lanes] += sum(jnp.sum(v, axis=0, keepdims=True) for v in grad_values[quad::quads])
        return carry

    lax.fori_loop(0, captions // group, several, 0)


def weight_grad_kernel(grid, size_at, place_ref, grads_ref, branch_ref, normed_ref, mixed_ref, own_ref, other_ref, total):
    share = total.shape[0] // grid.count

    def send(at):
        for core, out_ref in ((0, own_ref), (1, other_ref)):
            for slot, spot in enumerate(outgoing(grid, core)):
                start = pl.multiple_of(grid.away(*spot) * share, 8)
                out_ref[slot, at] = total[pl.ds(start, share), :].astype(BF16)

    def matrix(at, carry):
        def product(rows):
            total[...] = dot(grads_ref[at, 0:rows, :], normed_ref[0:rows, :], TN)

        by_size(place_ref[size_at], product)
        send(at)
        return carry

    lax.fori_loop(0, 3, matrix, 0)

    def product(rows):
        total[...] = dot(branch_ref[0:rows, :], mixed_ref[0:rows, :], TN)

    by_size(place_ref[size_at], product)
    send(3)


def input_grad_kernel(grid, size_at, place_ref, moved_ref, grad_ref, grads_ref, vec_in, down_vec, up_vec, mid_vec, att_vec, held, out_ref, vec_ref, found):
    rows = 128
    width = moved_ref.shape[1]
    vec_ref[...] = jnp.zeros_like(vec_ref)
    vec_ref[2:4, :] = att_vec[0:2, :]
    vec_ref[4:5, :] = mid_vec[2:3, :]
    vec_ref[5:7, :] = mid_vec[0:2, :]
    vec_ref[7:8, :] = down_vec[0:1, :]
    for part in range(4):
        vec_ref[8 + part : 9 + part, :] = up_vec[8 * part : 8 * part + 1, :]

    def block(step, carry):
        at = rows_at(step, rows)
        grads = dot(grads_ref[0, at, :], held[:, 0].reshape(width, width), NN)
        grads = grads + dot(grads_ref[1, at, :], held[:, 1].reshape(width, width), NN)
        grads = grads + dot(grads_ref[2, at, :], held[:, 2].reshape(width, width), NN)
        hat, scale = normal(moved_ref[at, :].astype(F32))
        found[at, :] = grad_ref[at, :] + normal_back(hat, scale, vec_in[0:1, :], grads)
        vec_ref[0:1, :] += jnp.sum(grads * hat, axis=0, keepdims=True)
        vec_ref[1:2, :] += jnp.sum(grads, axis=0, keepdims=True)
        return carry

    lax.fori_loop(0, lax.div(place_ref[size_at], rows), block, 0)
    total = place_ref[size_at + 1]

    def tile(index, carry):
        values = found[tile_rows(place_ref, index), :]
        out_ref[rows_at(index, TILE), :] = jnp.where(place_ref[index] < total, values, 0.0)
        return carry

    lax.fori_loop(0, out_ref.shape[0] // TILE, tile, 0)


def lower_kernel(place_ref, active_ref, middle_ref, vec_in, weight_ref, out_ref, found):
    step = pl.program_id(0)
    rows = middle_ref.shape[0]
    weight = weight_ref[...].reshape(middle_ref.shape[1], active_ref.shape[1])
    out = middle_ref[...] + dot(active_ref[...], weight, NT) + vec_in[7:8, :]
    found[rows_at(step, rows), :] = out.astype(BF16)

    @pl.when(step == pl.num_programs(0) - 1)
    def _():
        for index in range(out_ref.shape[0] // TILE):
            out_ref[index * TILE : (index + 1) * TILE, :] = found[tile_rows(place_ref, index), :]


def unpack_kernel(grid, vec_ref, *outs):
    me = grid.me()
    eight = pltpu.roll(vec_ref[0:8, :], lax.rem(768 - me * 24, 768), 1)
    for k in range(8):
        outs[k][...] = eight[k : k + 1, 0:24]
    row = lax.broadcasted_iota(jnp.int32, (8, 768), 0)
    four = jnp.sum(jnp.where(row == lax.div(me, 8), vec_ref[8:16, :], 0.0), axis=0, keepdims=True)
    four = jnp.broadcast_to(four, (8, 768))
    four = pltpu.roll(four, lax.rem(768 - lax.rem(me, 8) * 96, 768), 1)
    outs[8][...] = four[0:1, 0:96]


def whole(shape):
    return pl.BlockSpec(shape, lambda *_: (0,) * len(shape))


ANY = pl.BlockSpec(memory_space=pl.ANY)
SMEM = pl.BlockSpec(memory_space=pltpu.SMEM)


FAST = pl.BlockSpec(memory_space=pltpu.VMEM)
FAR = pl.BlockSpec(memory_space=pltpu.HBM)


def call(kernel, steps, in_specs, out_specs, outs, scratch, flops, moved, name, limit=8):
    return pl.pallas_call(
        kernel,
        grid=(steps,),
        in_specs=in_specs,
        out_specs=out_specs,
        out_shape=[jax.ShapeDtypeStruct(s, d) for s, d in outs],
        scratch_shapes=scratch,
        compiler_params=pltpu.CompilerParams(vmem_limit_bytes=limit * 1024 * 1024),
        cost_estimate=pl.CostEstimate(flops=flops, bytes_accessed=moved, transcendentals=0),
        name=name,
    )


def call_near(kernel, in_specs, outs, scratch, flops, name, limit=8, aliases=None, far=0):
    return pl.pallas_call(
        kernel,
        in_specs=in_specs,
        out_specs=[FAST] * (len(outs) - far) + [FAR] * far,
        input_output_aliases=aliases or {},
        out_shape=[jax.ShapeDtypeStruct(s, d) for s, d in outs],
        scratch_shapes=scratch,
        compiler_params=pltpu.CompilerParams(vmem_limit_bytes=limit * 1024 * 1024),
        cost_estimate=pl.CostEstimate(flops=flops, bytes_accessed=1_000_000, transcendentals=0),
        name=name,
    )


def fast_device(
    grid,
    hidden,
    lengths,
    cotangent,
    attgain,
    attshift,
    querymat,
    querybias,
    keymat,
    valuemat,
    valuebias,
    mixmat,
    mixbias,
    mlpgain,
    mlpshift,
    upmat_w,
    upbias,
    downmat,
    downbias,
):
    captions, length, width = hidden.shape
    tokens = captions * length
    hidden2 = hidden.reshape(tokens, width)
    cot2 = cotangent.reshape(tokens, width)
    share = width // grid.count
    ff = downmat.shape[0]
    small = jnp.stack(
        [attgain, attshift, querybias, valuebias, mixbias, mlpgain, mlpshift, downbias]
    ).astype(F32)
    upsmall = upbias.astype(F32).reshape(1, -1)
    first = call(
        functools.partial(pack_kernel, grid),
        1,
        [whole((8, share)), whole((1, 96))] + [whole((share, width))] * 3,
        [whole((4, share, width))],
        [((4, share, width), BF16)],
        [pltpu.VMEM((16, width), F32)],
        1000,
        1000,
        "pack",
    )(small, upsmall, querymat.T, keymat.T, valuemat.T)[0]
    second = jnp.concatenate([mixmat.T[None], upmat_w.T.reshape(4, share, width)], axis=0)
    third = downmat.T
    where = order_of(lengths, length)
    size_at = captions * (length // TILE) + captions
    places = gather_places()
    first_a = jnp.stack([first, grid.shift(first, kz=3)])
    first_z = grid.shift(first_a, kz=1)
    first_a, first_z, second = together((first_a, first_z, second))
    first_a = gather_one(grid, first_a, first_z)
    second_a = jnp.stack([second, grid.shift(second, kz=3)])
    first_a, second_a, where = together((first_a, second_a, where))
    first_b = gather_two(grid, first_a)
    first_c = gather_core(grid, first_b[:2])
    second_z = grid.shift(second_a, kz=1)
    first_b, first_c, second_z, third = together((first_b, first_c, second_z, third))
    first_in = first_b + first_c + gather_core(grid, first_b[2:])
    second_a = gather_one(grid, second_a, second_z)
    third_a = jnp.stack([third, grid.shift(third, kz=3)])
    half = grid.count // 2
    unit = 2 * tokens * width * width
    row = (tokens, width)
    heads = captions * (width // 256)
    tall = (tokens + 64, width)
    square = pltpu.VMEM((width, width), F32)
    moved, normed, query, keys, values, vec, held_one = call_near(
        functools.partial(project_kernel, grid, places),
        [SMEM] + [FAST] * (1 + len(first_in)),
        [(row, BF16)] * 5 + [((share, width), F32), ((grid.count, 3, share, width), BF16)],
        [],
        5 * unit,
        "project",
    )(where, hidden2, *first_in)
    second_a, third_a, query = together((second_a, third_a, query))
    third_z = grid.shift(third_a, kz=1)
    second_b = gather_two(grid, second_a)
    second_c = gather_core(grid, second_b[:2])
    probs, mixed = call_near(
        functools.partial(attend_kernel, length, 4),
        [SMEM] * 2 + [FAST] * 3,
        [((heads, length, 256), BF16), (row, BF16)],
        [],
        5 * unit,
        "attend",
    )(lengths, where, query, keys, values)
    second_b, second_c, third_z, mixed = together((second_b, second_c, third_z, mixed))
    second_in = second_b + second_c + gather_core(grid, second_b[2:])
    third_a = gather_one(grid, third_a, third_z)
    middle, normed2, active, slope, held_two = call_near(
        functools.partial(upper_kernel, grid, places),
        [FAST] * (3 + len(second_in)),
        [(row, F32), (row, BF16), ((tokens, ff), BF16), ((tokens, ff), BF16), ((grid.count,) + second.shape, BF16)],
        [],
        9 * unit,
        "upper",
    )(moved, mixed, vec, *second_in)
    third_a, active = together((third_a, active))
    third_b = gather_two(grid, third_a)
    third_c = gather_core(grid, third_b[:2])
    low, down_vec, down_own, down_other, active = call_near(
        functools.partial(down_grad_kernel, grid, length, size_at),
        [SMEM] * 2 + [FAST] * 2,
        [(row, BF16), ((8, width), F32)] + [((half, share, ff), BF16)] * 2 + [((tokens, ff), BF16)],
        [square, pltpu.SemaphoreType.DMA],
        5 * unit,
        "down_grad",
        far=1,
    )(lengths, where, cot2, active)
    third_b, third_c, down_own, down_other = together((third_b, third_c, down_own, down_other))
    third_in = third_b + third_c + gather_core(grid, third_b[2:])
    down_two = scatter_first(grid, down_own, scatter_core(grid, down_other))
    low = tie(low, down_two[-1])
    grad_upper, up_vec, up_own, up_other, lower_w = call_near(
        functools.partial(upper_grad_kernel, grid, places, size_at),
        [SMEM] + [FAST] * (3 + len(third_in)),
        [((tokens, ff), BF16), ((32, width), F32)]
        + [((half, 4, share, width), BF16)] * 2
        + [((grid.count, share, ff), BF16)],
        [pltpu.VMEM((grid.count, share, ff), BF16), square, pltpu.SemaphoreType.DMA],
        8 * unit,
        "upper_grad",
        limit=12,
        aliases={2: 0},
        far=1,
    )(where, low, slope, normed2, *third_in)
    down_two, up_vec, up_own, up_other = together((down_two, up_vec, up_own, up_other))
    down_three = scatter_second(grid, down_two, up_vec)
    up_one = scatter_core(grid, up_other)
    grad_upper = tie(grad_upper, down_three[-1])
    grad_middle, branch, dm, mid_vec = call_near(
        functools.partial(middle_grad_kernel, grid, size_at),
        [SMEM] + [FAST] * 5,
        [(row, F32), (row, BF16), (tall, BF16), ((8, width), F32)],
        [],
        6 * unit,
        "middle_grad",
    )(where, grad_upper, middle, low, vec, held_two)
    down_four = scatter_third(grid, down_three, mid_vec)
    up_two = scatter_first(grid, up_own, tie(up_one, mid_vec))
    dm = tie(dm, (up_two[-1], down_four[-1]))
    grads, att_vec = call_near(
        functools.partial(attend_grad_kernel, length, 4),
        [SMEM] * 2 + [FAST] * 5,
        [((3, tokens + 256, width), BF16), ((8, width), F32)],
        [],
        7 * unit,
        "attend_grad",
    )(lengths, where, dm, query, keys, values, probs)
    input_grad, all_vec = call_near(
        functools.partial(input_grad_kernel, grid, size_at),
        [SMEM] + [FAST] * 9,
        [(row, F32), ((16, width), F32)],
        [pltpu.VMEM(row, F32)],
        5 * unit,
        "input_grad",
    )(where, moved, grad_middle, grads, vec, down_vec, up_vec, mid_vec, att_vec, held_one)
    grads, all_vec = together((grads, all_vec))
    att_own, att_other = call_near(
        functools.partial(weight_grad_kernel, grid, size_at),
        [SMEM] + [FAST] * 4,
        [((half, 4, share, width), BF16)] * 2,
        [square],
        5 * unit,
        "weight_grad",
    )(where, grads, branch, normed, mixed)
    down_four, up_two, att_own, att_other, all_vec = together((down_four, up_two, att_own, att_other, all_vec))
    down_sum = scatter_last(down_four, all_vec)
    up_three = scatter_second(grid, up_two, all_vec)
    att_one = scatter_core(grid, att_other)
    all_vec = (all_vec + grid.shift(all_vec, kc=1)).reshape(2, 8, width)
    att_one = tie(att_one, up_three[-1])
    att_two = scatter_first(grid, att_own, att_one, all_vec)
    up_four = scatter_third(grid, up_three, att_two[-1])
    middle = tie(middle, (att_two[-1], up_four[-1]))
    steps = 4
    rows = tokens // steps
    block = pl.BlockSpec((rows, width), lambda i: (i, 0))
    (block_out,) = call(
        lower_kernel,
        steps,
        [SMEM, pl.BlockSpec((rows, ff), lambda i: (i, 0)), block, whole((share, width)), whole((grid.count, share, ff))],
        [whole(row)],
        [(row, BF16)],
        [pltpu.VMEM(row, BF16)],
        4 * unit,
        20_000_000,
        "lower",
        24,
    )(where, active, middle, vec, lower_w)
    out_gate = block_out[0:8, 0:128]
    att_three = scatter_second(grid, att_two, out_gate)
    up_sum = scatter_last(up_four, att_three[-1])
    att_four = scatter_third(grid, att_three, out_gate)
    att_sum, all_vec = scatter_last(att_four, out_gate)
    all_vec = all_vec.reshape(16, width)
    vecs = call(
        functools.partial(unpack_kernel, grid),
        1,
        [whole((16, width))],
        [whole((1, share))] * 8 + [whole((1, ff // grid.count))],
        [((1, share), F32)] * 8 + [((1, ff // grid.count), F32)],
        [],
        1000,
        1000,
        "unpack",
    )(all_vec)
    vecs = [v.reshape(-1) for v in vecs]
    return (
        block_out.reshape(hidden.shape),
        input_grad.reshape(hidden.shape),
        vecs[0],
        vecs[1],
        att_sum[0].T,
        vecs[2],
        att_sum[1].T,
        att_sum[2].T,
        vecs[3],
        att_sum[3].T,
        vecs[4],
        vecs[5],
        vecs[6],
        up_sum.reshape(ff // grid.count, width).T,
        vecs[8],
        down_sum.T,
        vecs[7],
    )


def fits(mesh):
    return mesh.shape["dp"] == 8 and mesh.shape["fsdp"] == 4


def solution(mesh):
    axes = ("dp", "fsdp")
    body = per_device
    if fits(mesh):
        axes = AXES
        grid = Grid3(mesh.shape["dp"], mesh.shape["fsdp"])
        mesh = jax.sharding.Mesh(mesh.devices.reshape(grid.z, grid.x, grid.y, grid.c), AXES)
        body = functools.partial(fast_device, grid)
    placed = (
        P(axes, None, None),
        P(axes),
        P(axes, None, None),
        P(axes),
        P(axes),
        P(None, axes),
        P(axes),
        P(None, axes),
        P(None, axes),
        P(axes),
        P(None, axes),
        P(axes),
        P(axes),
        P(axes),
        P(None, axes),
        P(axes),
        P(None, axes),
        P(axes),
    )
    return jax.shard_map(
        body,
        mesh=mesh,
        in_specs=placed,
        out_specs=(
            P(axes, None, None),
            P(axes, None, None),
            P(axes),
            P(axes),
            P(None, axes),
            P(axes),
            P(None, axes),
            P(None, axes),
            P(axes),
            P(None, axes),
            P(axes),
            P(axes),
            P(axes),
            P(None, axes),
            P(axes),
            P(None, axes),
            P(axes),
        ),
        check_vma=False,
    )
```

```python
import functools
import math

import jax
import jax.numpy as jnp
from jax import lax
from jax.experimental import pallas as pl
from jax.experimental.pallas import tpu as pltpu
from jax.sharding import PartitionSpec as P

HEADS = 12


def layer_norm(values, gain, shift):
    centre = jnp.mean(values, axis=-1, keepdims=True)
    centred = values - centre
    spread = jnp.mean(centred * centred, axis=-1, keepdims=True)
    return centred * lax.rsqrt(spread + 1e-06) * gain + shift


def smooth(values):
    return jax.nn.gelu(values, approximate=True)


def project(inputs, matrix):
    return jnp.einsum("cli,ij->clj", inputs, matrix, preferred_element_type=jnp.float32)


def project_back(grads, matrix):
    return jnp.einsum("clj,ij->cli", grads, matrix, preferred_element_type=jnp.float32)


def outer_sum(inputs, grads):
    return jnp.einsum("cli,clj->ij", inputs, grads, preferred_element_type=jnp.float32)


def token_sum(grads):
    return jnp.sum(grads.astype(jnp.float32), axis=(0, 1))


def masked_scores(query_low, keys_low, keymask, factor):
    raw = (
        jnp.einsum("clhd,cmhd->chlm", query_low, keys_low, preferred_element_type=jnp.float32)
        * factor
    )
    return jnp.where(keymask[:, None, None, :], raw, -1e30)


def per_device(
    hidden,
    lengths,
    cotangent,
    attgain,
    attshift,
    querymat,
    querybias,
    keymat,
    valuemat,
    valuebias,
    mixmat,
    mixbias,
    mlpgain,
    mlpshift,
    upmat_w,
    upbias,
    downmat,
    downbias,
):
    captions, length, width = hidden.shape
    head_size = width // HEADS
    factor = 1.0 / math.sqrt(head_size)
    positions = lax.broadcasted_iota(jnp.int32, (captions, length), 1)
    keymask = positions < lengths[:, None]
    rowmask = keymask.astype(jnp.float32)[..., None]
    gathered = (
        lax.all_gather(attgain, ("dp", "fsdp"), axis=0, tiled=True),
        lax.all_gather(attshift, ("dp", "fsdp"), axis=0, tiled=True),
        lax.all_gather(querymat, ("dp", "fsdp"), axis=1, tiled=True),
        lax.all_gather(querybias, ("dp", "fsdp"), axis=0, tiled=True),
        lax.all_gather(keymat, ("dp", "fsdp"), axis=1, tiled=True),
        lax.all_gather(valuemat, ("dp", "fsdp"), axis=1, tiled=True),
        lax.all_gather(valuebias, ("dp", "fsdp"), axis=0, tiled=True),
        lax.all_gather(mixmat, ("dp", "fsdp"), axis=1, tiled=True),
        lax.all_gather(mixbias, ("dp", "fsdp"), axis=0, tiled=True),
        lax.all_gather(mlpgain, ("dp", "fsdp"), axis=0, tiled=True),
        lax.all_gather(mlpshift, ("dp", "fsdp"), axis=0, tiled=True),
        lax.all_gather(upmat_w, ("dp", "fsdp"), axis=1, tiled=True),
        lax.all_gather(upbias, ("dp", "fsdp"), axis=0, tiled=True),
        lax.all_gather(downmat, ("dp", "fsdp"), axis=1, tiled=True),
        lax.all_gather(downbias, ("dp", "fsdp"), axis=0, tiled=True),
    )
    (
        gain_one,
        shift_one,
        query_w,
        query_b,
        keys_w,
        values_w,
        values_b,
        mixer_w,
        mixer_b,
        gain_two,
        shift_two,
        upper_w,
        upper_b,
        lower_w,
        lower_b,
    ) = gathered
    gain_one = gain_one.astype(jnp.float32)
    shift_one = shift_one.astype(jnp.float32)
    gain_two = gain_two.astype(jnp.float32)
    shift_two = shift_two.astype(jnp.float32)
    source = hidden.astype(jnp.float32)
    normed_low = layer_norm(source, gain_one, shift_one).astype(jnp.bfloat16)
    query_low = (project(normed_low, query_w) + query_b.astype(jnp.float32)).astype(jnp.bfloat16)
    keys_low = project(normed_low, keys_w).astype(jnp.bfloat16)
    values_low = (project(normed_low, values_w) + values_b.astype(jnp.float32)).astype(jnp.bfloat16)
    query_heads = query_low.reshape(captions, length, HEADS, head_size)
    keys_heads = keys_low.reshape(captions, length, HEADS, head_size)
    values_heads = values_low.reshape(captions, length, HEADS, head_size)
    scores = masked_scores(query_heads, keys_heads, keymask, factor)
    peak = jnp.max(scores, axis=-1, keepdims=True)
    logsum = peak + jnp.log(jnp.sum(jnp.exp(scores - peak), axis=-1, keepdims=True))
    probs_low = jnp.exp(scores - logsum).astype(jnp.bfloat16)
    mixed_low = (
        jnp.einsum("chlm,cmhd->clhd", probs_low, values_heads, preferred_element_type=jnp.float32)
        .reshape(captions, length, width)
        .astype(jnp.bfloat16)
    )
    middle = source + project(mixed_low, mixer_w) + mixer_b.astype(jnp.float32)
    normed2_low = layer_norm(middle, gain_two, shift_two).astype(jnp.bfloat16)
    upper = project(normed2_low, upper_w) + upper_b.astype(jnp.float32)
    active_low = smooth(upper).astype(jnp.bfloat16)
    result = middle + project(active_low, lower_w) + lower_b.astype(jnp.float32)
    block_out = result.astype(jnp.bfloat16)
    again = (
        lax.all_gather(attgain, ("dp", "fsdp"), axis=0, tiled=True),
        lax.all_gather(attshift, ("dp", "fsdp"), axis=0, tiled=True),
        lax.all_gather(querymat, ("dp", "fsdp"), axis=1, tiled=True),
        lax.all_gather(querybias, ("dp", "fsdp"), axis=0, tiled=True),
        lax.all_gather(keymat, ("dp", "fsdp"), axis=1, tiled=True),
        lax.all_gather(valuemat, ("dp", "fsdp"), axis=1, tiled=True),
        lax.all_gather(valuebias, ("dp", "fsdp"), axis=0, tiled=True),
        lax.all_gather(mixmat, ("dp", "fsdp"), axis=1, tiled=True),
        lax.all_gather(mixbias, ("dp", "fsdp"), axis=0, tiled=True),
        lax.all_gather(mlpgain, ("dp", "fsdp"), axis=0, tiled=True),
        lax.all_gather(mlpshift, ("dp", "fsdp"), axis=0, tiled=True),
        lax.all_gather(upmat_w, ("dp", "fsdp"), axis=1, tiled=True),
        lax.all_gather(upbias, ("dp", "fsdp"), axis=0, tiled=True),
        lax.all_gather(downmat, ("dp", "fsdp"), axis=1, tiled=True),
        lax.all_gather(downbias, ("dp", "fsdp"), axis=0, tiled=True),
    )
    (
        gain_one,
        shift_one,
        query_w,
        query_b,
        keys_w,
        values_w,
        values_b,
        mixer_w,
        mixer_b,
        gain_two,
        shift_two,
        upper_w,
        upper_b,
        lower_w,
        lower_b,
    ) = again
    gain_one = gain_one.astype(jnp.float32)
    shift_one = shift_one.astype(jnp.float32)
    gain_two = gain_two.astype(jnp.float32)
    shift_two = shift_two.astype(jnp.float32)
    grad_out = cotangent.astype(jnp.float32) * rowmask
    grad_low = grad_out.astype(jnp.bfloat16)
    downmat_grad = outer_sum(active_low, grad_low)
    downbias_grad = token_sum(grad_low)
    grad_active = project_back(grad_low, lower_w)
    gelu_pull = jax.vjp(smooth, upper)[1]
    grad_upper_low = gelu_pull(grad_active)[0].astype(jnp.bfloat16)
    upmat_grad = outer_sum(normed2_low, grad_upper_low)
    upbias_grad = token_sum(grad_upper_low)
    grad_normed2 = project_back(grad_upper_low, upper_w)
    norm_pull = jax.vjp(layer_norm, middle, gain_two, shift_two)[1]
    grad_ln_two, mlpgain_grad, mlpshift_grad = norm_pull(grad_normed2)
    grad_middle = grad_out + grad_ln_two
    mlpgain_grad, mlpshift_grad, upmat_grad, upbias_grad, downmat_grad, downbias_grad = (
        lax.psum_scatter(mlpgain_grad, ("dp", "fsdp"), scatter_dimension=0, tiled=True),
        lax.psum_scatter(mlpshift_grad, ("dp", "fsdp"), scatter_dimension=0, tiled=True),
        lax.psum_scatter(upmat_grad, ("dp", "fsdp"), scatter_dimension=1, tiled=True),
        lax.psum_scatter(upbias_grad, ("dp", "fsdp"), scatter_dimension=0, tiled=True),
        lax.psum_scatter(downmat_grad, ("dp", "fsdp"), scatter_dimension=1, tiled=True),
        lax.psum_scatter(downbias_grad, ("dp", "fsdp"), scatter_dimension=0, tiled=True),
    )
    grad_branch_low = grad_middle.astype(jnp.bfloat16)
    mixmat_grad = outer_sum(mixed_low, grad_branch_low)
    mixbias_grad = token_sum(grad_branch_low)
    grad_mixed_low = (
        project_back(grad_branch_low, mixer_w)
        .astype(jnp.bfloat16)
        .reshape(captions, length, HEADS, head_size)
    )
    scores_again = masked_scores(query_heads, keys_heads, keymask, factor)
    probs = jnp.exp(scores_again - logsum)
    probs_again = probs.astype(jnp.bfloat16)
    grad_values_low = jnp.einsum(
        "chlm,clhd->cmhd", probs_again, grad_mixed_low, preferred_element_type=jnp.float32
    ).astype(jnp.bfloat16)
    grad_probs = jnp.einsum(
        "clhd,cmhd->chlm", grad_mixed_low, values_heads, preferred_element_type=jnp.float32
    )
    weighted = jnp.sum(probs * grad_probs, axis=-1, keepdims=True)
    grad_scores_low = (probs * (grad_probs - weighted)).astype(jnp.bfloat16)
    grad_query_low = (
        jnp.einsum(
            "chlm,cmhd->clhd", grad_scores_low, keys_heads, preferred_element_type=jnp.float32
        )
        * factor
    ).astype(jnp.bfloat16)
    grad_keys_low = (
        jnp.einsum(
            "chlm,clhd->cmhd", grad_scores_low, query_heads, preferred_element_type=jnp.float32
        )
        * factor
    ).astype(jnp.bfloat16)
    grad_query_low = grad_query_low.reshape(captions, length, width)
    grad_keys_low = grad_keys_low.reshape(captions, length, width)
    grad_values_low = grad_values_low.reshape(captions, length, width)
    querymat_grad = outer_sum(normed_low, grad_query_low)
    querybias_grad = token_sum(grad_query_low)
    keymat_grad = outer_sum(normed_low, grad_keys_low)
    valuemat_grad = outer_sum(normed_low, grad_values_low)
    valuebias_grad = token_sum(grad_values_low)
    grad_normed = (
        project_back(grad_query_low, query_w)
        + project_back(grad_keys_low, keys_w)
        + project_back(grad_values_low, values_w)
    )
    first_pull = jax.vjp(layer_norm, source, gain_one, shift_one)[1]
    grad_ln_one, attgain_grad, attshift_grad = first_pull(grad_normed)
    input_grad = grad_middle + grad_ln_one
    (
        attgain_grad,
        attshift_grad,
        querymat_grad,
        querybias_grad,
        keymat_grad,
        valuemat_grad,
        valuebias_grad,
        mixmat_grad,
        mixbias_grad,
    ) = (
        lax.psum_scatter(attgain_grad, ("dp", "fsdp"), scatter_dimension=0, tiled=True),
        lax.psum_scatter(attshift_grad, ("dp", "fsdp"), scatter_dimension=0, tiled=True),
        lax.psum_scatter(querymat_grad, ("dp", "fsdp"), scatter_dimension=1, tiled=True),
        lax.psum_scatter(querybias_grad, ("dp", "fsdp"), scatter_dimension=0, tiled=True),
        lax.psum_scatter(keymat_grad, ("dp", "fsdp"), scatter_dimension=1, tiled=True),
        lax.psum_scatter(valuemat_grad, ("dp", "fsdp"), scatter_dimension=1, tiled=True),
        lax.psum_scatter(valuebias_grad, ("dp", "fsdp"), scatter_dimension=0, tiled=True),
        lax.psum_scatter(mixmat_grad, ("dp", "fsdp"), scatter_dimension=1, tiled=True),
        lax.psum_scatter(mixbias_grad, ("dp", "fsdp"), scatter_dimension=0, tiled=True),
    )
    return (
        block_out,
        input_grad,
        attgain_grad,
        attshift_grad,
        querymat_grad,
        querybias_grad,
        keymat_grad,
        valuemat_grad,
        valuebias_grad,
        mixmat_grad,
        mixbias_grad,
        mlpgain_grad,
        mlpshift_grad,
        upmat_grad,
        upbias_grad,
        downmat_grad,
        downbias_grad,
    )


NT = (((1,), (1,)), ((), ()))
NN = (((1,), (0,)), ((), ()))
TN = (((0,), (0,)), ((), ()))
F32 = jnp.float32
BF16 = jnp.bfloat16
AXES = ("z", "x", "y", "c")
QUAD = 4
VMEM_LIMIT = 56 * 1024 * 1024


def dot(left, right, dims):
    return lax.dot_general(left, right, dims, preferred_element_type=F32)


class Grid3:
    def __init__(self, dp, fsdp):
        self.c = 2
        self.y = fsdp // 2
        self.x = self.y
        self.z = dp // self.x
        self.count = dp * fsdp

    def index(self, z, x, y, c):
        return ((z * self.x + x) * self.y + y) * self.c + c

    def shift(self, values, kz=0, kx=0, ky=0, kc=0):
        pairs = []
        for z in range(self.z):
            for x in range(self.x):
                for y in range(self.y):
                    for c in range(self.c):
                        pairs.append((self.index(z, x, y, c), self.index(z ^ kz, x ^ kx, y ^ ky, c ^ kc)))
        return lax.ppermute(values, AXES, pairs)

    def here(self):
        return tuple(lax.axis_index(name) for name in AXES)

    def me(self):
        return self.index(*self.here())

    def away(self, *bits):
        return self.index(*(lax.bitwise_xor(at, jnp.int32(bit)) for at, bit in zip(self.here(), bits)))


def tie(values, gate):
    return lax.optimization_barrier((values, gate))[0]


def together(values):
    return lax.optimization_barrier(values)


COLUMN = (0, 3, 1, 2)


def gather_one(grid, first, second):
    return first, second, grid.shift(first, kx=1), grid.shift(second, ky=1)


def gather_two(grid, four):
    first, second, first_x, second_y = four
    one = jnp.concatenate([first, first_x])
    two = jnp.concatenate([second, second_y])
    return one, two, grid.shift(one, ky=1), grid.shift(two, kx=1)


def gather_core(grid, arrays):
    return tuple(grid.shift(array, kc=1) for array in arrays)


def gather_places():
    first, second = COLUMN[:2], COLUMN[2:]
    one = [(z, x, 0) for x in range(2) for z in first]
    two = [(z, 0, y) for y in range(2) for z in second]
    one_y = [(z, x, 1) for z, x, _ in one]
    two_x = [(z, 1, y) for z, _, y in two]
    return [[spot + (core,) for spot in group] for core, pair in ((0, 0), (0, 1), (1, 0), (1, 1)) for group in ((one, two), (one_y, two_x))[pair]]


def place(grid, places, refs, held):
    for ref, spots in zip(refs, places):
        for slot, spot in enumerate(spots):
            held[grid.away(*spot)] = ref[slot]


def outgoing(grid, core):
    half = grid.z // 2
    slots = []
    for which in range(2):
        for one in range(2):
            for two in range(2):
                for low in range(half):
                    kx, ky = (one, two) if which == 0 else (two, one)
                    slots.append((COLUMN[which * half + low], kx, ky, core))
    return slots


def plus(left, right):
    return (left.astype(F32) + right.astype(F32)).astype(BF16)


def scatter_core(grid, other):
    return grid.shift(other, kc=1)


def join(values, extra):
    values = values.reshape(-1, 8, values.shape[-1])
    return values if extra is None else jnp.concatenate([values, extra])


def part(values, shape):
    count = math.prod(shape[:-1]) // 8
    return values[:count].reshape(shape), values[count:]


def scatter_first(grid, own, arrived, extra=None):
    shape = (2, 2, 2, grid.z // 2) + own.shape[1:]
    own = own.reshape(shape)
    arrived = arrived.reshape(shape)
    send_a = plus(own[0, 1], arrived[0, 1])
    send_b = plus(own[1, 1], arrived[1, 1])
    keep_a = plus(own[0, 0], arrived[0, 0])
    keep_b = plus(own[1, 0], arrived[1, 0])
    if extra is not None:
        send_a = join(send_a, extra.astype(BF16))
    return keep_a, keep_b, grid.shift(send_a, kx=1), grid.shift(send_b, ky=1), extra, (send_a, send_b)


def scatter_second(grid, state, gate):
    keep_a, keep_b, got_a, got_b, extra, _ = state
    got_a, got_b = tie((got_a, got_b), gate)
    if extra is not None:
        got_a, more = part(got_a, keep_a.shape)
        extra = extra + more.astype(F32)
    next_a = plus(keep_a[1], got_a[1])
    next_b = plus(keep_b[1], got_b[1])
    rest_a = plus(keep_a[0], got_a[0])
    rest_b = plus(keep_b[0], got_b[0])
    if extra is not None:
        next_a = join(next_a, extra.astype(BF16))
    return rest_a, rest_b, grid.shift(next_a, ky=1), grid.shift(next_b, kx=1), extra, (next_a, next_b)


def scatter_third(grid, state, gate):
    rest_a, rest_b, last_a, last_b, extra, _ = state
    last_a, last_b = tie((last_a, last_b), gate)
    if extra is not None:
        last_a, more = part(last_a, rest_a.shape)
        extra = extra + more.astype(F32)
    half = grid.z // 2
    parts = [plus(rest_a[k], last_a[k]) for k in range(half)] + [plus(rest_b[k], last_b[k]) for k in range(half)]
    sends = parts[1:]
    if extra is not None:
        sends = [join(send, extra.astype(BF16)) for send in sends]
    return parts[0], [grid.shift(send, kz=k) for send, k in zip(sends, COLUMN[1:])], extra, sends


def scatter_last(state, gate):
    total, came, extra, _ = state
    shape = total.shape
    came = tie(came, gate)
    total = total.astype(F32)
    for values in came:
        if extra is not None:
            values, more = part(values, shape)
            extra = extra + more.astype(F32)
        total = total + values.astype(F32)
    return total if extra is None else (total, extra)


def lanes_of(rows):
    return lax.broadcasted_iota(jnp.int32, (rows, 256), 1) // 64


def spread(block):
    head = lanes_of(block.shape[0])
    zero = jnp.zeros_like(block)
    return jnp.concatenate([jnp.where(head == g, block, zero) for g in range(QUAD)], axis=0)


def collect(square):
    head = lanes_of(64)
    total = jnp.where(head == 0, square[0:64], 0.0)
    for g in range(1, QUAD):
        total = jnp.where(head == g, square[64 * g : 64 * g + 64], total)
    return total


def normal(values):
    centre = jnp.mean(values, axis=-1, keepdims=True)
    centred = values - centre
    spread_of = jnp.mean(centred * centred, axis=-1, keepdims=True)
    scale = lax.rsqrt(spread_of + 1e-06)
    return centred * scale, scale


def normal_back(hat, scale, gain, grads):
    weighted = grads * gain
    middle = jnp.mean(weighted, axis=-1, keepdims=True)
    along = jnp.mean(weighted * hat, axis=-1, keepdims=True)
    return scale * (weighted - middle - hat * along)


TILE = 16
SIZES = (384, 512, 640, 768, 896, 1024)


def order_of(lengths, length):
    captions = lengths.shape[0]
    tiles = length // TILE
    real = (lengths + (TILE - 1)) // TILE
    before = jnp.tril(jnp.ones((captions, captions), jnp.int32), -1)
    start = jnp.sum(before * real[None, :], axis=1)
    total = jnp.sum(real)
    late = total + jnp.sum(before * (tiles - real)[None, :], axis=1)
    at = jnp.arange(tiles, dtype=jnp.int32)[None, :]
    spots = jnp.where(at < real[:, None], start[:, None] + at, late[:, None] + at - real[:, None])
    sizes = jnp.array(SIZES, jnp.int32)
    size = jnp.min(jnp.where(sizes >= total * TILE, sizes, SIZES[-1]))
    return jnp.concatenate([spots.reshape(-1), start, jnp.stack([size, total])]).astype(jnp.int32)


def tile_rows(place_ref, index):
    return pl.ds(pl.multiple_of(place_ref[index] * TILE, TILE), TILE)


def by_size(size, body):
    for rows in SIZES:
        pl.when(size == rows)(functools.partial(body, rows))


def rows_at(step, rows):
    return pl.ds(pl.multiple_of(step * rows, rows), rows)


def pack_kernel(grid, small_ref, q_ref, k_ref, v_ref, out_ref, wide, sems):
    copies = [
        pltpu.make_async_copy(ref, out_ref.at[3 * at : 3 * at + 3], sems.at[at])
        for at, ref in enumerate((q_ref, k_ref, v_ref))
    ]
    for copy in copies:
        copy.start()
    share = small_ref.shape[1]
    wide[...] = jnp.zeros_like(wide)
    wide[:, 0:share] = small_ref[...].astype(F32)
    out_ref[9] = pltpu.roll(wide[...], grid.me() * share, 1).astype(BF16)
    for copy in copies:
        copy.wait()


def pack_up_kernel(grid, small_ref, out_ref, wide):
    width = wide.shape[1]
    wide[...] = jnp.zeros_like(wide)
    wide[0:1, 0 : small_ref.shape[1]] = small_ref[...]
    me = grid.me()
    four = pltpu.roll(wide[...], lax.rem(me, 8) * small_ref.shape[1], 1)
    row = lax.broadcasted_iota(jnp.int32, (8, width), 0)
    four = jnp.where(row == lax.div(me, 8), jnp.broadcast_to(four[0:1], (8, width)), 0.0)
    out_ref[0] = four.astype(BF16)


def project_kernel(grid, places, place_ref, hidden_ref, *rest):
    count = len(places)
    refs, rest = rest[:count], rest[count:]
    moved_ref, normed_out, q_ref, k_ref, v_ref, vec_ref, held = rest
    total = jnp.zeros(vec_ref.shape, F32)
    for ref, spots in zip(refs, places):
        for slot, spot in enumerate(spots):
            total = total + ref[slot, 9].astype(F32)
            held[grid.away(*spot)] = ref[slot, 0:9]
    vec_ref[...] = total
    width = hidden_ref.shape[1]
    rows = 256

    def block(step, carry):
        at = rows_at(step, rows)
        hidden = hidden_ref[at, :]
        hat, _ = normal(hidden.astype(F32))
        normed = (hat * vec_ref[0:1, :] + vec_ref[1:2, :]).astype(BF16)
        q_ref[at, :] = (dot(normed, held[:, 0 : 3].reshape(width, width), NT) + vec_ref[2:3, :]).astype(BF16)
        k_ref[at, :] = dot(normed, held[:, 3 : 6].reshape(width, width), NT).astype(BF16)
        v_ref[at, :] = (dot(normed, held[:, 6 : 9].reshape(width, width), NT) + vec_ref[3:4, :]).astype(BF16)
        for t in range(rows // TILE):
            to = tile_rows(place_ref, step * (rows // TILE) + t)
            part = slice(t * TILE, (t + 1) * TILE)
            normed_out[to, :] = normed[part, :]
            moved_ref[to, :] = hidden[part, :]
        return carry

    lax.fori_loop(0, hidden_ref.shape[0] // rows, block, 0)


def attend_kernel(length, group, lengths_ref, place_ref, q_ref, k_ref, v_ref, probs_ref, mixed_out):
    width = q_ref.shape[1]
    captions = q_ref.shape[0] // length
    tiles = length // TILE
    quads = width // 256
    position = lax.broadcasted_iota(jnp.int32, (length, 256), 0)

    def several(step, carry):
        items = [
            (step * group + g, quad, rows_at(step * group + g, length), slice(256 * quad, 256 * quad + 256))
            for g in range(group)
            for quad in range(quads)
        ]
        scores = [dot(k_ref[rows, lanes], spread(q_ref[rows, lanes]), NT) for _, _, rows, lanes in items]
        probs = []
        for (cap, _, _, _), score in zip(items, scores):
            score = jnp.where(position < lengths_ref[cap], score * 0.125, -1e30)
            raised = jnp.exp(score - jnp.max(score, axis=0, keepdims=True))
            probs.append((raised * (1.0 / jnp.sum(raised, axis=0, keepdims=True))).astype(BF16))
        for (cap, quad, _, _), prob in zip(items, probs):
            probs_ref[cap * quads + quad] = prob
        mixed = [
            collect(dot(prob, v_ref[rows, lanes], TN)).astype(BF16)
            for (_, _, rows, lanes), prob in zip(items, probs)
        ]
        for (cap, _, _, lanes), value in zip(items, mixed):
            for t in range(tiles):
                to = tile_rows(place_ref, cap * tiles + t)
                mixed_out[to, lanes] = value[t * TILE : (t + 1) * TILE, :]
        return carry

    lax.fori_loop(0, captions // group, several, 0)


def bend_parts(grid, parts, normed, bias_ref, held, at, active_ref, slope_ref):
    width = normed.shape[1]
    per = grid.count // 4
    root = math.sqrt(2.0 / math.pi)
    for part in parts:
        weight = held[per * part : per * part + per, 3:15].reshape(width, width)
        upper = dot(normed, weight, NT) + bias_ref[part : part + 1, :]
        square = upper * upper
        bend = jnp.tanh(upper * (root + (root * 0.044715) * square))
        half = 0.5 * bend + 0.5
        span = slice(width * part, width * part + width)
        active = upper * half
        active_ref[at, span] = active.astype(BF16)
        slope = half + active * ((1.0 - bend) * (root + (3.0 * root * 0.044715) * square))
        slope_ref[at, span] = slope.astype(BF16)


def upper_kernel(grid, places, moved_ref, mixed_ref, vec_ref, *rest):
    count = len(places)
    refs, rest = rest[:count], rest[count:]
    middle_ref, normed_ref, active_ref, slope_ref, bias_ref, held = rest
    place(grid, places, refs, held)
    bias = jnp.zeros(bias_ref.shape, F32)
    for ref, spots in zip(refs, places):
        for slot in range(len(spots)):
            bias = bias + ref[slot, 15].astype(F32)
    bias_ref[...] = bias
    width = moved_ref.shape[1]
    rows = 256

    def block(step, carry):
        at = rows_at(step, rows)
        middle = (
            moved_ref[at, :].astype(F32)
            + dot(mixed_ref[at, :], held[:, 0:3].reshape(width, width), NT)
            + vec_ref[4:5, :]
        )
        middle_ref[at, :] = middle
        hat, _ = normal(middle)
        normed = (hat * vec_ref[5:6, :] + vec_ref[6:7, :]).astype(BF16)
        normed_ref[at, :] = normed
        bend_parts(grid, (0, 1), normed, bias_ref, held, at, active_ref, slope_ref)
        return carry

    lax.fori_loop(0, moved_ref.shape[0] // rows, block, 0)


def upper_rest_kernel(grid, normed_ref, bias_ref, held, active_in, slope_in, active_ref, slope_ref):
    rows = 256

    def block(step, carry):
        at = rows_at(step, rows)
        bend_parts(grid, (2, 3), normed_ref[at, :], bias_ref, held, at, active_ref, slope_ref)
        return carry

    lax.fori_loop(0, normed_ref.shape[0] // rows, block, 0)


def down_grad_kernel(grid, length, size_at, lengths_ref, place_ref, cot_ref, active_ref, low_ref, vec_ref, own_ref, other_ref, far_ref, total, sem):
    keep = pltpu.make_async_copy(active_ref, far_ref.at[0 : active_ref.shape[0]], sem)
    keep.start()
    width = cot_ref.shape[1]
    captions = cot_ref.shape[0] // length
    tiles = length // TILE
    position = lax.broadcasted_iota(jnp.int32, (length, 1), 0)
    vec_ref[...] = jnp.zeros_like(vec_ref)

    def caption(cap, carry):
        part = cot_ref[rows_at(cap, length), :].astype(F32)
        part = jnp.where(position < lengths_ref[cap], part, 0.0)
        vec_ref[0:1, :] += jnp.sum(part, axis=0, keepdims=True)
        part = part.astype(BF16)
        for t in range(tiles):
            low_ref[tile_rows(place_ref, cap * tiles + t), :] = part[t * TILE : (t + 1) * TILE, :]
        return carry

    lax.fori_loop(0, captions, caption, 0)
    share = width // grid.count

    def column(step, carry):
        lanes = rows_at(step, width)

        def product(rows):
            total[...] = dot(low_ref[0:rows, :], active_ref[0:rows, lanes], TN)

        by_size(place_ref[size_at], product)
        for core, out_ref in ((0, own_ref), (1, other_ref)):
            for slot, spot in enumerate(outgoing(grid, core)):
                at = pl.multiple_of(grid.away(*spot) * share, 8)
                out_ref[slot, :, lanes] = total[pl.ds(at, share), :].astype(BF16)
        return carry

    lax.fori_loop(0, active_ref.shape[1] // width, column, 0)
    keep.wait()


def upper_grad_kernel(grid, places, size_at, place_ref, low_ref, slope_ref, normed_ref, *rest):
    count = len(places)
    refs, rest = rest[:count], rest[count:]
    upper_ref, vec_ref, own_ref, other_ref, far_ref, held, total, sem = rest
    place(grid, places, refs, held)
    keep = pltpu.make_async_copy(held, far_ref.at[0 : grid.count], sem)
    keep.start()
    width = low_ref.shape[1]
    per = grid.count // 4
    share = width // per
    half = grid.z // 2
    z, x, y, c = grid.here()
    shape = own_ref.shape[1:]
    mine = jnp.where(c == 0, 0, share)

    def column(step, carry):
        lanes = rows_at(step, width)

        def product(rows):
            grads = dot(low_ref[0:rows, :], held[:, :, lanes].reshape(width, width), NN) * slope_ref[0:rows, lanes].astype(F32)
            vec_ref[rows_at(step, 8), :] = jnp.broadcast_to(jnp.sum(grads, axis=0, keepdims=True), (8, width))
            grads = grads.astype(BF16)
            upper_ref[0:rows, lanes] = grads
            total[...] = dot(grads, normed_ref[0:rows, :], TN)

        by_size(place_ref[size_at], product)
        for k in range(per // 2):
            chip = step * (per // 2) + k
            kz = lax.bitwise_xor(lax.div(chip, grid.x * grid.y), z)
            kx = lax.bitwise_xor(lax.rem(lax.div(chip, grid.y), grid.x), x)
            ky = lax.bitwise_xor(lax.rem(chip, grid.y), y)
            low = lax.div(kz, 2)
            which = lax.bitwise_xor(low, lax.rem(kz, 2))
            one = jnp.where(which == 0, kx, ky)
            two = jnp.where(which == 0, ky, kx)
            slot = ((which * 2 + one) * 2 + two) * half + low
            own_at = pl.multiple_of(2 * share * k + mine, 8)
            other_at = pl.multiple_of(2 * share * k + (share - mine), 8)
            own_ref[slot] = total[pl.ds(own_at, share), :].astype(BF16).reshape(shape)
            other_ref[slot] = total[pl.ds(other_at, share), :].astype(BF16).reshape(shape)
        return carry

    lax.fori_loop(0, upper_ref.shape[1] // width, column, 0)
    keep.wait()


def middle_grad_kernel(grid, size_at, place_ref, upper_ref, middle_ref, low_ref, vec_in, held, grad_ref, branch_ref, dm_ref, vec_ref):
    width = middle_ref.shape[1]
    per = grid.count // 4
    rows = 128
    vec_ref[...] = jnp.zeros_like(vec_ref)

    def block(step, carry):
        at = rows_at(step, rows)
        grads = dot(upper_ref[at, 0:width], held[0:per, 3:15].reshape(width, width), NN)
        for part in range(1, 4):
            weight = held[per * part : per * part + per, 3:15].reshape(width, width)
            grads = grads + dot(upper_ref[at, width * part : width * part + width], weight, NN)
        hat, scale = normal(middle_ref[at, :])
        grad_middle = low_ref[at, :].astype(F32) + normal_back(hat, scale, vec_in[5:6, :], grads)
        grad_ref[at, :] = grad_middle
        branch = grad_middle.astype(BF16)
        branch_ref[at, :] = branch
        dm_ref[at, :] = dot(branch, held[:, 0:3].reshape(width, width), NN).astype(BF16)
        vec_ref[0:1, :] += jnp.sum(grads * hat, axis=0, keepdims=True)
        vec_ref[1:2, :] += jnp.sum(grads, axis=0, keepdims=True)
        vec_ref[2:3, :] += jnp.sum(grad_middle, axis=0, keepdims=True)
        return carry

    lax.fori_loop(0, lax.div(place_ref[size_at], rows), block, 0)


def attend_grad_kernel(length, group, lengths_ref, place_ref, dm_ref, q_ref, k_ref, v_ref, probs_ref, grads_ref, vec_ref):
    width = dm_ref.shape[1]
    quads = width // 256
    tiles = length // TILE
    captions = probs_ref.shape[0] // quads
    starts = captions * tiles
    end = place_ref[starts + captions + 1]
    clear = pl.ds(pl.multiple_of(end * TILE, TILE), 256)
    for which in range(3):
        grads_ref[which, clear, :] = jnp.zeros((256, width), BF16)
    vec_ref[...] = jnp.zeros_like(vec_ref)
    row = lax.broadcasted_iota(jnp.int32, (length, 1), 0)

    def several(step, carry):
        items = []
        for g in range(group):
            cap = step * group + g
            packed = pl.ds(pl.multiple_of(place_ref[starts + cap] * TILE, TILE), length)
            plain = pl.ds(pl.multiple_of(cap * length, length), length)
            for quad in range(quads):
                items.append((cap, quad, packed, plain, slice(256 * quad, 256 * quad + 256)))
        probs = [probs_ref[cap * quads + quad] for cap, quad, _, _, _ in items]
        wide = []
        for cap, _, packed, _, lanes in items:
            dm = dm_ref[packed, lanes]
            wide.append(spread(jnp.where(row < lengths_ref[cap], dm, jnp.zeros_like(dm))))
        grad_probs = [dot(v_ref[plain, lanes], w, NT) for (_, _, _, plain, lanes), w in zip(items, wide)]
        grad_values = [dot(p, w, NN) for p, w in zip(probs, wide)]
        grad_scores = []
        for p, grad in zip(probs, grad_probs):
            p = p.astype(F32)
            along = p * grad
            grad_scores.append((along - p * jnp.sum(along, axis=0, keepdims=True)).astype(BF16))
        grad_keys = [
            dot(g, spread(q_ref[plain, lanes]), NN) * 0.125 for (_, _, _, plain, lanes), g in zip(items, grad_scores)
        ]
        grad_query = [
            collect(dot(g, k_ref[plain, lanes], TN)) * 0.125 for (_, _, _, plain, lanes), g in zip(items, grad_scores)
        ]
        for at, (_, _, packed, _, lanes) in enumerate(items):
            grads_ref[0, packed, lanes] = grad_query[at].astype(BF16)
            grads_ref[1, packed, lanes] = grad_keys[at].astype(BF16)
            grads_ref[2, packed, lanes] = grad_values[at].astype(BF16)
        for quad in range(quads):
            lanes = slice(256 * quad, 256 * quad + 256)
            vec_ref[0:1, lanes] += sum(jnp.sum(v, axis=0, keepdims=True) for v in grad_query[quad::quads])
            vec_ref[1:2, lanes] += sum(jnp.sum(v, axis=0, keepdims=True) for v in grad_values[quad::quads])
        return carry

    lax.fori_loop(0, captions // group, several, 0)


def weight_grad_kernel(grid, size_at, place_ref, grads_ref, branch_ref, normed_ref, mixed_ref, own_ref, other_ref, total):
    share = total.shape[0] // grid.count

    def send(at):
        for core, out_ref in ((0, own_ref), (1, other_ref)):
            for slot, spot in enumerate(outgoing(grid, core)):
                start = pl.multiple_of(grid.away(*spot) * share, 8)
                out_ref[slot, at] = total[pl.ds(start, share), :].astype(BF16)

    def matrix(at, carry):
        def product(rows):
            total[...] = dot(grads_ref[at, 0:rows, :], normed_ref[0:rows, :], TN)

        by_size(place_ref[size_at], product)
        send(at)
        return carry

    lax.fori_loop(0, 3, matrix, 0)

    def product(rows):
        total[...] = dot(branch_ref[0:rows, :], mixed_ref[0:rows, :], TN)

    by_size(place_ref[size_at], product)
    send(3)


def input_grad_kernel(grid, size_at, place_ref, moved_ref, grad_ref, grads_ref, vec_in, down_vec, up_vec, mid_vec, att_vec, held, out_ref, vec_ref, found):
    rows = 128
    width = moved_ref.shape[1]
    vec_ref[...] = jnp.zeros_like(vec_ref)
    vec_ref[2:4, :] = att_vec[0:2, :]
    vec_ref[4:5, :] = mid_vec[2:3, :]
    vec_ref[5:7, :] = mid_vec[0:2, :]
    vec_ref[7:8, :] = down_vec[0:1, :]
    for part in range(4):
        vec_ref[8 + part : 9 + part, :] = up_vec[8 * part : 8 * part + 1, :]

    def block(step, carry):
        at = rows_at(step, rows)
        grads = dot(grads_ref[0, at, :], held[:, 0 : 3].reshape(width, width), NN)
        grads = grads + dot(grads_ref[1, at, :], held[:, 3 : 6].reshape(width, width), NN)
        grads = grads + dot(grads_ref[2, at, :], held[:, 6 : 9].reshape(width, width), NN)
        hat, scale = normal(moved_ref[at, :].astype(F32))
        found[at, :] = grad_ref[at, :] + normal_back(hat, scale, vec_in[0:1, :], grads)
        vec_ref[0:1, :] += jnp.sum(grads * hat, axis=0, keepdims=True)
        vec_ref[1:2, :] += jnp.sum(grads, axis=0, keepdims=True)
        return carry

    lax.fori_loop(0, lax.div(place_ref[size_at], rows), block, 0)
    total = place_ref[size_at + 1]

    def tile(index, carry):
        values = found[tile_rows(place_ref, index), :]
        out_ref[rows_at(index, TILE), :] = jnp.where(place_ref[index] < total, values, 0.0)
        return carry

    lax.fori_loop(0, out_ref.shape[0] // TILE, tile, 0)


def lower_kernel(place_ref, active_far, middle_ref, vec_in, weight_far, out_ref, weight, active, found, sems):
    count, rows = active.shape[0], active.shape[1]
    copies = [
        pltpu.make_async_copy(active_far.at[rows * step : rows * step + rows], active.at[step], sems.at[step])
        for step in range(count)
    ]
    fetch = pltpu.make_async_copy(weight_far.at[0 : weight.shape[0]], weight, sems.at[count])
    fetch.start()
    for copy in copies:
        copy.start()
    fetch.wait()
    for copy in copies:
        copy.wait()

    def block(step, carry):
        at = rows_at(step, rows)
        whole_weight = weight[...].reshape(middle_ref.shape[1], active.shape[2])
        out = middle_ref[at, :] + dot(active[step], whole_weight, NT) + vec_in[7:8, :]
        found[at, :] = out.astype(BF16)
        return carry

    lax.fori_loop(0, count, block, 0)

    def tile(index, carry):
        out_ref[rows_at(index, TILE), :] = found[tile_rows(place_ref, index), :]
        return carry

    lax.fori_loop(0, out_ref.shape[0] // TILE, tile, 0)


def unpack_kernel(grid, vec_ref, *outs):
    me = grid.me()
    eight = pltpu.roll(vec_ref[0:8, :], lax.rem(768 - me * 24, 768), 1)
    for k in range(8):
        outs[k][...] = eight[k : k + 1, 0:24]
    row = lax.broadcasted_iota(jnp.int32, (8, 768), 0)
    four = jnp.sum(jnp.where(row == lax.div(me, 8), vec_ref[8:16, :], 0.0), axis=0, keepdims=True)
    four = jnp.broadcast_to(four, (8, 768))
    four = pltpu.roll(four, lax.rem(768 - lax.rem(me, 8) * 96, 768), 1)
    outs[8][...] = four[0:1, 0:96]


def whole(shape):
    return pl.BlockSpec(shape, lambda *_: (0,) * len(shape))


ANY = pl.BlockSpec(memory_space=pl.ANY)
SMEM = pl.BlockSpec(memory_space=pltpu.SMEM)


FAST = pl.BlockSpec(memory_space=pltpu.VMEM)
FAR = pl.BlockSpec(memory_space=pltpu.HBM)
LARGE = 1 << 26


def call(kernel, steps, in_specs, out_specs, outs, scratch, flops, moved, name, limit=8):
    return pl.pallas_call(
        kernel,
        grid=(steps,),
        in_specs=in_specs,
        out_specs=out_specs,
        out_shape=[jax.ShapeDtypeStruct(s, d) for s, d in outs],
        scratch_shapes=scratch,
        compiler_params=pltpu.CompilerParams(vmem_limit_bytes=limit * 1024 * 1024),
        cost_estimate=pl.CostEstimate(flops=flops, bytes_accessed=moved, transcendentals=0),
        name=name,
    )


def call_near(kernel, in_specs, outs, scratch, flops, name, limit=8, aliases=None, far=0):
    return pl.pallas_call(
        kernel,
        in_specs=in_specs,
        out_specs=[FAST] * (len(outs) - far) + [FAR] * far,
        input_output_aliases=aliases or {},
        out_shape=[jax.ShapeDtypeStruct(s, d) for s, d in outs],
        scratch_shapes=scratch,
        compiler_params=pltpu.CompilerParams(vmem_limit_bytes=limit * 1024 * 1024),
        cost_estimate=pl.CostEstimate(flops=flops, bytes_accessed=1_000_000, transcendentals=0),
        name=name,
    )


def fast_device(
    grid,
    hidden,
    lengths,
    cotangent,
    attgain,
    attshift,
    querymat,
    querybias,
    keymat,
    valuemat,
    valuebias,
    mixmat,
    mixbias,
    mlpgain,
    mlpshift,
    upmat_w,
    upbias,
    downmat,
    downbias,
):
    captions, length, width = hidden.shape
    tokens = captions * length
    hidden2 = hidden.reshape(tokens, width)
    cot2 = cotangent.reshape(tokens, width)
    share = width // grid.count
    ff = downmat.shape[0]
    small = jnp.stack([attgain, attshift, querybias, valuebias, mixbias, mlpgain, mlpshift, downbias])
    units = share // 8
    (first,) = pl.pallas_call(
        functools.partial(pack_kernel, grid),
        in_specs=[FAST] + [FAR] * 3,
        out_specs=[FAST],
        out_shape=[jax.ShapeDtypeStruct((3 * units + 1, 8, width), BF16)],
        scratch_shapes=[pltpu.VMEM((8, width), F32), pltpu.SemaphoreType.DMA((3,))],
        name="pack",
    )(small, *(w.T.reshape(units, 8, width) for w in (querymat, keymat, valuemat)))
    (up_bias,) = call_near(
        functools.partial(pack_up_kernel, grid),
        [FAST],
        [((1, 8, width), BF16)],
        [pltpu.VMEM((8, width), F32)],
        1000,
        "pack_up",
    )(upbias.astype(F32).reshape(1, -1))
    second = jnp.concatenate(
        [mixmat.T.reshape(units, 8, width), upmat_w.T.reshape(4 * units, 8, width), up_bias], axis=0
    )
    third = downmat.T
    where = order_of(lengths, length)
    size_at = captions * (length // TILE) + captions
    places = gather_places()
    first_a = jnp.stack([first, grid.shift(first, kz=3)])
    first_z = grid.shift(first_a, kz=1)
    first_a, first_z, second = together((first_a, first_z, second))
    first_a = gather_one(grid, first_a, first_z)
    second_a = jnp.stack([second, grid.shift(second, kz=3)])
    first_a, second_a, where = together((first_a, second_a, where))
    first_b = gather_two(grid, first_a)
    first_c = gather_core(grid, first_b[:2])
    second_z = grid.shift(second_a, kz=1)
    first_b, first_c, second_z, third = together((first_b, first_c, second_z, third))
    first_in = first_b + first_c + gather_core(grid, first_b[2:])
    second_a = gather_one(grid, second_a, second_z)
    third_a = jnp.stack([third, grid.shift(third, kz=3)])
    half = grid.count // 2
    unit = 2 * tokens * width * width
    row = (tokens, width)
    heads = captions * (width // 256)
    tall = (tokens + 64, width)
    square = pltpu.VMEM((width, width), F32)
    moved, normed, query, keys, values, vec, held_one = call_near(
        functools.partial(project_kernel, grid, places),
        [SMEM] + [FAST] * (1 + len(first_in)),
        [(row, BF16)] * 5 + [((8, width), F32), ((grid.count, 3 * units, 8, width), BF16)],
        [],
        5 * unit,
        "project",
    )(where, hidden2, *first_in)
    second_a, third_a, query = together((second_a, third_a, query))
    third_z = grid.shift(third_a, kz=1)
    second_b = gather_two(grid, second_a)
    second_c = gather_core(grid, second_b[:2])
    probs, mixed = call_near(
        functools.partial(attend_kernel, length, 4),
        [SMEM] * 2 + [FAST] * 3,
        [((heads, length, 256), BF16), (row, BF16)],
        [],
        5 * unit,
        "attend",
    )(lengths, where, query, keys, values)
    second_b, second_c, third_z, mixed = together((second_b, second_c, third_z, mixed))
    second_in = second_b + second_c + gather_core(grid, second_b[2:])
    third_a = gather_one(grid, third_a, third_z)
    middle, normed2, active, slope, bias, held_two = call_near(
        functools.partial(upper_kernel, grid, places),
        [FAST] * (3 + len(second_in)),
        [(row, F32), (row, BF16), ((tokens, ff), BF16), ((tokens, ff), BF16), ((8, width), F32)]
        + [((grid.count,) + second.shape, BF16)],
        [],
        6 * unit,
        "upper",
    )(moved, mixed, vec, *second_in)
    third_a, normed2 = together((third_a, normed2))
    active, slope = call_near(
        functools.partial(upper_rest_kernel, grid),
        [FAST] * 5,
        [((tokens, ff), BF16)] * 2,
        [],
        4 * unit,
        "upper_rest",
        aliases={3: 0, 4: 1},
    )(normed2, bias, held_two, active, slope)
    third_b = gather_two(grid, third_a)
    third_c = gather_core(grid, third_b[:2])
    low, down_vec, down_own, down_other, active_far = call_near(
        functools.partial(down_grad_kernel, grid, length, size_at),
        [SMEM] * 2 + [FAST] * 2,
        [(row, BF16), ((8, width), F32)] + [((half, share, ff), BF16)] * 2 + [((LARGE // (2 * ff), ff), BF16)],
        [square, pltpu.SemaphoreType.DMA],
        5 * unit,
        "down_grad",
        far=1,
    )(lengths, where, cot2, active)
    third_b, third_c, down_own, down_other = together((third_b, third_c, down_own, down_other))
    third_in = third_b + third_c + gather_core(grid, third_b[2:])
    down_two = scatter_first(grid, down_own, scatter_core(grid, down_other))
    low = tie(low, down_two[-1])
    grad_upper, up_vec, up_own, up_other, lower_w = call_near(
        functools.partial(upper_grad_kernel, grid, places, size_at),
        [SMEM] + [FAST] * (3 + len(third_in)),
        [((tokens, ff), BF16), ((32, width), F32)]
        + [((half, 4, share, width), BF16)] * 2
        + [((LARGE // (2 * share * ff), share, ff), BF16)],
        [pltpu.VMEM((grid.count, share, ff), BF16), square, pltpu.SemaphoreType.DMA],
        8 * unit,
        "upper_grad",
        limit=12,
        aliases={2: 0},
        far=1,
    )(where, low, slope, normed2, *third_in)
    down_two, up_vec, up_own, up_other = together((down_two, up_vec, up_own, up_other))
    down_three = scatter_second(grid, down_two, up_vec)
    up_one = scatter_core(grid, up_other)
    grad_upper = tie(grad_upper, down_three[-1])
    grad_middle, branch, dm, mid_vec = call_near(
        functools.partial(middle_grad_kernel, grid, size_at),
        [SMEM] + [FAST] * 5,
        [(row, F32), (row, BF16), (tall, BF16), ((8, width), F32)],
        [],
        6 * unit,
        "middle_grad",
    )(where, grad_upper, middle, low, vec, held_two)
    down_four = scatter_third(grid, down_three, mid_vec)
    up_two = scatter_first(grid, up_own, tie(up_one, mid_vec))
    dm = tie(dm, (up_two[-1], down_four[-1]))
    grads, att_vec = call_near(
        functools.partial(attend_grad_kernel, length, 4),
        [SMEM] * 2 + [FAST] * 5,
        [((3, tokens + 256, width), BF16), ((8, width), F32)],
        [],
        7 * unit,
        "attend_grad",
    )(lengths, where, dm, query, keys, values, probs)
    input_grad, all_vec = call_near(
        functools.partial(input_grad_kernel, grid, size_at),
        [SMEM] + [FAST] * 9,
        [(row, F32), ((16, width), F32)],
        [pltpu.VMEM(row, F32)],
        5 * unit,
        "input_grad",
    )(where, moved, grad_middle, grads, vec, down_vec, up_vec, mid_vec, att_vec, held_one)
    grads, all_vec = together((grads, all_vec))
    att_own, att_other = call_near(
        functools.partial(weight_grad_kernel, grid, size_at),
        [SMEM] + [FAST] * 4,
        [((half, 4, share, width), BF16)] * 2,
        [square],
        5 * unit,
        "weight_grad",
    )(where, grads, branch, normed, mixed)
    down_four, up_two, att_own, att_other, all_vec = together((down_four, up_two, att_own, att_other, all_vec))
    down_sum = scatter_last(down_four, all_vec)
    up_three = scatter_second(grid, up_two, all_vec)
    att_one = scatter_core(grid, att_other)
    all_vec = (all_vec + grid.shift(all_vec, kc=1)).reshape(2, 8, width)
    att_one = tie(att_one, up_three[-1])
    att_two = scatter_first(grid, att_own, att_one, all_vec)
    up_four = scatter_third(grid, up_three, att_two[-1])
    middle = tie(middle, (att_two[-1], up_four[-1]))
    (block_out,) = call_near(
        lower_kernel,
        [SMEM, FAR, FAST, FAST, FAR],
        [(row, BF16)],
        [
            pltpu.VMEM((grid.count, share, ff), BF16),
            pltpu.VMEM((4, tokens // 4, ff), BF16),
            pltpu.VMEM(row, BF16),
            pltpu.SemaphoreType.DMA((5,)),
        ],
        5 * unit,
        "lower",
        limit=20,
    )(where, active_far, middle, vec, lower_w)
    out_gate = block_out[0:8, 0:128]
    att_three = scatter_second(grid, att_two, out_gate)
    up_sum = scatter_last(up_four, att_three[-1])
    att_four = scatter_third(grid, att_three, out_gate)
    att_sum, all_vec = scatter_last(att_four, out_gate)
    all_vec = all_vec.reshape(16, width)
    vecs = call(
        functools.partial(unpack_kernel, grid),
        1,
        [whole((16, width))],
        [whole((1, share))] * 8 + [whole((1, ff // grid.count))],
        [((1, share), F32)] * 8 + [((1, ff // grid.count), F32)],
        [],
        1000,
        1000,
        "unpack",
    )(all_vec)
    vecs = [v.reshape(-1) for v in vecs]
    return (
        block_out.reshape(hidden.shape),
        input_grad.reshape(hidden.shape),
        vecs[0],
        vecs[1],
        att_sum[0].T,
        vecs[2],
        att_sum[1].T,
        att_sum[2].T,
        vecs[3],
        att_sum[3].T,
        vecs[4],
        vecs[5],
        vecs[6],
        up_sum.reshape(ff // grid.count, width).T,
        vecs[8],
        down_sum.T,
        vecs[7],
    )


def fits(mesh):
    return mesh.shape["dp"] == 8 and mesh.shape["fsdp"] == 4


def solution(mesh):
    axes = ("dp", "fsdp")
    body = per_device
    if fits(mesh):
        axes = AXES
        grid = Grid3(mesh.shape["dp"], mesh.shape["fsdp"])
        mesh = jax.sharding.Mesh(mesh.devices.reshape(grid.z, grid.x, grid.y, grid.c), AXES)
        body = functools.partial(fast_device, grid)
    placed = (
        P(axes, None, None),
        P(axes),
        P(axes, None, None),
        P(axes),
        P(axes),
        P(None, axes),
        P(axes),
        P(None, axes),
        P(None, axes),
        P(axes),
        P(None, axes),
        P(axes),
        P(axes),
        P(axes),
        P(None, axes),
        P(axes),
        P(None, axes),
        P(axes),
    )
    return jax.shard_map(
        body,
        mesh=mesh,
        in_specs=placed,
        out_specs=(
            P(axes, None, None),
            P(axes, None, None),
            P(axes),
            P(axes),
            P(None, axes),
            P(axes),
            P(None, axes),
            P(None, axes),
            P(axes),
            P(None, axes),
            P(axes),
            P(axes),
            P(axes),
            P(None, axes),
            P(axes),
            P(None, axes),
            P(axes),
        ),
        check_vma=False,
    )
```

```python
import functools
import math

import jax
import jax.numpy as jnp
from jax import lax
from jax.experimental import pallas as pl
from jax.experimental.pallas import tpu as pltpu
from jax.sharding import PartitionSpec as P

HEADS = 12


def layer_norm(values, gain, shift):
    centre = jnp.mean(values, axis=-1, keepdims=True)
    centred = values - centre
    spread = jnp.mean(centred * centred, axis=-1, keepdims=True)
    return centred * lax.rsqrt(spread + 1e-06) * gain + shift


def smooth(values):
    return jax.nn.gelu(values, approximate=True)


def project(inputs, matrix):
    return jnp.einsum("cli,ij->clj", inputs, matrix, preferred_element_type=jnp.float32)


def project_back(grads, matrix):
    return jnp.einsum("clj,ij->cli", grads, matrix, preferred_element_type=jnp.float32)


def outer_sum(inputs, grads):
    return jnp.einsum("cli,clj->ij", inputs, grads, preferred_element_type=jnp.float32)


def token_sum(grads):
    return jnp.sum(grads.astype(jnp.float32), axis=(0, 1))


def masked_scores(query_low, keys_low, keymask, factor):
    raw = (
        jnp.einsum("clhd,cmhd->chlm", query_low, keys_low, preferred_element_type=jnp.float32)
        * factor
    )
    return jnp.where(keymask[:, None, None, :], raw, -1e30)


def per_device(
    hidden,
    lengths,
    cotangent,
    attgain,
    attshift,
    querymat,
    querybias,
    keymat,
    valuemat,
    valuebias,
    mixmat,
    mixbias,
    mlpgain,
    mlpshift,
    upmat_w,
    upbias,
    downmat,
    downbias,
):
    captions, length, width = hidden.shape
    head_size = width // HEADS
    factor = 1.0 / math.sqrt(head_size)
    positions = lax.broadcasted_iota(jnp.int32, (captions, length), 1)
    keymask = positions < lengths[:, None]
    rowmask = keymask.astype(jnp.float32)[..., None]
    gathered = (
        lax.all_gather(attgain, ("dp", "fsdp"), axis=0, tiled=True),
        lax.all_gather(attshift, ("dp", "fsdp"), axis=0, tiled=True),
        lax.all_gather(querymat, ("dp", "fsdp"), axis=1, tiled=True),
        lax.all_gather(querybias, ("dp", "fsdp"), axis=0, tiled=True),
        lax.all_gather(keymat, ("dp", "fsdp"), axis=1, tiled=True),
        lax.all_gather(valuemat, ("dp", "fsdp"), axis=1, tiled=True),
        lax.all_gather(valuebias, ("dp", "fsdp"), axis=0, tiled=True),
        lax.all_gather(mixmat, ("dp", "fsdp"), axis=1, tiled=True),
        lax.all_gather(mixbias, ("dp", "fsdp"), axis=0, tiled=True),
        lax.all_gather(mlpgain, ("dp", "fsdp"), axis=0, tiled=True),
        lax.all_gather(mlpshift, ("dp", "fsdp"), axis=0, tiled=True),
        lax.all_gather(upmat_w, ("dp", "fsdp"), axis=1, tiled=True),
        lax.all_gather(upbias, ("dp", "fsdp"), axis=0, tiled=True),
        lax.all_gather(downmat, ("dp", "fsdp"), axis=1, tiled=True),
        lax.all_gather(downbias, ("dp", "fsdp"), axis=0, tiled=True),
    )
    (
        gain_one,
        shift_one,
        query_w,
        query_b,
        keys_w,
        values_w,
        values_b,
        mixer_w,
        mixer_b,
        gain_two,
        shift_two,
        upper_w,
        upper_b,
        lower_w,
        lower_b,
    ) = gathered
    gain_one = gain_one.astype(jnp.float32)
    shift_one = shift_one.astype(jnp.float32)
    gain_two = gain_two.astype(jnp.float32)
    shift_two = shift_two.astype(jnp.float32)
    source = hidden.astype(jnp.float32)
    normed_low = layer_norm(source, gain_one, shift_one).astype(jnp.bfloat16)
    query_low = (project(normed_low, query_w) + query_b.astype(jnp.float32)).astype(jnp.bfloat16)
    keys_low = project(normed_low, keys_w).astype(jnp.bfloat16)
    values_low = (project(normed_low, values_w) + values_b.astype(jnp.float32)).astype(jnp.bfloat16)
    query_heads = query_low.reshape(captions, length, HEADS, head_size)
    keys_heads = keys_low.reshape(captions, length, HEADS, head_size)
    values_heads = values_low.reshape(captions, length, HEADS, head_size)
    scores = masked_scores(query_heads, keys_heads, keymask, factor)
    peak = jnp.max(scores, axis=-1, keepdims=True)
    logsum = peak + jnp.log(jnp.sum(jnp.exp(scores - peak), axis=-1, keepdims=True))
    probs_low = jnp.exp(scores - logsum).astype(jnp.bfloat16)
    mixed_low = (
        jnp.einsum("chlm,cmhd->clhd", probs_low, values_heads, preferred_element_type=jnp.float32)
        .reshape(captions, length, width)
        .astype(jnp.bfloat16)
    )
    middle = source + project(mixed_low, mixer_w) + mixer_b.astype(jnp.float32)
    normed2_low = layer_norm(middle, gain_two, shift_two).astype(jnp.bfloat16)
    upper = project(normed2_low, upper_w) + upper_b.astype(jnp.float32)
    active_low = smooth(upper).astype(jnp.bfloat16)
    result = middle + project(active_low, lower_w) + lower_b.astype(jnp.float32)
    block_out = result.astype(jnp.bfloat16)
    again = (
        lax.all_gather(attgain, ("dp", "fsdp"), axis=0, tiled=True),
        lax.all_gather(attshift, ("dp", "fsdp"), axis=0, tiled=True),
        lax.all_gather(querymat, ("dp", "fsdp"), axis=1, tiled=True),
        lax.all_gather(querybias, ("dp", "fsdp"), axis=0, tiled=True),
        lax.all_gather(keymat, ("dp", "fsdp"), axis=1, tiled=True),
        lax.all_gather(valuemat, ("dp", "fsdp"), axis=1, tiled=True),
        lax.all_gather(valuebias, ("dp", "fsdp"), axis=0, tiled=True),
        lax.all_gather(mixmat, ("dp", "fsdp"), axis=1, tiled=True),
        lax.all_gather(mixbias, ("dp", "fsdp"), axis=0, tiled=True),
        lax.all_gather(mlpgain, ("dp", "fsdp"), axis=0, tiled=True),
        lax.all_gather(mlpshift, ("dp", "fsdp"), axis=0, tiled=True),
        lax.all_gather(upmat_w, ("dp", "fsdp"), axis=1, tiled=True),
        lax.all_gather(upbias, ("dp", "fsdp"), axis=0, tiled=True),
        lax.all_gather(downmat, ("dp", "fsdp"), axis=1, tiled=True),
        lax.all_gather(downbias, ("dp", "fsdp"), axis=0, tiled=True),
    )
    (
        gain_one,
        shift_one,
        query_w,
        query_b,
        keys_w,
        values_w,
        values_b,
        mixer_w,
        mixer_b,
        gain_two,
        shift_two,
        upper_w,
        upper_b,
        lower_w,
        lower_b,
    ) = again
    gain_one = gain_one.astype(jnp.float32)
    shift_one = shift_one.astype(jnp.float32)
    gain_two = gain_two.astype(jnp.float32)
    shift_two = shift_two.astype(jnp.float32)
    grad_out = cotangent.astype(jnp.float32) * rowmask
    grad_low = grad_out.astype(jnp.bfloat16)
    downmat_grad = outer_sum(active_low, grad_low)
    downbias_grad = token_sum(grad_low)
    grad_active = project_back(grad_low, lower_w)
    gelu_pull = jax.vjp(smooth, upper)[1]
    grad_upper_low = gelu_pull(grad_active)[0].astype(jnp.bfloat16)
    upmat_grad = outer_sum(normed2_low, grad_upper_low)
    upbias_grad = token_sum(grad_upper_low)
    grad_normed2 = project_back(grad_upper_low, upper_w)
    norm_pull = jax.vjp(layer_norm, middle, gain_two, shift_two)[1]
    grad_ln_two, mlpgain_grad, mlpshift_grad = norm_pull(grad_normed2)
    grad_middle = grad_out + grad_ln_two
    mlpgain_grad, mlpshift_grad, upmat_grad, upbias_grad, downmat_grad, downbias_grad = (
        lax.psum_scatter(mlpgain_grad, ("dp", "fsdp"), scatter_dimension=0, tiled=True),
        lax.psum_scatter(mlpshift_grad, ("dp", "fsdp"), scatter_dimension=0, tiled=True),
        lax.psum_scatter(upmat_grad, ("dp", "fsdp"), scatter_dimension=1, tiled=True),
        lax.psum_scatter(upbias_grad, ("dp", "fsdp"), scatter_dimension=0, tiled=True),
        lax.psum_scatter(downmat_grad, ("dp", "fsdp"), scatter_dimension=1, tiled=True),
        lax.psum_scatter(downbias_grad, ("dp", "fsdp"), scatter_dimension=0, tiled=True),
    )
    grad_branch_low = grad_middle.astype(jnp.bfloat16)
    mixmat_grad = outer_sum(mixed_low, grad_branch_low)
    mixbias_grad = token_sum(grad_branch_low)
    grad_mixed_low = (
        project_back(grad_branch_low, mixer_w)
        .astype(jnp.bfloat16)
        .reshape(captions, length, HEADS, head_size)
    )
    scores_again = masked_scores(query_heads, keys_heads, keymask, factor)
    probs = jnp.exp(scores_again - logsum)
    probs_again = probs.astype(jnp.bfloat16)
    grad_values_low = jnp.einsum(
        "chlm,clhd->cmhd", probs_again, grad_mixed_low, preferred_element_type=jnp.float32
    ).astype(jnp.bfloat16)
    grad_probs = jnp.einsum(
        "clhd,cmhd->chlm", grad_mixed_low, values_heads, preferred_element_type=jnp.float32
    )
    weighted = jnp.sum(probs * grad_probs, axis=-1, keepdims=True)
    grad_scores_low = (probs * (grad_probs - weighted)).astype(jnp.bfloat16)
    grad_query_low = (
        jnp.einsum(
            "chlm,cmhd->clhd", grad_scores_low, keys_heads, preferred_element_type=jnp.float32
        )
        * factor
    ).astype(jnp.bfloat16)
    grad_keys_low = (
        jnp.einsum(
            "chlm,clhd->cmhd", grad_scores_low, query_heads, preferred_element_type=jnp.float32
        )
        * factor
    ).astype(jnp.bfloat16)
    grad_query_low = grad_query_low.reshape(captions, length, width)
    grad_keys_low = grad_keys_low.reshape(captions, length, width)
    grad_values_low = grad_values_low.reshape(captions, length, width)
    querymat_grad = outer_sum(normed_low, grad_query_low)
    querybias_grad = token_sum(grad_query_low)
    keymat_grad = outer_sum(normed_low, grad_keys_low)
    valuemat_grad = outer_sum(normed_low, grad_values_low)
    valuebias_grad = token_sum(grad_values_low)
    grad_normed = (
        project_back(grad_query_low, query_w)
        + project_back(grad_keys_low, keys_w)
        + project_back(grad_values_low, values_w)
    )
    first_pull = jax.vjp(layer_norm, source, gain_one, shift_one)[1]
    grad_ln_one, attgain_grad, attshift_grad = first_pull(grad_normed)
    input_grad = grad_middle + grad_ln_one
    (
        attgain_grad,
        attshift_grad,
        querymat_grad,
        querybias_grad,
        keymat_grad,
        valuemat_grad,
        valuebias_grad,
        mixmat_grad,
        mixbias_grad,
    ) = (
        lax.psum_scatter(attgain_grad, ("dp", "fsdp"), scatter_dimension=0, tiled=True),
        lax.psum_scatter(attshift_grad, ("dp", "fsdp"), scatter_dimension=0, tiled=True),
        lax.psum_scatter(querymat_grad, ("dp", "fsdp"), scatter_dimension=1, tiled=True),
        lax.psum_scatter(querybias_grad, ("dp", "fsdp"), scatter_dimension=0, tiled=True),
        lax.psum_scatter(keymat_grad, ("dp", "fsdp"), scatter_dimension=1, tiled=True),
        lax.psum_scatter(valuemat_grad, ("dp", "fsdp"), scatter_dimension=1, tiled=True),
        lax.psum_scatter(valuebias_grad, ("dp", "fsdp"), scatter_dimension=0, tiled=True),
        lax.psum_scatter(mixmat_grad, ("dp", "fsdp"), scatter_dimension=1, tiled=True),
        lax.psum_scatter(mixbias_grad, ("dp", "fsdp"), scatter_dimension=0, tiled=True),
    )
    return (
        block_out,
        input_grad,
        attgain_grad,
        attshift_grad,
        querymat_grad,
        querybias_grad,
        keymat_grad,
        valuemat_grad,
        valuebias_grad,
        mixmat_grad,
        mixbias_grad,
        mlpgain_grad,
        mlpshift_grad,
        upmat_grad,
        upbias_grad,
        downmat_grad,
        downbias_grad,
    )


NT = (((1,), (1,)), ((), ()))
NN = (((1,), (0,)), ((), ()))
TN = (((0,), (0,)), ((), ()))
F32 = jnp.float32
BF16 = jnp.bfloat16
AXES = ("z", "x", "y", "c")
QUAD = 4
VMEM_LIMIT = 56 * 1024 * 1024


def dot(left, right, dims):
    return lax.dot_general(left, right, dims, preferred_element_type=F32)


class Grid3:
    def __init__(self, dp, fsdp):
        self.c = 2
        self.y = fsdp // 2
        self.x = self.y
        self.z = dp // self.x
        self.count = dp * fsdp

    def index(self, z, x, y, c):
        return ((z * self.x + x) * self.y + y) * self.c + c

    def shift(self, values, kz=0, kx=0, ky=0, kc=0):
        pairs = []
        for z in range(self.z):
            for x in range(self.x):
                for y in range(self.y):
                    for c in range(self.c):
                        pairs.append((self.index(z, x, y, c), self.index(z ^ kz, x ^ kx, y ^ ky, c ^ kc)))
        return lax.ppermute(values, AXES, pairs)

    def here(self):
        return tuple(lax.axis_index(name) for name in AXES)

    def me(self):
        return self.index(*self.here())

    def away(self, *bits):
        return self.index(*(lax.bitwise_xor(at, jnp.int32(bit)) for at, bit in zip(self.here(), bits)))


def tie(values, gate):
    return lax.optimization_barrier((values, gate))[0]


def together(values):
    return lax.optimization_barrier(values)


COLUMN = (0, 3, 1, 2)


def gather_one(grid, first, second):
    return first, second, grid.shift(first, kx=1), grid.shift(second, ky=1)


def gather_two(grid, four):
    first, second, first_x, second_y = four
    one = jnp.concatenate([first, first_x])
    two = jnp.concatenate([second, second_y])
    return one, two, grid.shift(one, ky=1), grid.shift(two, kx=1)


def gather_core(grid, arrays):
    return tuple(grid.shift(array, kc=1) for array in arrays)


def gather_places():
    first, second = COLUMN[:2], COLUMN[2:]
    one = [(z, x, 0) for x in range(2) for z in first]
    two = [(z, 0, y) for y in range(2) for z in second]
    one_y = [(z, x, 1) for z, x, _ in one]
    two_x = [(z, 1, y) for z, _, y in two]
    return [[spot + (core,) for spot in group] for core, pair in ((0, 0), (0, 1), (1, 0), (1, 1)) for group in ((one, two), (one_y, two_x))[pair]]


def place(grid, places, refs, held):
    for ref, spots in zip(refs, places):
        for slot, spot in enumerate(spots):
            held[grid.away(*spot)] = ref[slot]


def outgoing(grid, core):
    half = grid.z // 2
    slots = []
    for which in range(2):
        for one in range(2):
            for two in range(2):
                for low in range(half):
                    kx, ky = (one, two) if which == 0 else (two, one)
                    slots.append((COLUMN[which * half + low], kx, ky, core))
    return slots


def plus(left, right):
    return (left.astype(F32) + right.astype(F32)).astype(BF16)


def scatter_core(grid, other):
    return grid.shift(other, kc=1)


def join(values, extra):
    values = values.reshape(-1, 8, values.shape[-1])
    return values if extra is None else jnp.concatenate([values, extra])


def part(values, shape):
    count = math.prod(shape[:-1]) // 8
    return values[:count].reshape(shape), values[count:]


def scatter_first(grid, own, arrived, extra=None):
    shape = (2, 2, 2, grid.z // 2) + own.shape[1:]
    own = own.reshape(shape)
    arrived = arrived.reshape(shape)
    send_a = plus(own[0, 1], arrived[0, 1])
    send_b = plus(own[1, 1], arrived[1, 1])
    keep_a = plus(own[0, 0], arrived[0, 0])
    keep_b = plus(own[1, 0], arrived[1, 0])
    if extra is not None:
        send_a = join(send_a, extra.astype(BF16))
    return keep_a, keep_b, grid.shift(send_a, kx=1), grid.shift(send_b, ky=1), extra, (send_a, send_b)


def scatter_second(grid, state, gate):
    keep_a, keep_b, got_a, got_b, extra, _ = state
    got_a, got_b = tie((got_a, got_b), gate)
    if extra is not None:
        got_a, more = part(got_a, keep_a.shape)
        extra = extra + more.astype(F32)
    next_a = plus(keep_a[1], got_a[1])
    next_b = plus(keep_b[1], got_b[1])
    rest_a = plus(keep_a[0], got_a[0])
    rest_b = plus(keep_b[0], got_b[0])
    if extra is not None:
        next_a = join(next_a, extra.astype(BF16))
    return rest_a, rest_b, grid.shift(next_a, ky=1), grid.shift(next_b, kx=1), extra, (next_a, next_b)


def scatter_third(grid, state, gate):
    rest_a, rest_b, last_a, last_b, extra, _ = state
    last_a, last_b = tie((last_a, last_b), gate)
    if extra is not None:
        last_a, more = part(last_a, rest_a.shape)
        extra = extra + more.astype(F32)
    half = grid.z // 2
    parts = [plus(rest_a[k], last_a[k]) for k in range(half)] + [plus(rest_b[k], last_b[k]) for k in range(half)]
    sends = parts[1:]
    if extra is not None:
        sends = [join(send, extra.astype(BF16)) for send in sends]
    return parts[0], [grid.shift(send, kz=k) for send, k in zip(sends, COLUMN[1:])], extra, sends


def scatter_near(grid, state, gate):
    rest_a, rest_b, last_a, last_b, _, _ = state
    last_a, last_b = tie((last_a, last_b), gate)
    send = plus(rest_b, last_b)
    return plus(rest_a, last_a), grid.shift(send, kz=1), send


def scatter_far(grid, state, gate):
    keep, got, _ = state
    got = tie(got, gate)
    send = plus(keep[1], got[1])
    return keep[0].astype(F32) + got[0].astype(F32), grid.shift(send, kz=3), send


def scatter_end(state, gate):
    total, got, _ = state
    return total + tie(got, gate).astype(F32)


def scatter_last(state, gate):
    total, came, extra, _ = state
    shape = total.shape
    came = tie(came, gate)
    total = total.astype(F32)
    for values in came:
        if extra is not None:
            values, more = part(values, shape)
            extra = extra + more.astype(F32)
        total = total + values.astype(F32)
    return total if extra is None else (total, extra)


def lanes_of(rows):
    return lax.broadcasted_iota(jnp.int32, (rows, 256), 1) // 64


def spread(block):
    head = lanes_of(block.shape[0])
    zero = jnp.zeros_like(block)
    return jnp.concatenate([jnp.where(head == g, block, zero) for g in range(QUAD)], axis=0)


def collect(square):
    head = lanes_of(64)
    total = jnp.where(head == 0, square[0:64], 0.0)
    for g in range(1, QUAD):
        total = jnp.where(head == g, square[64 * g : 64 * g + 64], total)
    return total


def normal(values):
    centre = jnp.mean(values, axis=-1, keepdims=True)
    centred = values - centre
    spread_of = jnp.mean(centred * centred, axis=-1, keepdims=True)
    scale = lax.rsqrt(spread_of + 1e-06)
    return centred * scale, scale


def normal_back(hat, scale, gain, grads):
    weighted = grads * gain
    middle = jnp.mean(weighted, axis=-1, keepdims=True)
    along = jnp.mean(weighted * hat, axis=-1, keepdims=True)
    return scale * (weighted - middle - hat * along)


TILE = 16
SIZES = (384, 512, 640, 768, 896, 1024)


def order_of(lengths, length):
    captions = lengths.shape[0]
    tiles = length // TILE
    real = (lengths + (TILE - 1)) // TILE
    before = jnp.tril(jnp.ones((captions, captions), jnp.int32), -1)
    start = jnp.sum(before * real[None, :], axis=1)
    total = jnp.sum(real)
    late = total + jnp.sum(before * (tiles - real)[None, :], axis=1)
    at = jnp.arange(tiles, dtype=jnp.int32)[None, :]
    spots = jnp.where(at < real[:, None], start[:, None] + at, late[:, None] + at - real[:, None])
    sizes = jnp.array(SIZES, jnp.int32)
    size = jnp.min(jnp.where(sizes >= total * TILE, sizes, SIZES[-1]))
    return jnp.concatenate([spots.reshape(-1), start, jnp.stack([size, total])]).astype(jnp.int32)


def tile_rows(place_ref, index):
    return pl.ds(pl.multiple_of(place_ref[index] * TILE, TILE), TILE)


def by_size(size, body):
    for rows in SIZES:
        pl.when(size == rows)(functools.partial(body, rows))


def rows_at(step, rows):
    return pl.ds(pl.multiple_of(step * rows, rows), rows)


def pack_kernel(grid, small_ref, q_ref, k_ref, v_ref, out_ref, wide, sems):
    copies = [
        pltpu.make_async_copy(ref, out_ref.at[3 * at : 3 * at + 3], sems.at[at])
        for at, ref in enumerate((q_ref, k_ref, v_ref))
    ]
    for copy in copies:
        copy.start()
    share = small_ref.shape[1]
    wide[...] = jnp.zeros_like(wide)
    wide[:, 0:share] = small_ref[...].astype(F32)
    out_ref[9] = pltpu.roll(wide[...], grid.me() * share, 1).astype(BF16)
    for copy in copies:
        copy.wait()


def pack_up_kernel(grid, small_ref, out_ref, wide):
    width = wide.shape[1]
    wide[...] = jnp.zeros_like(wide)
    wide[0:1, 0 : small_ref.shape[1]] = small_ref[...]
    me = grid.me()
    four = pltpu.roll(wide[...], lax.rem(me, 8) * small_ref.shape[1], 1)
    row = lax.broadcasted_iota(jnp.int32, (8, width), 0)
    four = jnp.where(row == lax.div(me, 8), jnp.broadcast_to(four[0:1], (8, width)), 0.0)
    out_ref[0] = four.astype(BF16)


def project_kernel(grid, places, place_ref, hidden_ref, *rest):
    count = len(places)
    refs, rest = rest[:count], rest[count:]
    moved_ref, normed_out, q_ref, k_ref, v_ref, vec_ref, held = rest
    total = jnp.zeros(vec_ref.shape, F32)
    for ref, spots in zip(refs, places):
        for slot, spot in enumerate(spots):
            total = total + ref[slot, 9].astype(F32)
            held[grid.away(*spot)] = ref[slot, 0:9]
    vec_ref[...] = total
    width = hidden_ref.shape[1]
    rows = 256

    def block(step, carry):
        at = rows_at(step, rows)
        hidden = hidden_ref[at, :]
        hat, _ = normal(hidden.astype(F32))
        normed = (hat * vec_ref[0:1, :] + vec_ref[1:2, :]).astype(BF16)
        q_ref[at, :] = (dot(normed, held[:, 0 : 3].reshape(width, width), NT) + vec_ref[2:3, :]).astype(BF16)
        k_ref[at, :] = dot(normed, held[:, 3 : 6].reshape(width, width), NT).astype(BF16)
        v_ref[at, :] = (dot(normed, held[:, 6 : 9].reshape(width, width), NT) + vec_ref[3:4, :]).astype(BF16)
        for t in range(rows // TILE):
            to = tile_rows(place_ref, step * (rows // TILE) + t)
            part = slice(t * TILE, (t + 1) * TILE)
            normed_out[to, :] = normed[part, :]
            moved_ref[to, :] = hidden[part, :]
        return carry

    lax.fori_loop(0, hidden_ref.shape[0] // rows, block, 0)


def attend_kernel(length, group, lengths_ref, place_ref, q_ref, k_ref, v_ref, probs_ref, mixed_out):
    width = q_ref.shape[1]
    captions = q_ref.shape[0] // length
    tiles = length // TILE
    quads = width // 256
    position = lax.broadcasted_iota(jnp.int32, (length, 256), 0)

    def several(step, carry):
        items = [
            (step * group + g, quad, rows_at(step * group + g, length), slice(256 * quad, 256 * quad + 256))
            for g in range(group)
            for quad in range(quads)
        ]
        scores = [dot(k_ref[rows, lanes], spread(q_ref[rows, lanes]), NT) for _, _, rows, lanes in items]
        probs = []
        for (cap, _, _, _), score in zip(items, scores):
            score = jnp.where(position < lengths_ref[cap], score * 0.125, -1e30)
            raised = jnp.exp(score - jnp.max(score, axis=0, keepdims=True))
            probs.append((raised * (1.0 / jnp.sum(raised, axis=0, keepdims=True))).astype(BF16))
        for (cap, quad, _, _), prob in zip(items, probs):
            probs_ref[cap * quads + quad] = prob
        mixed = [
            collect(dot(prob, v_ref[rows, lanes], TN)).astype(BF16)
            for (_, _, rows, lanes), prob in zip(items, probs)
        ]
        for (cap, _, _, lanes), value in zip(items, mixed):
            for t in range(tiles):
                to = tile_rows(place_ref, cap * tiles + t)
                mixed_out[to, lanes] = value[t * TILE : (t + 1) * TILE, :]
        return carry

    lax.fori_loop(0, captions // group, several, 0)


def bend_parts(grid, parts, normed, bias_ref, held, at, active_ref, slope_ref):
    width = normed.shape[1]
    per = grid.count // 4
    root = math.sqrt(2.0 / math.pi)
    for part in parts:
        weight = held[per * part : per * part + per, 3:15].reshape(width, width)
        upper = dot(normed, weight, NT) + bias_ref[part : part + 1, :]
        square = upper * upper
        bend = jnp.tanh(upper * (root + (root * 0.044715) * square))
        half = 0.5 * bend + 0.5
        span = slice(width * part, width * part + width)
        active = upper * half
        active_ref[at, span] = active.astype(BF16)
        slope = half + active * ((1.0 - bend) * (root + (3.0 * root * 0.044715) * square))
        slope_ref[at, span] = slope.astype(BF16)


def upper_kernel(grid, places, moved_ref, mixed_ref, vec_ref, *rest):
    count = len(places)
    refs, rest = rest[:count], rest[count:]
    middle_ref, normed_ref, active_ref, slope_ref, bias_ref, held = rest
    place(grid, places, refs, held)
    bias = jnp.zeros(bias_ref.shape, F32)
    for ref, spots in zip(refs, places):
        for slot in range(len(spots)):
            bias = bias + ref[slot, 15].astype(F32)
    bias_ref[...] = bias
    width = moved_ref.shape[1]
    rows = 256

    def block(step, carry):
        at = rows_at(step, rows)
        middle = (
            moved_ref[at, :].astype(F32)
            + dot(mixed_ref[at, :], held[:, 0:3].reshape(width, width), NT)
            + vec_ref[4:5, :]
        )
        middle_ref[at, :] = middle
        hat, _ = normal(middle)
        normed = (hat * vec_ref[5:6, :] + vec_ref[6:7, :]).astype(BF16)
        normed_ref[at, :] = normed
        bend_parts(grid, (0, 1, 2, 3), normed, bias_ref, held, at, active_ref, slope_ref)
        return carry

    lax.fori_loop(0, moved_ref.shape[0] // rows, block, 0)


def down_grad_kernel(grid, length, size_at, lengths_ref, place_ref, cot_ref, active_ref, low_ref, vec_ref, own_ref, other_ref, far_ref, total, sem):
    keep = pltpu.make_async_copy(active_ref, far_ref.at[0 : active_ref.shape[0]], sem)
    keep.start()
    width = cot_ref.shape[1]
    captions = cot_ref.shape[0] // length
    tiles = length // TILE
    position = lax.broadcasted_iota(jnp.int32, (length, 1), 0)
    vec_ref[...] = jnp.zeros_like(vec_ref)

    def caption(cap, carry):
        part = cot_ref[rows_at(cap, length), :].astype(F32)
        part = jnp.where(position < lengths_ref[cap], part, 0.0)
        vec_ref[0:1, :] += jnp.sum(part, axis=0, keepdims=True)
        part = part.astype(BF16)
        for t in range(tiles):
            low_ref[tile_rows(place_ref, cap * tiles + t), :] = part[t * TILE : (t + 1) * TILE, :]
        return carry

    lax.fori_loop(0, captions, caption, 0)
    share = width // grid.count

    def column(step, carry):
        lanes = rows_at(step, width)

        def product(rows):
            total[...] = dot(low_ref[0:rows, :], active_ref[0:rows, lanes], TN)

        by_size(place_ref[size_at], product)
        for core, out_ref in ((0, own_ref), (1, other_ref)):
            for slot, spot in enumerate(outgoing(grid, core)):
                at = pl.multiple_of(grid.away(*spot) * share, 8)
                out_ref[slot, :, lanes] = total[pl.ds(at, share), :].astype(BF16)
        return carry

    lax.fori_loop(0, active_ref.shape[1] // width, column, 0)
    keep.wait()


def upper_grad_kernel(grid, places, size_at, place_ref, low_ref, slope_ref, normed_ref, *rest):
    count = len(places)
    refs, rest = rest[:count], rest[count:]
    upper_ref, vec_ref, own_ref, other_ref, far_ref, held, total, sem = rest
    place(grid, places, refs, held)
    keep = pltpu.make_async_copy(held, far_ref.at[0 : grid.count], sem)
    keep.start()
    width = low_ref.shape[1]
    per = grid.count // 4
    share = width // per
    half = grid.z // 2
    z, x, y, c = grid.here()
    shape = own_ref.shape[1:]
    mine = jnp.where(c == 0, 0, share)

    def column(step, carry):
        lanes = rows_at(step, width)

        def product(rows):
            grads = dot(low_ref[0:rows, :], held[:, :, lanes].reshape(width, width), NN) * slope_ref[0:rows, lanes].astype(F32)
            vec_ref[rows_at(step, 8), :] = jnp.broadcast_to(jnp.sum(grads, axis=0, keepdims=True), (8, width))
            grads = grads.astype(BF16)
            upper_ref[0:rows, lanes] = grads
            total[...] = dot(grads, normed_ref[0:rows, :], TN)

        by_size(place_ref[size_at], product)
        for k in range(per // 2):
            chip = step * (per // 2) + k
            kz = lax.bitwise_xor(lax.div(chip, grid.x * grid.y), z)
            kx = lax.bitwise_xor(lax.rem(lax.div(chip, grid.y), grid.x), x)
            ky = lax.bitwise_xor(lax.rem(chip, grid.y), y)
            low = lax.div(kz, 2)
            which = lax.bitwise_xor(low, lax.rem(kz, 2))
            one = jnp.where(which == 0, kx, ky)
            two = jnp.where(which == 0, ky, kx)
            slot = ((which * 2 + one) * 2 + two) * half + low
            own_at = pl.multiple_of(2 * share * k + mine, 8)
            other_at = pl.multiple_of(2 * share * k + (share - mine), 8)
            own_ref[slot] = total[pl.ds(own_at, share), :].astype(BF16).reshape(shape)
            other_ref[slot] = total[pl.ds(other_at, share), :].astype(BF16).reshape(shape)
        return carry

    lax.fori_loop(0, upper_ref.shape[1] // width, column, 0)
    keep.wait()


def middle_grad_kernel(grid, size_at, place_ref, upper_ref, middle_ref, low_ref, vec_in, held, grad_ref, branch_ref, dm_ref, vec_ref):
    width = middle_ref.shape[1]
    per = grid.count // 4
    rows = 128
    vec_ref[...] = jnp.zeros_like(vec_ref)

    def block(step, carry):
        at = rows_at(step, rows)
        grads = dot(upper_ref[at, 0:width], held[0:per, 3:15].reshape(width, width), NN)
        for part in range(1, 4):
            weight = held[per * part : per * part + per, 3:15].reshape(width, width)
            grads = grads + dot(upper_ref[at, width * part : width * part + width], weight, NN)
        hat, scale = normal(middle_ref[at, :])
        grad_middle = low_ref[at, :].astype(F32) + normal_back(hat, scale, vec_in[5:6, :], grads)
        grad_ref[at, :] = grad_middle
        branch = grad_middle.astype(BF16)
        branch_ref[at, :] = branch
        dm_ref[at, :] = dot(branch, held[:, 0:3].reshape(width, width), NN).astype(BF16)
        vec_ref[0:1, :] += jnp.sum(grads * hat, axis=0, keepdims=True)
        vec_ref[1:2, :] += jnp.sum(grads, axis=0, keepdims=True)
        vec_ref[2:3, :] += jnp.sum(grad_middle, axis=0, keepdims=True)
        return carry

    lax.fori_loop(0, lax.div(place_ref[size_at], rows), block, 0)


def attend_grad_kernel(length, group, lengths_ref, place_ref, dm_ref, q_ref, k_ref, v_ref, probs_ref, grads_ref, vec_ref):
    width = dm_ref.shape[1]
    quads = width // 256
    tiles = length // TILE
    captions = probs_ref.shape[0] // quads
    starts = captions * tiles
    end = place_ref[starts + captions + 1]
    clear = pl.ds(pl.multiple_of(end * TILE, TILE), 256)
    for which in range(3):
        grads_ref[which, clear, :] = jnp.zeros((256, width), BF16)
    vec_ref[...] = jnp.zeros_like(vec_ref)
    row = lax.broadcasted_iota(jnp.int32, (length, 1), 0)

    def several(step, carry):
        items = []
        for g in range(group):
            cap = step * group + g
            packed = pl.ds(pl.multiple_of(place_ref[starts + cap] * TILE, TILE), length)
            plain = pl.ds(pl.multiple_of(cap * length, length), length)
            for quad in range(quads):
                items.append((cap, quad, packed, plain, slice(256 * quad, 256 * quad + 256)))
        probs = [probs_ref[cap * quads + quad] for cap, quad, _, _, _ in items]
        wide = []
        for cap, _, packed, _, lanes in items:
            dm = dm_ref[packed, lanes]
            wide.append(spread(jnp.where(row < lengths_ref[cap], dm, jnp.zeros_like(dm))))
        grad_probs = [dot(v_ref[plain, lanes], w, NT) for (_, _, _, plain, lanes), w in zip(items, wide)]
        grad_values = [dot(p, w, NN) for p, w in zip(probs, wide)]
        grad_scores = []
        for p, grad in zip(probs, grad_probs):
            p = p.astype(F32)
            along = p * grad
            grad_scores.append((along - p * jnp.sum(along, axis=0, keepdims=True)).astype(BF16))
        grad_keys = [
            dot(g, spread(q_ref[plain, lanes]), NN) * 0.125 for (_, _, _, plain, lanes), g in zip(items, grad_scores)
        ]
        grad_query = [
            collect(dot(g, k_ref[plain, lanes], TN)) * 0.125 for (_, _, _, plain, lanes), g in zip(items, grad_scores)
        ]
        for at, (_, _, packed, _, lanes) in enumerate(items):
            grads_ref[0, packed, lanes] = grad_query[at].astype(BF16)
            grads_ref[1, packed, lanes] = grad_keys[at].astype(BF16)
            grads_ref[2, packed, lanes] = grad_values[at].astype(BF16)
        for quad in range(quads):
            lanes = slice(256 * quad, 256 * quad + 256)
            vec_ref[0:1, lanes] += sum(jnp.sum(v, axis=0, keepdims=True) for v in grad_query[quad::quads])
            vec_ref[1:2, lanes] += sum(jnp.sum(v, axis=0, keepdims=True) for v in grad_values[quad::quads])
        return carry

    lax.fori_loop(0, captions // group, several, 0)


def weight_grad_kernel(grid, size_at, place_ref, grads_ref, branch_ref, normed_ref, mixed_ref, own_ref, other_ref, total):
    share = total.shape[0] // grid.count

    def send(at):
        for core, out_ref in ((0, own_ref), (1, other_ref)):
            for slot, spot in enumerate(outgoing(grid, core)):
                start = pl.multiple_of(grid.away(*spot) * share, 8)
                out_ref[slot, at] = total[pl.ds(start, share), :].astype(BF16)

    def matrix(at, carry):
        def product(rows):
            total[...] = dot(grads_ref[at, 0:rows, :], normed_ref[0:rows, :], TN)

        by_size(place_ref[size_at], product)
        send(at)
        return carry

    lax.fori_loop(0, 3, matrix, 0)

    def product(rows):
        total[...] = dot(branch_ref[0:rows, :], mixed_ref[0:rows, :], TN)

    by_size(place_ref[size_at], product)
    send(3)


def input_grad_kernel(grid, size_at, place_ref, moved_ref, grad_ref, grads_ref, vec_in, down_vec, up_vec, mid_vec, att_vec, held, out_ref, vec_ref, found):
    rows = 128
    width = moved_ref.shape[1]
    vec_ref[...] = jnp.zeros_like(vec_ref)
    vec_ref[2:4, :] = att_vec[0:2, :]
    vec_ref[4:5, :] = mid_vec[2:3, :]
    vec_ref[5:7, :] = mid_vec[0:2, :]
    vec_ref[7:8, :] = down_vec[0:1, :]
    for part in range(4):
        vec_ref[8 + part : 9 + part, :] = up_vec[8 * part : 8 * part + 1, :]

    def block(step, carry):
        at = rows_at(step, rows)
        grads = dot(grads_ref[0, at, :], held[:, 0 : 3].reshape(width, width), NN)
        grads = grads + dot(grads_ref[1, at, :], held[:, 3 : 6].reshape(width, width), NN)
        grads = grads + dot(grads_ref[2, at, :], held[:, 6 : 9].reshape(width, width), NN)
        hat, scale = normal(moved_ref[at, :].astype(F32))
        found[at, :] = grad_ref[at, :] + normal_back(hat, scale, vec_in[0:1, :], grads)
        vec_ref[0:1, :] += jnp.sum(grads * hat, axis=0, keepdims=True)
        vec_ref[1:2, :] += jnp.sum(grads, axis=0, keepdims=True)
        return carry

    lax.fori_loop(0, lax.div(place_ref[size_at], rows), block, 0)
    total = place_ref[size_at + 1]

    def tile(index, carry):
        values = found[tile_rows(place_ref, index), :]
        out_ref[rows_at(index, TILE), :] = jnp.where(place_ref[index] < total, values, 0.0)
        return carry

    lax.fori_loop(0, out_ref.shape[0] // TILE, tile, 0)


def lower_kernel(place_ref, active_far, middle_ref, vec_in, weight_far, out_ref, weight, active, found, sems):
    count, rows = active.shape[0], active.shape[1]

    def fetch(step):
        return pltpu.make_async_copy(active_far.at[rows_at(step, rows), :], active.at[step], sems.at[step])

    load = pltpu.make_async_copy(weight_far.at[0 : weight.shape[0]], weight, sems.at[count])
    load.start()
    fetch(0).start()
    load.wait()

    def block(step, carry):
        @pl.when(step + 1 < count)
        def _():
            fetch(step + 1).start()

        fetch(step).wait()
        at = rows_at(step, rows)
        out = middle_ref[at, :] + dot(active[step], weight[...].reshape(middle_ref.shape[1], active.shape[2]), NT) + vec_in[7:8, :]
        found[at, :] = out.astype(BF16)
        return carry

    lax.fori_loop(0, count, block, 0)

    def tile(index, carry):
        out_ref[rows_at(index, TILE), :] = found[tile_rows(place_ref, index), :]
        return carry

    lax.fori_loop(0, out_ref.shape[0] // TILE, tile, 0)


def unpack_kernel(grid, vec_ref, *outs):
    me = grid.me()
    eight = pltpu.roll(vec_ref[0:8, :], lax.rem(768 - me * 24, 768), 1)
    for k in range(8):
        outs[k][...] = eight[k : k + 1, 0:24]
    row = lax.broadcasted_iota(jnp.int32, (8, 768), 0)
    four = jnp.sum(jnp.where(row == lax.div(me, 8), vec_ref[8:16, :], 0.0), axis=0, keepdims=True)
    four = jnp.broadcast_to(four, (8, 768))
    four = pltpu.roll(four, lax.rem(768 - lax.rem(me, 8) * 96, 768), 1)
    outs[8][...] = four[0:1, 0:96]


def whole(shape):
    return pl.BlockSpec(shape, lambda *_: (0,) * len(shape))


ANY = pl.BlockSpec(memory_space=pl.ANY)
SMEM = pl.BlockSpec(memory_space=pltpu.SMEM)


FAST = pl.BlockSpec(memory_space=pltpu.VMEM)
FAR = pl.BlockSpec(memory_space=pltpu.HBM)
LARGE = 1 << 26


def call(kernel, steps, in_specs, out_specs, outs, scratch, flops, moved, name, limit=8):
    return pl.pallas_call(
        kernel,
        grid=(steps,),
        in_specs=in_specs,
        out_specs=out_specs,
        out_shape=[jax.ShapeDtypeStruct(s, d) for s, d in outs],
        scratch_shapes=scratch,
        compiler_params=pltpu.CompilerParams(vmem_limit_bytes=limit * 1024 * 1024),
        cost_estimate=pl.CostEstimate(flops=flops, bytes_accessed=moved, transcendentals=0),
        name=name,
    )


def call_near(kernel, in_specs, outs, scratch, flops, name, limit=8, aliases=None, far=0):
    return pl.pallas_call(
        kernel,
        in_specs=in_specs,
        out_specs=[FAST] * (len(outs) - far) + [FAR] * far,
        input_output_aliases=aliases or {},
        out_shape=[jax.ShapeDtypeStruct(s, d) for s, d in outs],
        scratch_shapes=scratch,
        compiler_params=pltpu.CompilerParams(vmem_limit_bytes=limit * 1024 * 1024),
        cost_estimate=pl.CostEstimate(flops=flops, bytes_accessed=1_000_000, transcendentals=0),
        name=name,
    )


def fast_device(
    grid,
    hidden,
    lengths,
    cotangent,
    attgain,
    attshift,
    querymat,
    querybias,
    keymat,
    valuemat,
    valuebias,
    mixmat,
    mixbias,
    mlpgain,
    mlpshift,
    upmat_w,
    upbias,
    downmat,
    downbias,
):
    captions, length, width = hidden.shape
    tokens = captions * length
    hidden2 = hidden.reshape(tokens, width)
    cot2 = cotangent.reshape(tokens, width)
    share = width // grid.count
    ff = downmat.shape[0]
    small = jnp.stack([attgain, attshift, querybias, valuebias, mixbias, mlpgain, mlpshift, downbias])
    units = share // 8
    (first,) = pl.pallas_call(
        functools.partial(pack_kernel, grid),
        in_specs=[FAST] + [FAR] * 3,
        out_specs=[FAST],
        out_shape=[jax.ShapeDtypeStruct((3 * units + 1, 8, width), BF16)],
        scratch_shapes=[pltpu.VMEM((8, width), F32), pltpu.SemaphoreType.DMA((3,))],
        name="pack",
    )(small, *(w.T.reshape(units, 8, width) for w in (querymat, keymat, valuemat)))
    (up_bias,) = call_near(
        functools.partial(pack_up_kernel, grid),
        [FAST],
        [((1, 8, width), BF16)],
        [pltpu.VMEM((8, width), F32)],
        1000,
        "pack_up",
    )(upbias.astype(F32).reshape(1, -1))
    second = jnp.concatenate(
        [mixmat.T.reshape(units, 8, width), upmat_w.T.reshape(4 * units, 8, width), up_bias], axis=0
    )
    third = downmat.T
    where = order_of(lengths, length)
    size_at = captions * (length // TILE) + captions
    places = gather_places()
    first_a = jnp.stack([first, grid.shift(first, kz=3)])
    first_z = grid.shift(first_a, kz=1)
    first_a, first_z, second = together((first_a, first_z, second))
    first_a = gather_one(grid, first_a, first_z)
    second_a = jnp.stack([second, grid.shift(second, kz=3)])
    first_a, second_a, where = together((first_a, second_a, where))
    first_b = gather_two(grid, first_a)
    first_c = gather_core(grid, first_b[:2])
    second_z = grid.shift(second_a, kz=1)
    first_b, first_c, second_z, third = together((first_b, first_c, second_z, third))
    first_in = first_b + first_c + gather_core(grid, first_b[2:])
    second_a = gather_one(grid, second_a, second_z)
    third_z = grid.shift(third, kz=3)
    half = grid.count // 2
    unit = 2 * tokens * width * width
    row = (tokens, width)
    heads = captions * (width // 256)
    tall = (tokens + 64, width)
    square = pltpu.VMEM((width, width), F32)
    moved, normed, query, keys, values, vec, held_one = call_near(
        functools.partial(project_kernel, grid, places),
        [SMEM] + [FAST] * (1 + len(first_in)),
        [(row, BF16)] * 5 + [((8, width), F32), ((grid.count, 3 * units, 8, width), BF16)],
        [],
        5 * unit,
        "project",
    )(where, hidden2, *first_in)
    second_a, third_z, query = together((second_a, third_z, query))
    third_a = jnp.stack([third, third_z])
    third_z = grid.shift(third_a, kz=1)
    second_b = gather_two(grid, second_a)
    second_c = gather_core(grid, second_b[:2])
    probs, mixed = call_near(
        functools.partial(attend_kernel, length, 4),
        [SMEM] * 2 + [FAST] * 3,
        [((heads, length, 256), BF16), (row, BF16)],
        [],
        5 * unit,
        "attend",
    )(lengths, where, query, keys, values)
    second_c, third_z, mixed = together((second_c, third_z, mixed))
    third_a = gather_one(grid, third_a, third_z)
    second_b, third_a = together((second_b, third_a))
    second_in = second_b + second_c + gather_core(grid, second_b[2:])
    middle, normed2, active, slope, bias, held_two = call_near(
        functools.partial(upper_kernel, grid, places),
        [FAST] * (3 + len(second_in)),
        [(row, F32), (row, BF16), ((tokens, ff), BF16), ((tokens, ff), BF16), ((8, width), F32)]
        + [((grid.count,) + second.shape, BF16)],
        [],
        9 * unit,
        "upper",
    )(moved, mixed, vec, *second_in)
    third_b = gather_two(grid, third_a)
    third_c = gather_core(grid, third_b[:2])
    low, down_vec, down_own, down_other, active_far = call_near(
        functools.partial(down_grad_kernel, grid, length, size_at),
        [SMEM] * 2 + [FAST] * 2,
        [(row, BF16), ((8, width), F32)] + [((half, share, ff), BF16)] * 2 + [((LARGE // (2 * ff), ff), BF16)],
        [square, pltpu.SemaphoreType.DMA],
        5 * unit,
        "down_grad",
        far=1,
    )(lengths, where, cot2, active)
    third_b, third_c, down_own, down_other = together((third_b, third_c, down_own, down_other))
    third_in = third_b + third_c + gather_core(grid, third_b[2:])
    down_two = scatter_first(grid, down_own, scatter_core(grid, down_other))
    low = tie(low, down_two[-1])
    grad_upper, up_vec, up_own, up_other, lower_w = call_near(
        functools.partial(upper_grad_kernel, grid, places, size_at),
        [SMEM] + [FAST] * (3 + len(third_in)),
        [((tokens, ff), BF16), ((32, width), F32)]
        + [((half, 4, share, width), BF16)] * 2
        + [((LARGE // (2 * share * ff), share, ff), BF16)],
        [pltpu.VMEM((grid.count, share, ff), BF16), square, pltpu.SemaphoreType.DMA],
        8 * unit,
        "upper_grad",
        limit=12,
        aliases={2: 0},
        far=1,
    )(where, low, slope, normed2, *third_in)
    down_two, up_vec, up_own, up_other = together((down_two, up_vec, up_own, up_other))
    down_three = scatter_second(grid, down_two, up_vec)
    up_one = scatter_core(grid, up_other)
    grad_upper = tie(grad_upper, down_three[-1])
    grad_middle, branch, dm, mid_vec = call_near(
        functools.partial(middle_grad_kernel, grid, size_at),
        [SMEM] + [FAST] * 5,
        [(row, F32), (row, BF16), (tall, BF16), ((8, width), F32)],
        [],
        6 * unit,
        "middle_grad",
    )(where, grad_upper, middle, low, vec, held_two)
    down_four = scatter_near(grid, down_three, mid_vec)
    up_two = scatter_first(grid, up_own, tie(up_one, mid_vec))
    dm = tie(dm, (up_two[-1], down_four[-1]))
    grads, att_vec = call_near(
        functools.partial(attend_grad_kernel, length, 4),
        [SMEM] * 2 + [FAST] * 5,
        [((3, tokens + 256, width), BF16), ((8, width), F32)],
        [],
        7 * unit,
        "attend_grad",
    )(lengths, where, dm, query, keys, values, probs)
    input_grad, all_vec = call_near(
        functools.partial(input_grad_kernel, grid, size_at),
        [SMEM] + [FAST] * 9,
        [(row, F32), ((16, width), F32)],
        [pltpu.VMEM(row, F32)],
        5 * unit,
        "input_grad",
    )(where, moved, grad_middle, grads, vec, down_vec, up_vec, mid_vec, att_vec, held_one)
    grads, all_vec = together((grads, all_vec))
    att_own, att_other = call_near(
        functools.partial(weight_grad_kernel, grid, size_at),
        [SMEM] + [FAST] * 4,
        [((half, 4, share, width), BF16)] * 2,
        [square],
        5 * unit,
        "weight_grad",
    )(where, grads, branch, normed, mixed)
    down_four, up_two, att_own, att_other, all_vec = together((down_four, up_two, att_own, att_other, all_vec))
    down_four = scatter_far(grid, down_four, all_vec)
    up_three = scatter_second(grid, up_two, all_vec)
    att_one = scatter_core(grid, att_other)
    all_vec = (all_vec + grid.shift(all_vec, kc=1)).reshape(2, 8, width)
    att_one = tie(att_one, up_three[-1])
    att_two = scatter_first(grid, att_own, att_one, all_vec)
    up_four = scatter_near(grid, up_three, att_two[-1])
    down_sum = scatter_end(down_four, att_two[-1])
    middle = tie(middle, (att_two[-1], up_four[-1]))
    (block_out,) = call_near(
        lower_kernel,
        [SMEM, FAR, FAST, FAST, FAR],
        [(row, BF16)],
        [
            pltpu.VMEM((grid.count, share, ff), BF16),
            pltpu.VMEM((4, tokens // 4, ff), BF16),
            pltpu.VMEM(row, BF16),
            pltpu.SemaphoreType.DMA((5,)),
        ],
        5 * unit,
        "lower",
        limit=20,
    )(where, active_far, middle, vec, lower_w)
    out_gate = block_out[0:8, 0:128]
    att_three = scatter_second(grid, att_two, out_gate)
    up_four = scatter_far(grid, up_four, att_three[-1])
    att_four = scatter_third(grid, att_three, up_four[-1])
    up_sum = scatter_end(up_four, att_four[-1])
    att_sum, all_vec = scatter_last(att_four, out_gate)
    all_vec = all_vec.reshape(16, width)
    vecs = call(
        functools.partial(unpack_kernel, grid),
        1,
        [whole((16, width))],
        [whole((1, share))] * 8 + [whole((1, ff // grid.count))],
        [((1, share), F32)] * 8 + [((1, ff // grid.count), F32)],
        [],
        1000,
        1000,
        "unpack",
    )(all_vec)
    vecs = [v.reshape(-1) for v in vecs]
    return (
        block_out.reshape(hidden.shape),
        input_grad.reshape(hidden.shape),
        vecs[0],
        vecs[1],
        att_sum[0].T,
        vecs[2],
        att_sum[1].T,
        att_sum[2].T,
        vecs[3],
        att_sum[3].T,
        vecs[4],
        vecs[5],
        vecs[6],
        up_sum.reshape(ff // grid.count, width).T,
        vecs[8],
        down_sum.T,
        vecs[7],
    )


def fits(mesh):
    return mesh.shape["dp"] == 8 and mesh.shape["fsdp"] == 4


def solution(mesh):
    axes = ("dp", "fsdp")
    body = per_device
    if fits(mesh):
        axes = AXES
        grid = Grid3(mesh.shape["dp"], mesh.shape["fsdp"])
        mesh = jax.sharding.Mesh(mesh.devices.reshape(grid.z, grid.x, grid.y, grid.c), AXES)
        body = functools.partial(fast_device, grid)
    placed = (
        P(axes, None, None),
        P(axes),
        P(axes, None, None),
        P(axes),
        P(axes),
        P(None, axes),
        P(axes),
        P(None, axes),
        P(None, axes),
        P(axes),
        P(None, axes),
        P(axes),
        P(axes),
        P(axes),
        P(None, axes),
        P(axes),
        P(None, axes),
        P(axes),
    )
    return jax.shard_map(
        body,
        mesh=mesh,
        in_specs=placed,
        out_specs=(
            P(axes, None, None),
            P(axes, None, None),
            P(axes),
            P(axes),
            P(None, axes),
            P(axes),
            P(None, axes),
            P(None, axes),
            P(axes),
            P(None, axes),
            P(axes),
            P(axes),
            P(axes),
            P(None, axes),
            P(axes),
            P(None, axes),
            P(axes),
        ),
        check_vma=False,
    )
```

```python
import functools
import math

import jax
import jax.numpy as jnp
from jax import lax
from jax.experimental import pallas as pl
from jax.experimental.pallas import tpu as pltpu
from jax.sharding import PartitionSpec as P

HEADS = 12


def layer_norm(values, gain, shift):
    centre = jnp.mean(values, axis=-1, keepdims=True)
    centred = values - centre
    spread = jnp.mean(centred * centred, axis=-1, keepdims=True)
    return centred * lax.rsqrt(spread + 1e-06) * gain + shift


def smooth(values):
    return jax.nn.gelu(values, approximate=True)


def project(inputs, matrix):
    return jnp.einsum("cli,ij->clj", inputs, matrix, preferred_element_type=jnp.float32)


def project_back(grads, matrix):
    return jnp.einsum("clj,ij->cli", grads, matrix, preferred_element_type=jnp.float32)


def outer_sum(inputs, grads):
    return jnp.einsum("cli,clj->ij", inputs, grads, preferred_element_type=jnp.float32)


def token_sum(grads):
    return jnp.sum(grads.astype(jnp.float32), axis=(0, 1))


def masked_scores(query_low, keys_low, keymask, factor):
    raw = (
        jnp.einsum("clhd,cmhd->chlm", query_low, keys_low, preferred_element_type=jnp.float32)
        * factor
    )
    return jnp.where(keymask[:, None, None, :], raw, -1e30)


def per_device(
    hidden,
    lengths,
    cotangent,
    attgain,
    attshift,
    querymat,
    querybias,
    keymat,
    valuemat,
    valuebias,
    mixmat,
    mixbias,
    mlpgain,
    mlpshift,
    upmat_w,
    upbias,
    downmat,
    downbias,
):
    captions, length, width = hidden.shape
    head_size = width // HEADS
    factor = 1.0 / math.sqrt(head_size)
    positions = lax.broadcasted_iota(jnp.int32, (captions, length), 1)
    keymask = positions < lengths[:, None]
    rowmask = keymask.astype(jnp.float32)[..., None]
    gathered = (
        lax.all_gather(attgain, ("dp", "fsdp"), axis=0, tiled=True),
        lax.all_gather(attshift, ("dp", "fsdp"), axis=0, tiled=True),
        lax.all_gather(querymat, ("dp", "fsdp"), axis=1, tiled=True),
        lax.all_gather(querybias, ("dp", "fsdp"), axis=0, tiled=True),
        lax.all_gather(keymat, ("dp", "fsdp"), axis=1, tiled=True),
        lax.all_gather(valuemat, ("dp", "fsdp"), axis=1, tiled=True),
        lax.all_gather(valuebias, ("dp", "fsdp"), axis=0, tiled=True),
        lax.all_gather(mixmat, ("dp", "fsdp"), axis=1, tiled=True),
        lax.all_gather(mixbias, ("dp", "fsdp"), axis=0, tiled=True),
        lax.all_gather(mlpgain, ("dp", "fsdp"), axis=0, tiled=True),
        lax.all_gather(mlpshift, ("dp", "fsdp"), axis=0, tiled=True),
        lax.all_gather(upmat_w, ("dp", "fsdp"), axis=1, tiled=True),
        lax.all_gather(upbias, ("dp", "fsdp"), axis=0, tiled=True),
        lax.all_gather(downmat, ("dp", "fsdp"), axis=1, tiled=True),
        lax.all_gather(downbias, ("dp", "fsdp"), axis=0, tiled=True),
    )
    (
        gain_one,
        shift_one,
        query_w,
        query_b,
        keys_w,
        values_w,
        values_b,
        mixer_w,
        mixer_b,
        gain_two,
        shift_two,
        upper_w,
        upper_b,
        lower_w,
        lower_b,
    ) = gathered
    gain_one = gain_one.astype(jnp.float32)
    shift_one = shift_one.astype(jnp.float32)
    gain_two = gain_two.astype(jnp.float32)
    shift_two = shift_two.astype(jnp.float32)
    source = hidden.astype(jnp.float32)
    normed_low = layer_norm(source, gain_one, shift_one).astype(jnp.bfloat16)
    query_low = (project(normed_low, query_w) + query_b.astype(jnp.float32)).astype(jnp.bfloat16)
    keys_low = project(normed_low, keys_w).astype(jnp.bfloat16)
    values_low = (project(normed_low, values_w) + values_b.astype(jnp.float32)).astype(jnp.bfloat16)
    query_heads = query_low.reshape(captions, length, HEADS, head_size)
    keys_heads = keys_low.reshape(captions, length, HEADS, head_size)
    values_heads = values_low.reshape(captions, length, HEADS, head_size)
    scores = masked_scores(query_heads, keys_heads, keymask, factor)
    peak = jnp.max(scores, axis=-1, keepdims=True)
    logsum = peak + jnp.log(jnp.sum(jnp.exp(scores - peak), axis=-1, keepdims=True))
    probs_low = jnp.exp(scores - logsum).astype(jnp.bfloat16)
    mixed_low = (
        jnp.einsum("chlm,cmhd->clhd", probs_low, values_heads, preferred_element_type=jnp.float32)
        .reshape(captions, length, width)
        .astype(jnp.bfloat16)
    )
    middle = source + project(mixed_low, mixer_w) + mixer_b.astype(jnp.float32)
    normed2_low = layer_norm(middle, gain_two, shift_two).astype(jnp.bfloat16)
    upper = project(normed2_low, upper_w) + upper_b.astype(jnp.float32)
    active_low = smooth(upper).astype(jnp.bfloat16)
    result = middle + project(active_low, lower_w) + lower_b.astype(jnp.float32)
    block_out = result.astype(jnp.bfloat16)
    again = (
        lax.all_gather(attgain, ("dp", "fsdp"), axis=0, tiled=True),
        lax.all_gather(attshift, ("dp", "fsdp"), axis=0, tiled=True),
        lax.all_gather(querymat, ("dp", "fsdp"), axis=1, tiled=True),
        lax.all_gather(querybias, ("dp", "fsdp"), axis=0, tiled=True),
        lax.all_gather(keymat, ("dp", "fsdp"), axis=1, tiled=True),
        lax.all_gather(valuemat, ("dp", "fsdp"), axis=1, tiled=True),
        lax.all_gather(valuebias, ("dp", "fsdp"), axis=0, tiled=True),
        lax.all_gather(mixmat, ("dp", "fsdp"), axis=1, tiled=True),
        lax.all_gather(mixbias, ("dp", "fsdp"), axis=0, tiled=True),
        lax.all_gather(mlpgain, ("dp", "fsdp"), axis=0, tiled=True),
        lax.all_gather(mlpshift, ("dp", "fsdp"), axis=0, tiled=True),
        lax.all_gather(upmat_w, ("dp", "fsdp"), axis=1, tiled=True),
        lax.all_gather(upbias, ("dp", "fsdp"), axis=0, tiled=True),
        lax.all_gather(downmat, ("dp", "fsdp"), axis=1, tiled=True),
        lax.all_gather(downbias, ("dp", "fsdp"), axis=0, tiled=True),
    )
    (
        gain_one,
        shift_one,
        query_w,
        query_b,
        keys_w,
        values_w,
        values_b,
        mixer_w,
        mixer_b,
        gain_two,
        shift_two,
        upper_w,
        upper_b,
        lower_w,
        lower_b,
    ) = again
    gain_one = gain_one.astype(jnp.float32)
    shift_one = shift_one.astype(jnp.float32)
    gain_two = gain_two.astype(jnp.float32)
    shift_two = shift_two.astype(jnp.float32)
    grad_out = cotangent.astype(jnp.float32) * rowmask
    grad_low = grad_out.astype(jnp.bfloat16)
    downmat_grad = outer_sum(active_low, grad_low)
    downbias_grad = token_sum(grad_low)
    grad_active = project_back(grad_low, lower_w)
    gelu_pull = jax.vjp(smooth, upper)[1]
    grad_upper_low = gelu_pull(grad_active)[0].astype(jnp.bfloat16)
    upmat_grad = outer_sum(normed2_low, grad_upper_low)
    upbias_grad = token_sum(grad_upper_low)
    grad_normed2 = project_back(grad_upper_low, upper_w)
    norm_pull = jax.vjp(layer_norm, middle, gain_two, shift_two)[1]
    grad_ln_two, mlpgain_grad, mlpshift_grad = norm_pull(grad_normed2)
    grad_middle = grad_out + grad_ln_two
    mlpgain_grad, mlpshift_grad, upmat_grad, upbias_grad, downmat_grad, downbias_grad = (
        lax.psum_scatter(mlpgain_grad, ("dp", "fsdp"), scatter_dimension=0, tiled=True),
        lax.psum_scatter(mlpshift_grad, ("dp", "fsdp"), scatter_dimension=0, tiled=True),
        lax.psum_scatter(upmat_grad, ("dp", "fsdp"), scatter_dimension=1, tiled=True),
        lax.psum_scatter(upbias_grad, ("dp", "fsdp"), scatter_dimension=0, tiled=True),
        lax.psum_scatter(downmat_grad, ("dp", "fsdp"), scatter_dimension=1, tiled=True),
        lax.psum_scatter(downbias_grad, ("dp", "fsdp"), scatter_dimension=0, tiled=True),
    )
    grad_branch_low = grad_middle.astype(jnp.bfloat16)
    mixmat_grad = outer_sum(mixed_low, grad_branch_low)
    mixbias_grad = token_sum(grad_branch_low)
    grad_mixed_low = (
        project_back(grad_branch_low, mixer_w)
        .astype(jnp.bfloat16)
        .reshape(captions, length, HEADS, head_size)
    )
    scores_again = masked_scores(query_heads, keys_heads, keymask, factor)
    probs = jnp.exp(scores_again - logsum)
    probs_again = probs.astype(jnp.bfloat16)
    grad_values_low = jnp.einsum(
        "chlm,clhd->cmhd", probs_again, grad_mixed_low, preferred_element_type=jnp.float32
    ).astype(jnp.bfloat16)
    grad_probs = jnp.einsum(
        "clhd,cmhd->chlm", grad_mixed_low, values_heads, preferred_element_type=jnp.float32
    )
    weighted = jnp.sum(probs * grad_probs, axis=-1, keepdims=True)
    grad_scores_low = (probs * (grad_probs - weighted)).astype(jnp.bfloat16)
    grad_query_low = (
        jnp.einsum(
            "chlm,cmhd->clhd", grad_scores_low, keys_heads, preferred_element_type=jnp.float32
        )
        * factor
    ).astype(jnp.bfloat16)
    grad_keys_low = (
        jnp.einsum(
            "chlm,clhd->cmhd", grad_scores_low, query_heads, preferred_element_type=jnp.float32
        )
        * factor
    ).astype(jnp.bfloat16)
    grad_query_low = grad_query_low.reshape(captions, length, width)
    grad_keys_low = grad_keys_low.reshape(captions, length, width)
    grad_values_low = grad_values_low.reshape(captions, length, width)
    querymat_grad = outer_sum(normed_low, grad_query_low)
    querybias_grad = token_sum(grad_query_low)
    keymat_grad = outer_sum(normed_low, grad_keys_low)
    valuemat_grad = outer_sum(normed_low, grad_values_low)
    valuebias_grad = token_sum(grad_values_low)
    grad_normed = (
        project_back(grad_query_low, query_w)
        + project_back(grad_keys_low, keys_w)
        + project_back(grad_values_low, values_w)
    )
    first_pull = jax.vjp(layer_norm, source, gain_one, shift_one)[1]
    grad_ln_one, attgain_grad, attshift_grad = first_pull(grad_normed)
    input_grad = grad_middle + grad_ln_one
    (
        attgain_grad,
        attshift_grad,
        querymat_grad,
        querybias_grad,
        keymat_grad,
        valuemat_grad,
        valuebias_grad,
        mixmat_grad,
        mixbias_grad,
    ) = (
        lax.psum_scatter(attgain_grad, ("dp", "fsdp"), scatter_dimension=0, tiled=True),
        lax.psum_scatter(attshift_grad, ("dp", "fsdp"), scatter_dimension=0, tiled=True),
        lax.psum_scatter(querymat_grad, ("dp", "fsdp"), scatter_dimension=1, tiled=True),
        lax.psum_scatter(querybias_grad, ("dp", "fsdp"), scatter_dimension=0, tiled=True),
        lax.psum_scatter(keymat_grad, ("dp", "fsdp"), scatter_dimension=1, tiled=True),
        lax.psum_scatter(valuemat_grad, ("dp", "fsdp"), scatter_dimension=1, tiled=True),
        lax.psum_scatter(valuebias_grad, ("dp", "fsdp"), scatter_dimension=0, tiled=True),
        lax.psum_scatter(mixmat_grad, ("dp", "fsdp"), scatter_dimension=1, tiled=True),
        lax.psum_scatter(mixbias_grad, ("dp", "fsdp"), scatter_dimension=0, tiled=True),
    )
    return (
        block_out,
        input_grad,
        attgain_grad,
        attshift_grad,
        querymat_grad,
        querybias_grad,
        keymat_grad,
        valuemat_grad,
        valuebias_grad,
        mixmat_grad,
        mixbias_grad,
        mlpgain_grad,
        mlpshift_grad,
        upmat_grad,
        upbias_grad,
        downmat_grad,
        downbias_grad,
    )


NT = (((1,), (1,)), ((), ()))
NN = (((1,), (0,)), ((), ()))
TN = (((0,), (0,)), ((), ()))
F32 = jnp.float32
BF16 = jnp.bfloat16
AXES = ("z", "x", "y", "c")
QUAD = 4
VMEM_LIMIT = 56 * 1024 * 1024


def dot(left, right, dims):
    return lax.dot_general(left, right, dims, preferred_element_type=F32)


class Grid3:
    def __init__(self, dp, fsdp):
        self.c = 2
        self.y = fsdp // 2
        self.x = self.y
        self.z = dp // self.x
        self.count = dp * fsdp

    def index(self, z, x, y, c):
        return ((z * self.x + x) * self.y + y) * self.c + c

    def shift(self, values, kz=0, kx=0, ky=0, kc=0):
        pairs = []
        for z in range(self.z):
            for x in range(self.x):
                for y in range(self.y):
                    for c in range(self.c):
                        pairs.append((self.index(z, x, y, c), self.index(z ^ kz, x ^ kx, y ^ ky, c ^ kc)))
        return lax.ppermute(values, AXES, pairs)

    def here(self):
        return tuple(lax.axis_index(name) for name in AXES)

    def me(self):
        return self.index(*self.here())

    def away(self, *bits):
        return self.index(*(lax.bitwise_xor(at, jnp.int32(bit)) for at, bit in zip(self.here(), bits)))


def tie(values, gate):
    return lax.optimization_barrier((values, gate))[0]


def together(values):
    return lax.optimization_barrier(values)


COLUMN = (0, 3, 1, 2)


def gather_one(grid, first, second):
    return first, second, grid.shift(first, kx=1), grid.shift(second, ky=1)


def gather_two(grid, four):
    first, second, first_x, second_y = four
    one = jnp.concatenate([first, first_x])
    two = jnp.concatenate([second, second_y])
    return one, two, grid.shift(one, ky=1), grid.shift(two, kx=1)


def gather_core(grid, arrays):
    return tuple(grid.shift(array, kc=1) for array in arrays)


def gather_places():
    first, second = COLUMN[:2], COLUMN[2:]
    one = [(z, x, 0) for x in range(2) for z in first]
    two = [(z, 0, y) for y in range(2) for z in second]
    one_y = [(z, x, 1) for z, x, _ in one]
    two_x = [(z, 1, y) for z, _, y in two]
    return [[spot + (core,) for spot in group] for core, pair in ((0, 0), (0, 1), (1, 0), (1, 1)) for group in ((one, two), (one_y, two_x))[pair]]


def place(grid, places, refs, held):
    for ref, spots in zip(refs, places):
        for slot, spot in enumerate(spots):
            held[grid.away(*spot)] = ref[slot]


def place_kernel(grid, places, *refs):
    place(grid, places, refs[:-1], refs[-1])


def outgoing(grid, core):
    half = grid.z // 2
    slots = []
    for which in range(2):
        for one in range(2):
            for two in range(2):
                for low in range(half):
                    kx, ky = (one, two) if which == 0 else (two, one)
                    slots.append((COLUMN[which * half + low], kx, ky, core))
    return slots


def plus(left, right):
    return (left.astype(F32) + right.astype(F32)).astype(BF16)


def scatter_core(grid, other):
    return grid.shift(other, kc=1)


def join(values, extra):
    values = values.reshape(-1, 8, values.shape[-1])
    return values if extra is None else jnp.concatenate([values, extra])


def part(values, shape):
    count = math.prod(shape[:-1]) // 8
    return values[:count].reshape(shape), values[count:]


def scatter_first(grid, own, arrived, extra=None):
    shape = (2, 2, 2, grid.z // 2) + own.shape[1:]
    own = own.reshape(shape)
    arrived = arrived.reshape(shape)
    send_a = plus(own[0, 1], arrived[0, 1])
    send_b = plus(own[1, 1], arrived[1, 1])
    keep_a = plus(own[0, 0], arrived[0, 0])
    keep_b = plus(own[1, 0], arrived[1, 0])
    if extra is not None:
        send_a = join(send_a, extra.astype(BF16))
    return keep_a, keep_b, grid.shift(send_a, kx=1), grid.shift(send_b, ky=1), extra, (send_a, send_b)


def scatter_second(grid, state, gate):
    keep_a, keep_b, got_a, got_b, extra, _ = state
    got_a, got_b = tie((got_a, got_b), gate)
    if extra is not None:
        got_a, more = part(got_a, keep_a.shape)
        extra = extra + more.astype(F32)
    next_a = plus(keep_a[1], got_a[1])
    next_b = plus(keep_b[1], got_b[1])
    rest_a = plus(keep_a[0], got_a[0])
    rest_b = plus(keep_b[0], got_b[0])
    if extra is not None:
        next_a = join(next_a, extra.astype(BF16))
    return rest_a, rest_b, grid.shift(next_a, ky=1), grid.shift(next_b, kx=1), extra, (next_a, next_b)


def scatter_third(grid, state, gate):
    rest_a, rest_b, last_a, last_b, extra, _ = state
    last_a, last_b = tie((last_a, last_b), gate)
    if extra is not None:
        last_a, more = part(last_a, rest_a.shape)
        extra = extra + more.astype(F32)
    half = grid.z // 2
    parts = [plus(rest_a[k], last_a[k]) for k in range(half)] + [plus(rest_b[k], last_b[k]) for k in range(half)]
    sends = parts[1:]
    if extra is not None:
        sends = [join(send, extra.astype(BF16)) for send in sends]
    return parts[0], [grid.shift(send, kz=k) for send, k in zip(sends, COLUMN[1:])], extra, sends


def scatter_near(grid, state, gate):
    rest_a, rest_b, last_a, last_b, _, _ = state
    last_a, last_b = tie((last_a, last_b), gate)
    send = plus(rest_b, last_b)
    return plus(rest_a, last_a), grid.shift(send, kz=1), send


def scatter_far(grid, state, gate):
    keep, got, _ = state
    got = tie(got, gate)
    send = plus(keep[1], got[1])
    return keep[0].astype(F32) + got[0].astype(F32), grid.shift(send, kz=3), send


def scatter_end(state, gate):
    total, got, _ = state
    return total + tie(got, gate).astype(F32)


def scatter_last(state, gate):
    total, came, extra, _ = state
    shape = total.shape
    came = tie(came, gate)
    total = total.astype(F32)
    for values in came:
        if extra is not None:
            values, more = part(values, shape)
            extra = extra + more.astype(F32)
        total = total + values.astype(F32)
    return total if extra is None else (total, extra)


def lanes_of(rows):
    return lax.broadcasted_iota(jnp.int32, (rows, 256), 1) // 64


def spread(block):
    head = lanes_of(block.shape[0])
    zero = jnp.zeros_like(block)
    return jnp.concatenate([jnp.where(head == g, block, zero) for g in range(QUAD)], axis=0)


def collect(square):
    head = lanes_of(64)
    total = jnp.where(head == 0, square[0:64], 0.0)
    for g in range(1, QUAD):
        total = jnp.where(head == g, square[64 * g : 64 * g + 64], total)
    return total


def normal(values):
    centre = jnp.mean(values, axis=-1, keepdims=True)
    centred = values - centre
    spread_of = jnp.mean(centred * centred, axis=-1, keepdims=True)
    scale = lax.rsqrt(spread_of + 1e-06)
    return centred * scale, scale


def normal_back(hat, scale, gain, grads):
    weighted = grads * gain
    middle = jnp.mean(weighted, axis=-1, keepdims=True)
    along = jnp.mean(weighted * hat, axis=-1, keepdims=True)
    return scale * (weighted - middle - hat * along)


TILE = 16
SIZES = (384, 512, 640, 768, 896, 1024)


def order_of(lengths, length):
    captions = lengths.shape[0]
    tiles = length // TILE
    real = (lengths + (TILE - 1)) // TILE
    before = jnp.tril(jnp.ones((captions, captions), jnp.int32), -1)
    start = jnp.sum(before * real[None, :], axis=1)
    total = jnp.sum(real)
    late = total + jnp.sum(before * (tiles - real)[None, :], axis=1)
    at = jnp.arange(tiles, dtype=jnp.int32)[None, :]
    spots = jnp.where(at < real[:, None], start[:, None] + at, late[:, None] + at - real[:, None])
    sizes = jnp.array(SIZES, jnp.int32)
    size = jnp.min(jnp.where(sizes >= total * TILE, sizes, SIZES[-1]))
    return jnp.concatenate([spots.reshape(-1), start, jnp.stack([size, total])]).astype(jnp.int32)


def tile_rows(place_ref, index):
    return pl.ds(pl.multiple_of(place_ref[index] * TILE, TILE), TILE)


def by_size(size, body):
    for rows in SIZES:
        pl.when(size == rows)(functools.partial(body, rows))


def rows_at(step, rows):
    return pl.ds(pl.multiple_of(step * rows, rows), rows)


def pack_kernel(grid, small_ref, q_ref, k_ref, v_ref, out_ref, wide, sems):
    copies = [
        pltpu.make_async_copy(ref, out_ref.at[3 * at : 3 * at + 3], sems.at[at])
        for at, ref in enumerate((q_ref, k_ref, v_ref))
    ]
    for copy in copies:
        copy.start()
    share = small_ref.shape[1]
    wide[...] = jnp.zeros_like(wide)
    wide[:, 0:share] = small_ref[...].astype(F32)
    out_ref[9] = pltpu.roll(wide[...], grid.me() * share, 1).astype(BF16)
    for copy in copies:
        copy.wait()


def pack_up_kernel(grid, small_ref, out_ref, wide):
    width = wide.shape[1]
    wide[...] = jnp.zeros_like(wide)
    wide[0:1, 0 : small_ref.shape[1]] = small_ref[...]
    me = grid.me()
    four = pltpu.roll(wide[...], lax.rem(me, 8) * small_ref.shape[1], 1)
    row = lax.broadcasted_iota(jnp.int32, (8, width), 0)
    four = jnp.where(row == lax.div(me, 8), jnp.broadcast_to(four[0:1], (8, width)), 0.0)
    out_ref[0] = four.astype(BF16)


def project_kernel(grid, places, place_ref, hidden_ref, *rest):
    count = len(places)
    refs, rest = rest[:count], rest[count:]
    moved_ref, normed_out, q_ref, k_ref, v_ref, vec_ref, held = rest
    total = jnp.zeros(vec_ref.shape, F32)
    for ref, spots in zip(refs, places):
        for slot, spot in enumerate(spots):
            total = total + ref[slot, 9].astype(F32)
            held[grid.away(*spot)] = ref[slot, 0:9]
    vec_ref[...] = total
    width = hidden_ref.shape[1]
    rows = 256

    def block(step, carry):
        at = rows_at(step, rows)
        hidden = hidden_ref[at, :]
        hat, _ = normal(hidden.astype(F32))
        normed = (hat * vec_ref[0:1, :] + vec_ref[1:2, :]).astype(BF16)
        q_ref[at, :] = (dot(normed, held[:, 0 : 3].reshape(width, width), NT) + vec_ref[2:3, :]).astype(BF16)
        k_ref[at, :] = dot(normed, held[:, 3 : 6].reshape(width, width), NT).astype(BF16)
        v_ref[at, :] = (dot(normed, held[:, 6 : 9].reshape(width, width), NT) + vec_ref[3:4, :]).astype(BF16)
        for t in range(rows // TILE):
            to = tile_rows(place_ref, step * (rows // TILE) + t)
            part = slice(t * TILE, (t + 1) * TILE)
            normed_out[to, :] = normed[part, :]
            moved_ref[to, :] = hidden[part, :]
        return carry

    lax.fori_loop(0, hidden_ref.shape[0] // rows, block, 0)


def attend_kernel(length, group, lengths_ref, place_ref, q_ref, k_ref, v_ref, probs_ref, mixed_out):
    width = q_ref.shape[1]
    captions = q_ref.shape[0] // length
    tiles = length // TILE
    quads = width // 256
    position = lax.broadcasted_iota(jnp.int32, (length, 256), 0)

    def several(step, carry):
        items = [
            (step * group + g, quad, rows_at(step * group + g, length), slice(256 * quad, 256 * quad + 256))
            for g in range(group)
            for quad in range(quads)
        ]
        scores = [dot(k_ref[rows, lanes], spread(q_ref[rows, lanes]), NT) for _, _, rows, lanes in items]
        probs = []
        for (cap, _, _, _), score in zip(items, scores):
            score = jnp.where(position < lengths_ref[cap], score * 0.125, -1e30)
            raised = jnp.exp(score - jnp.max(score, axis=0, keepdims=True))
            probs.append((raised * (1.0 / jnp.sum(raised, axis=0, keepdims=True))).astype(BF16))
        for (cap, quad, _, _), prob in zip(items, probs):
            probs_ref[cap * quads + quad] = prob
        mixed = [
            collect(dot(prob, v_ref[rows, lanes], TN)).astype(BF16)
            for (_, _, rows, lanes), prob in zip(items, probs)
        ]
        for (cap, _, _, lanes), value in zip(items, mixed):
            for t in range(tiles):
                to = tile_rows(place_ref, cap * tiles + t)
                mixed_out[to, lanes] = value[t * TILE : (t + 1) * TILE, :]
        return carry

    lax.fori_loop(0, captions // group, several, 0)


def bend_parts(grid, parts, normed, bias_ref, held, at, active_ref, slope_ref):
    width = normed.shape[1]
    per = grid.count // 4
    root = math.sqrt(2.0 / math.pi)
    for part in parts:
        weight = held[per * part : per * part + per, 3:15].reshape(width, width)
        upper = dot(normed, weight, NT) + bias_ref[part : part + 1, :]
        square = upper * upper
        bend = jnp.tanh(upper * (root + (root * 0.044715) * square))
        half = 0.5 * bend + 0.5
        span = slice(width * part, width * part + width)
        active = upper * half
        active_ref[at, span] = active.astype(BF16)
        slope = half + active * ((1.0 - bend) * (root + (3.0 * root * 0.044715) * square))
        slope_ref[at, span] = slope.astype(BF16)


def upper_kernel(grid, places, moved_ref, mixed_ref, vec_ref, *rest):
    count = len(places)
    refs, rest = rest[:count], rest[count + 1 :]
    middle_ref, normed_ref, active_ref, slope_ref, bias_ref, held = rest
    place(grid, places, refs, held)
    bias = jnp.zeros(bias_ref.shape, F32)
    for device in range(grid.count):
        bias = bias + held[device, 15].astype(F32)
    bias_ref[...] = bias
    width = moved_ref.shape[1]
    rows = 256

    def block(step, carry):
        at = rows_at(step, rows)
        middle = (
            moved_ref[at, :].astype(F32)
            + dot(mixed_ref[at, :], held[:, 0:3].reshape(width, width), NT)
            + vec_ref[4:5, :]
        )
        middle_ref[at, :] = middle
        hat, _ = normal(middle)
        normed = (hat * vec_ref[5:6, :] + vec_ref[6:7, :]).astype(BF16)
        normed_ref[at, :] = normed
        bend_parts(grid, (0, 1, 2, 3), normed, bias_ref, held, at, active_ref, slope_ref)
        return carry

    lax.fori_loop(0, moved_ref.shape[0] // rows, block, 0)


def down_grad_kernel(grid, length, size_at, lengths_ref, place_ref, cot_ref, active_ref, low_ref, vec_ref, own_ref, other_ref, far_ref, total, sem):
    keep = pltpu.make_async_copy(active_ref, far_ref.at[0 : active_ref.shape[0]], sem)
    keep.start()
    width = cot_ref.shape[1]
    captions = cot_ref.shape[0] // length
    tiles = length // TILE
    position = lax.broadcasted_iota(jnp.int32, (length, 1), 0)
    vec_ref[...] = jnp.zeros_like(vec_ref)

    def caption(cap, carry):
        part = cot_ref[rows_at(cap, length), :].astype(F32)
        part = jnp.where(position < lengths_ref[cap], part, 0.0)
        vec_ref[0:1, :] += jnp.sum(part, axis=0, keepdims=True)
        part = part.astype(BF16)
        for t in range(tiles):
            low_ref[tile_rows(place_ref, cap * tiles + t), :] = part[t * TILE : (t + 1) * TILE, :]
        return carry

    lax.fori_loop(0, captions, caption, 0)
    share = width // grid.count

    def column(step, carry):
        lanes = rows_at(step, width)

        def product(rows):
            total[...] = dot(low_ref[0:rows, :], active_ref[0:rows, lanes], TN)

        by_size(place_ref[size_at], product)
        for core, out_ref in ((0, own_ref), (1, other_ref)):
            for slot, spot in enumerate(outgoing(grid, core)):
                at = pl.multiple_of(grid.away(*spot) * share, 8)
                out_ref[slot, :, lanes] = total[pl.ds(at, share), :].astype(BF16)
        return carry

    lax.fori_loop(0, active_ref.shape[1] // width, column, 0)
    keep.wait()


def upper_grad_kernel(grid, places, size_at, place_ref, low_ref, slope_ref, normed_ref, *rest):
    count = len(places)
    refs, rest = rest[:count], rest[count + 1 :]
    upper_ref, vec_ref, own_ref, other_ref, held, far_ref, total, sem = rest
    place(grid, places, refs, held)
    keep = pltpu.make_async_copy(held, far_ref.at[0 : grid.count], sem)
    keep.start()
    width = low_ref.shape[1]
    per = grid.count // 4
    share = width // per
    half = grid.z // 2
    z, x, y, c = grid.here()
    shape = own_ref.shape[1:]
    mine = jnp.where(c == 0, 0, share)

    def column(step, carry):
        lanes = rows_at(step, width)

        def product(rows):
            grads = dot(low_ref[0:rows, :], held[:, :, lanes].reshape(width, width), NN) * slope_ref[0:rows, lanes].astype(F32)
            vec_ref[rows_at(step, 8), :] = jnp.broadcast_to(jnp.sum(grads, axis=0, keepdims=True), (8, width))
            grads = grads.astype(BF16)
            upper_ref[0:rows, lanes] = grads
            total[...] = dot(grads, normed_ref[0:rows, :], TN)

        by_size(place_ref[size_at], product)
        for k in range(per // 2):
            chip = step * (per // 2) + k
            kz = lax.bitwise_xor(lax.div(chip, grid.x * grid.y), z)
            kx = lax.bitwise_xor(lax.rem(lax.div(chip, grid.y), grid.x), x)
            ky = lax.bitwise_xor(lax.rem(chip, grid.y), y)
            low = lax.div(kz, 2)
            which = lax.bitwise_xor(low, lax.rem(kz, 2))
            one = jnp.where(which == 0, kx, ky)
            two = jnp.where(which == 0, ky, kx)
            slot = ((which * 2 + one) * 2 + two) * half + low
            own_at = pl.multiple_of(2 * share * k + mine, 8)
            other_at = pl.multiple_of(2 * share * k + (share - mine), 8)
            own_ref[slot] = total[pl.ds(own_at, share), :].astype(BF16).reshape(shape)
            other_ref[slot] = total[pl.ds(other_at, share), :].astype(BF16).reshape(shape)
        return carry

    lax.fori_loop(0, upper_ref.shape[1] // width, column, 0)
    keep.wait()


def by_block(size, block):
    whole = lax.div(size, 256)

    def two(step, carry):
        block(rows_at(step, 256), 256)
        return carry

    lax.fori_loop(0, whole, two, 0)

    @pl.when(lax.rem(size, 256) > 0)
    def _():
        block(pl.ds(pl.multiple_of(whole * 256, 256), 128), 128)


def middle_grad_kernel(grid, size_at, place_ref, upper_ref, middle_ref, low_ref, vec_in, held, grad_ref, branch_ref, dm_ref, vec_ref):
    width = middle_ref.shape[1]
    vec_ref[...] = jnp.zeros_like(vec_ref)

    def block(at, rows):
        weight = held[:, 3:15].reshape(upper_ref.shape[1], width)
        grads = dot(upper_ref[at, :], weight, NN)
        hat, scale = normal(middle_ref[at, :])
        grad_middle = low_ref[at, :].astype(F32) + normal_back(hat, scale, vec_in[5:6, :], grads)
        grad_ref[at, :] = grad_middle
        branch = grad_middle.astype(BF16)
        branch_ref[at, :] = branch
        dm_ref[at, :] = dot(branch, held[:, 0:3].reshape(width, width), NN).astype(BF16)
        vec_ref[0:1, :] += jnp.sum(grads * hat, axis=0, keepdims=True)
        vec_ref[1:2, :] += jnp.sum(grads, axis=0, keepdims=True)
        vec_ref[2:3, :] += jnp.sum(grad_middle, axis=0, keepdims=True)

    by_block(place_ref[size_at], block)


def attend_grad_kernel(length, group, lengths_ref, place_ref, dm_ref, q_ref, k_ref, v_ref, probs_ref, grads_ref, vec_ref):
    width = dm_ref.shape[1]
    quads = width // 256
    tiles = length // TILE
    captions = probs_ref.shape[0] // quads
    starts = captions * tiles
    end = place_ref[starts + captions + 1]
    clear = pl.ds(pl.multiple_of(end * TILE, TILE), 256)
    for which in range(3):
        grads_ref[which, clear, :] = jnp.zeros((256, width), BF16)
    vec_ref[...] = jnp.zeros_like(vec_ref)
    row = lax.broadcasted_iota(jnp.int32, (length, 1), 0)

    def several(step, carry):
        items = []
        for g in range(group):
            cap = step * group + g
            packed = pl.ds(pl.multiple_of(place_ref[starts + cap] * TILE, TILE), length)
            plain = pl.ds(pl.multiple_of(cap * length, length), length)
            for quad in range(quads):
                items.append((cap, quad, packed, plain, slice(256 * quad, 256 * quad + 256)))
        probs = [probs_ref[cap * quads + quad] for cap, quad, _, _, _ in items]
        wide = []
        for cap, _, packed, _, lanes in items:
            dm = dm_ref[packed, lanes]
            wide.append(spread(jnp.where(row < lengths_ref[cap], dm, jnp.zeros_like(dm))))
        grad_probs = [dot(v_ref[plain, lanes], w, NT) for (_, _, _, plain, lanes), w in zip(items, wide)]
        grad_values = [dot(p, w, NN) for p, w in zip(probs, wide)]
        grad_scores = []
        for p, grad in zip(probs, grad_probs):
            p = p.astype(F32)
            along = p * grad
            grad_scores.append((along - p * jnp.sum(along, axis=0, keepdims=True)).astype(BF16))
        grad_keys = [
            dot(g, spread(q_ref[plain, lanes]), NN) * 0.125 for (_, _, _, plain, lanes), g in zip(items, grad_scores)
        ]
        grad_query = [
            collect(dot(g, k_ref[plain, lanes], TN)) * 0.125 for (_, _, _, plain, lanes), g in zip(items, grad_scores)
        ]
        for at, (_, _, packed, _, lanes) in enumerate(items):
            grads_ref[0, packed, lanes] = grad_query[at].astype(BF16)
            grads_ref[1, packed, lanes] = grad_keys[at].astype(BF16)
            grads_ref[2, packed, lanes] = grad_values[at].astype(BF16)
        for quad in range(quads):
            lanes = slice(256 * quad, 256 * quad + 256)
            vec_ref[0:1, lanes] += sum(jnp.sum(v, axis=0, keepdims=True) for v in grad_query[quad::quads])
            vec_ref[1:2, lanes] += sum(jnp.sum(v, axis=0, keepdims=True) for v in grad_values[quad::quads])
        return carry

    lax.fori_loop(0, captions // group, several, 0)


def weight_grad_kernel(grid, size_at, place_ref, grads_ref, branch_ref, normed_ref, mixed_ref, own_ref, other_ref, total):
    share = total.shape[0] // grid.count

    def send(at):
        for core, out_ref in ((0, own_ref), (1, other_ref)):
            for slot, spot in enumerate(outgoing(grid, core)):
                start = pl.multiple_of(grid.away(*spot) * share, 8)
                out_ref[slot, at] = total[pl.ds(start, share), :].astype(BF16)

    def matrix(at, carry):
        def product(rows):
            total[...] = dot(grads_ref[at, 0:rows, :], normed_ref[0:rows, :], TN)

        by_size(place_ref[size_at], product)
        send(at)
        return carry

    lax.fori_loop(0, 3, matrix, 0)

    def product(rows):
        total[...] = dot(branch_ref[0:rows, :], mixed_ref[0:rows, :], TN)

    by_size(place_ref[size_at], product)
    send(3)


def input_grad_kernel(grid, size_at, place_ref, moved_ref, grad_ref, grads_ref, vec_in, down_vec, up_vec, mid_vec, att_vec, held, far_ref, out_ref, vec_ref, near_ref, found, sem):
    load = pltpu.make_async_copy(far_ref.at[0 : near_ref.shape[0]], near_ref, sem)
    load.start()
    width = moved_ref.shape[1]
    vec_ref[...] = jnp.zeros_like(vec_ref)
    vec_ref[2:4, :] = att_vec[0:2, :]
    vec_ref[4:5, :] = mid_vec[2:3, :]
    vec_ref[5:7, :] = mid_vec[0:2, :]
    vec_ref[7:8, :] = down_vec[0:1, :]
    for part in range(4):
        vec_ref[8 + part : 9 + part, :] = up_vec[8 * part : 8 * part + 1, :]

    def block(at, rows):
        grads = dot(grads_ref[0, at, :], held[:, 0 : 3].reshape(width, width), NN)
        grads = grads + dot(grads_ref[1, at, :], held[:, 3 : 6].reshape(width, width), NN)
        grads = grads + dot(grads_ref[2, at, :], held[:, 6 : 9].reshape(width, width), NN)
        hat, scale = normal(moved_ref[at, :].astype(F32))
        found[at, :] = grad_ref[at, :] + normal_back(hat, scale, vec_in[0:1, :], grads)
        vec_ref[0:1, :] += jnp.sum(grads * hat, axis=0, keepdims=True)
        vec_ref[1:2, :] += jnp.sum(grads, axis=0, keepdims=True)

    by_block(place_ref[size_at], block)
    total = place_ref[size_at + 1]

    def tile(index, carry):
        values = found[tile_rows(place_ref, index), :]
        out_ref[rows_at(index, TILE), :] = jnp.where(place_ref[index] < total, values, 0.0)
        return carry

    lax.fori_loop(0, out_ref.shape[0] // TILE, tile, 0)
    load.wait()


def lower_kernel(place_ref, active_far, middle_ref, vec_in, weight_ref, out_ref, active, found, sems):
    count, rows = active.shape[0], active.shape[1]

    def fetch(step):
        return pltpu.make_async_copy(active_far.at[rows_at(step, rows), :], active.at[step], sems.at[step])

    fetch(0).start()

    def block(step, carry):
        fetch(step).wait()

        @pl.when(step + 1 < count)
        def _():
            fetch(step + 1).start()

        at = rows_at(step, rows)
        weight = weight_ref[...].reshape(middle_ref.shape[1], active.shape[2])
        out = middle_ref[at, :] + dot(active[step], weight, NT) + vec_in[7:8, :]
        found[at, :] = out.astype(BF16)
        return carry

    lax.fori_loop(0, count, block, 0)

    def tile(index, carry):
        out_ref[rows_at(index, TILE), :] = found[tile_rows(place_ref, index), :]
        return carry

    lax.fori_loop(0, out_ref.shape[0] // TILE, tile, 0)


def unpack_kernel(grid, vec_ref, *outs):
    me = grid.me()
    eight = pltpu.roll(vec_ref[0:8, :], lax.rem(768 - me * 24, 768), 1)
    for k in range(8):
        outs[k][...] = eight[k : k + 1, 0:24]
    row = lax.broadcasted_iota(jnp.int32, (8, 768), 0)
    four = jnp.sum(jnp.where(row == lax.div(me, 8), vec_ref[8:16, :], 0.0), axis=0, keepdims=True)
    four = jnp.broadcast_to(four, (8, 768))
    four = pltpu.roll(four, lax.rem(768 - lax.rem(me, 8) * 96, 768), 1)
    outs[8][...] = four[0:1, 0:96]


def whole(shape):
    return pl.BlockSpec(shape, lambda *_: (0,) * len(shape))


ANY = pl.BlockSpec(memory_space=pl.ANY)
SMEM = pl.BlockSpec(memory_space=pltpu.SMEM)


FAST = pl.BlockSpec(memory_space=pltpu.VMEM)
FAR = pl.BlockSpec(memory_space=pltpu.HBM)
LARGE = 1 << 26


def call(kernel, steps, in_specs, out_specs, outs, scratch, flops, moved, name, limit=8):
    return pl.pallas_call(
        kernel,
        grid=(steps,),
        in_specs=in_specs,
        out_specs=out_specs,
        out_shape=[jax.ShapeDtypeStruct(s, d) for s, d in outs],
        scratch_shapes=scratch,
        compiler_params=pltpu.CompilerParams(vmem_limit_bytes=limit * 1024 * 1024),
        cost_estimate=pl.CostEstimate(flops=flops, bytes_accessed=moved, transcendentals=0),
        name=name,
    )


def call_near(kernel, in_specs, outs, scratch, flops, name, limit=8, aliases=None, far=0):
    return pl.pallas_call(
        kernel,
        in_specs=in_specs,
        out_specs=[FAST] * (len(outs) - far) + [FAR] * far,
        input_output_aliases=aliases or {},
        out_shape=[jax.ShapeDtypeStruct(s, d) for s, d in outs],
        scratch_shapes=scratch,
        compiler_params=pltpu.CompilerParams(vmem_limit_bytes=limit * 1024 * 1024),
        cost_estimate=pl.CostEstimate(flops=flops, bytes_accessed=1_000_000, transcendentals=0),
        name=name,
    )


def fast_device(
    grid,
    hidden,
    lengths,
    cotangent,
    attgain,
    attshift,
    querymat,
    querybias,
    keymat,
    valuemat,
    valuebias,
    mixmat,
    mixbias,
    mlpgain,
    mlpshift,
    upmat_w,
    upbias,
    downmat,
    downbias,
):
    captions, length, width = hidden.shape
    tokens = captions * length
    hidden2 = hidden.reshape(tokens, width)
    cot2 = cotangent.reshape(tokens, width)
    share = width // grid.count
    ff = downmat.shape[0]
    small = jnp.stack([attgain, attshift, querybias, valuebias, mixbias, mlpgain, mlpshift, downbias])
    units = share // 8
    (first,) = pl.pallas_call(
        functools.partial(pack_kernel, grid),
        in_specs=[FAST] + [FAR] * 3,
        out_specs=[FAST],
        out_shape=[jax.ShapeDtypeStruct((3 * units + 1, 8, width), BF16)],
        scratch_shapes=[pltpu.VMEM((8, width), F32), pltpu.SemaphoreType.DMA((3,))],
        name="pack",
    )(small, *(w.T.reshape(units, 8, width) for w in (querymat, keymat, valuemat)))
    (up_bias,) = call_near(
        functools.partial(pack_up_kernel, grid),
        [FAST],
        [((1, 8, width), BF16)],
        [pltpu.VMEM((8, width), F32)],
        1000,
        "pack_up",
    )(upbias.astype(F32).reshape(1, -1))
    second = jnp.concatenate(
        [mixmat.T.reshape(units, 8, width), upmat_w.T.reshape(4 * units, 8, width), up_bias], axis=0
    )
    third = downmat.T
    where = order_of(lengths, length)
    size_at = captions * (length // TILE) + captions
    places = gather_places()
    first_a = jnp.stack([first, grid.shift(first, kz=3)])
    first_z = grid.shift(first_a, kz=1)
    first_a, first_z, second = together((first_a, first_z, second))
    first_a = gather_one(grid, first_a, first_z)
    second_a = jnp.stack([second, grid.shift(second, kz=3)])
    first_a, second_a, where = together((first_a, second_a, where))
    first_b = gather_two(grid, first_a)
    first_c = gather_core(grid, first_b[:2])
    second_z = grid.shift(second_a, kz=1)
    first_b, first_c, second_z, third = together((first_b, first_c, second_z, third))
    first_in = first_b + first_c + gather_core(grid, first_b[2:])
    second_a = gather_one(grid, second_a, second_z)
    third_z = grid.shift(third, kz=3)
    half = grid.count // 2
    unit = 2 * tokens * width * width
    row = (tokens, width)
    heads = captions * (width // 256)
    tall = (tokens + 64, width)
    square = pltpu.VMEM((width, width), F32)
    moved, normed, query, keys, values, vec, held_one = call_near(
        functools.partial(project_kernel, grid, places),
        [SMEM] + [FAST] * (1 + len(first_in)),
        [(row, BF16)] * 5 + [((8, width), F32), ((grid.count, 3 * units, 8, width), BF16)],
        [],
        5 * unit,
        "project",
    )(where, hidden2, *first_in)
    second_a, third_z, query = together((second_a, third_z, query))
    third_a = jnp.stack([third, third_z])
    third_z = grid.shift(third_a, kz=1)
    second_b = gather_two(grid, second_a)
    second_c = gather_core(grid, second_b[:2])
    probs, mixed = call_near(
        functools.partial(attend_kernel, length, 4),
        [SMEM] * 2 + [FAST] * 3,
        [((heads, length, 256), BF16), (row, BF16)],
        [],
        5 * unit,
        "attend",
    )(lengths, where, query, keys, values)
    second_c, third_z, mixed = together((second_c, third_z, mixed))
    third_a = gather_one(grid, third_a, third_z)
    early = places[:2] + places[4:6]
    late = places[2:4] + places[6:]
    (held_two,) = call_near(
        functools.partial(place_kernel, grid, early),
        [FAST] * 4,
        [((grid.count,) + second.shape, BF16)],
        [],
        unit,
        "place_up",
    )(*second_b[:2], *second_c)
    second_b, third_a, held_two = together((second_b, third_a, held_two))
    second_in = second_b[2:] + gather_core(grid, second_b[2:])
    middle, normed2, active, slope, bias, held_two = call_near(
        functools.partial(upper_kernel, grid, late),
        [FAST] * (4 + len(second_in)),
        [(row, F32), (row, BF16), ((tokens, ff), BF16), ((tokens, ff), BF16), ((8, width), F32)]
        + [((grid.count,) + second.shape, BF16)],
        [],
        9 * unit,
        "upper",
        aliases={3 + len(second_in): 5},
    )(moved, mixed, vec, *second_in, held_two)
    third_b = gather_two(grid, third_a)
    third_c = gather_core(grid, third_b[:2])
    low, down_vec, down_own, down_other, active_far = call_near(
        functools.partial(down_grad_kernel, grid, length, size_at),
        [SMEM] * 2 + [FAST] * 2,
        [(row, BF16), ((8, width), F32)] + [((half, share, ff), BF16)] * 2 + [((LARGE // (2 * ff), ff), BF16)],
        [square, pltpu.SemaphoreType.DMA],
        5 * unit,
        "down_grad",
        far=1,
    )(lengths, where, cot2, active)
    third_b, third_c, down_own, down_other = together((third_b, third_c, down_own, down_other))
    third_in = third_b[2:] + gather_core(grid, third_b[2:])
    (held_three,) = call_near(
        functools.partial(place_kernel, grid, early),
        [FAST] * 4,
        [((grid.count, share, ff), BF16)],
        [],
        unit,
        "place_down",
    )(*third_b[:2], *third_c)
    down_two = scatter_first(grid, down_own, scatter_core(grid, down_other))
    low = tie(low, down_two[-1])
    grad_upper, up_vec, up_own, up_other, _, lower_w = call_near(
        functools.partial(upper_grad_kernel, grid, late, size_at),
        [SMEM] + [FAST] * (4 + len(third_in)),
        [((tokens, ff), BF16), ((32, width), F32)]
        + [((half, 4, share, width), BF16)] * 2
        + [((grid.count, share, ff), BF16)]
        + [((LARGE // (2 * share * ff), share, ff), BF16)],
        [square, pltpu.SemaphoreType.DMA],
        8 * unit,
        "upper_grad",
        aliases={2: 0, 4 + len(third_in): 4},
        far=1,
    )(where, low, slope, normed2, *third_in, held_three)
    down_two, up_vec, up_own, up_other = together((down_two, up_vec, up_own, up_other))
    down_three = scatter_second(grid, down_two, up_vec)
    up_one = scatter_core(grid, up_other)
    grad_upper = tie(grad_upper, down_three[-1])
    grad_middle, branch, dm, mid_vec = call_near(
        functools.partial(middle_grad_kernel, grid, size_at),
        [SMEM] + [FAST] * 5,
        [(row, F32), (row, BF16), (tall, BF16), ((8, width), F32)],
        [],
        6 * unit,
        "middle_grad",
    )(where, grad_upper, middle, low, vec, held_two)
    down_four = scatter_near(grid, down_three, mid_vec)
    up_two = scatter_first(grid, up_own, tie(up_one, mid_vec))
    dm = tie(dm, (up_two[-1], down_four[-1]))
    grads, att_vec = call_near(
        functools.partial(attend_grad_kernel, length, 4),
        [SMEM] * 2 + [FAST] * 5,
        [((3, tokens + 256, width), BF16), ((8, width), F32)],
        [],
        7 * unit,
        "attend_grad",
    )(lengths, where, dm, query, keys, values, probs)
    input_grad, all_vec, lower_w = call_near(
        functools.partial(input_grad_kernel, grid, size_at),
        [SMEM] + [FAST] * 9 + [FAR],
        [(row, F32), ((16, width), F32), ((grid.count, share, ff), BF16)],
        [pltpu.VMEM(row, F32), pltpu.SemaphoreType.DMA],
        5 * unit,
        "input_grad",
        limit=10,
    )(where, moved, grad_middle, grads, vec, down_vec, up_vec, mid_vec, att_vec, held_one, lower_w)
    grads, all_vec = together((grads, all_vec))
    att_own, att_other = call_near(
        functools.partial(weight_grad_kernel, grid, size_at),
        [SMEM] + [FAST] * 4,
        [((half, 4, share, width), BF16)] * 2,
        [square],
        5 * unit,
        "weight_grad",
    )(where, grads, branch, normed, mixed)
    down_four, up_two, att_own, att_other, all_vec = together((down_four, up_two, att_own, att_other, all_vec))
    down_four = scatter_far(grid, down_four, all_vec)
    up_three = scatter_second(grid, up_two, all_vec)
    att_one = scatter_core(grid, att_other)
    all_vec = (all_vec + grid.shift(all_vec, kc=1)).reshape(2, 8, width)
    att_one = tie(att_one, up_three[-1])
    att_two = scatter_first(grid, att_own, att_one, all_vec)
    up_four = scatter_near(grid, up_three, att_two[-1])
    down_sum = scatter_end(down_four, att_two[-1])
    middle = tie(middle, (att_two[-1], up_four[-1]))
    (block_out,) = call_near(
        lower_kernel,
        [SMEM, FAR, FAST, FAST, FAST],
        [(row, BF16)],
        [pltpu.VMEM((4, tokens // 4, ff), BF16), pltpu.VMEM(row, BF16), pltpu.SemaphoreType.DMA((4,))],
        5 * unit,
        "lower",
        limit=16,
    )(where, active_far, middle, vec, lower_w)
    out_gate = block_out[0:8, 0:128]
    att_three = scatter_second(grid, att_two, out_gate)
    up_four = scatter_far(grid, up_four, att_three[-1])
    att_four = scatter_third(grid, att_three, up_four[-1])
    up_sum = scatter_end(up_four, att_four[-1])
    att_sum, all_vec = scatter_last(att_four, out_gate)
    all_vec = all_vec.reshape(16, width)
    vecs = call(
        functools.partial(unpack_kernel, grid),
        1,
        [whole((16, width))],
        [whole((1, share))] * 8 + [whole((1, ff // grid.count))],
        [((1, share), F32)] * 8 + [((1, ff // grid.count), F32)],
        [],
        1000,
        1000,
        "unpack",
    )(all_vec)
    vecs = [v.reshape(-1) for v in vecs]
    return (
        block_out.reshape(hidden.shape),
        input_grad.reshape(hidden.shape),
        vecs[0],
        vecs[1],
        att_sum[0].T,
        vecs[2],
        att_sum[1].T,
        att_sum[2].T,
        vecs[3],
        att_sum[3].T,
        vecs[4],
        vecs[5],
        vecs[6],
        up_sum.reshape(ff // grid.count, width).T,
        vecs[8],
        down_sum.T,
        vecs[7],
    )


def fits(mesh):
    return mesh.shape["dp"] == 8 and mesh.shape["fsdp"] == 4


def solution(mesh):
    axes = ("dp", "fsdp")
    body = per_device
    if fits(mesh):
        axes = AXES
        grid = Grid3(mesh.shape["dp"], mesh.shape["fsdp"])
        mesh = jax.sharding.Mesh(mesh.devices.reshape(grid.z, grid.x, grid.y, grid.c), AXES)
        body = functools.partial(fast_device, grid)
    placed = (
        P(axes, None, None),
        P(axes),
        P(axes, None, None),
        P(axes),
        P(axes),
        P(None, axes),
        P(axes),
        P(None, axes),
        P(None, axes),
        P(axes),
        P(None, axes),
        P(axes),
        P(axes),
        P(axes),
        P(None, axes),
        P(axes),
        P(None, axes),
        P(axes),
    )
    return jax.shard_map(
        body,
        mesh=mesh,
        in_specs=placed,
        out_specs=(
            P(axes, None, None),
            P(axes, None, None),
            P(axes),
            P(axes),
            P(None, axes),
            P(axes),
            P(None, axes),
            P(None, axes),
            P(axes),
            P(None, axes),
            P(axes),
            P(axes),
            P(axes),
            P(None, axes),
            P(axes),
            P(None, axes),
            P(axes),
        ),
        check_vma=False,
    )
```
